32 devices in a mesh: groups: 2 (over x), visit: 16 (over z, y, core).
Axes of the slice: x: 2, y: 2, z: 4, core: 2. Of those that a mesh axis runs over, the one named last changes fastest.
Arguments:
- visit_image: bfloat16 [32, 256, 1024], P(('groups', 'visit')), parts along dimension 0, may hold values from -6 to 6
- band_offset: int32 [32, 2], P(('groups', 'visit')), parts along dimension 0, may hold values from -8 to 8
- shift_frac: float32 [32, 2], P(('groups', 'visit')), parts along dimension 0, may hold values from 0 to 1
- weights: bfloat16 [32], P(('groups', 'visit')), parts along dimension 0, may hold values from 0.29882812 to 3
- box_owner: int32 [32, 128, 1], P(('groups', 'visit')), parts along dimension 0, may hold values from 0 to 15; in each aligned block of 128 rows (0 to 127, 128 to 255, ..., all dimensions but the last counted through in order) at most 16 rows name the same one
- box_slot: int32 [32, 128], P(('groups', 'visit')), parts along dimension 0, may hold values from 0 to 15
- basis_index: int32 [32, 6], P(('groups', 'visit')), parts along dimension 0, may hold values from 0 to 11
- basis_coef: float32 [32, 6], P(('groups', 'visit')), parts along dimension 0, may hold values from 0.1 to 0.3
- basis_width: float32 [12], replicated, may hold values from 0.7 to 4
Outputs:
- template_coadd: bfloat16 [512, 16, 128], P(('groups', 'visit')), parts along dimension 0
- difference_coadd: float32 [512, 16, 128], P(('groups', 'visit')), parts along dimension 0
The draws below stay inside these ranges and needn't reach their ends.
There are 2 independent parts, one for each index of `groups`. The reference program is written for one: setup_inputs(seed, part) draws one part's arguments, and reference() takes and returns one part's arrays. A program takes and returns all parts, laid end to end along the dimension named above; an argument that names none is the same for every part. Nothing has to cross between parts.
Inputs may be any that keep to these rules, and one draw needn't show every extreme that they name: `box_owner`: among the 128 boxes of one visit no owner is named more than 16 times, and in every draw some visit names some owner exactly 16 times.
All inputs are finite; a program needn't handle non-finite values.
Results may differ from the reference program's by a relative error of at most 0.012.
The reference program's roundings to bfloat16 on the way count: a program that leaves them out, or rounds other values in their place, can miss the bound.
Values may be sent and summed in bfloat16 or wider, within the bound.
No kernel may reach another device: no remote copies, remote signals or barrier semaphores. Data moves between devices by JAX's collectives and lax.ppermute only.
A program may use at most 64 MiB of HBM per device.

```python
import math
import jax
import jax.numpy as jnp
import numpy as np
from jax import lax

H = 256
W = 1024
BH = 16
BW = 128
PS = 16
KB = 6
NBASIS = 12
NB = 128
CAP = 16
N_VISIT = 16


def draw_visit_image(key, part):
    noise_key, base_key, slope_key = jax.random.split(key, 3)
    down_place = (jnp.arange(H, dtype=jnp.float32) / H - 0.5)[:, None]
    across_place = (jnp.arange(W, dtype=jnp.float32) / W - 0.5)[None, :]
    sky_base = jax.random.uniform(base_key, (), jnp.float32, 1.8, 2.2)
    sky_slopes = jax.random.uniform(slope_key, (2,), jnp.float32, -0.5, 0.5)
    noise_field = 0.7 * jax.random.normal(noise_key, (N_VISIT, H, W), jnp.float32)
    background = sky_base + sky_slopes[0] * down_place + sky_slopes[1] * across_place
    return jnp.clip(background[None, :, :] + noise_field, -6.0, 6.0).astype(jnp.bfloat16)


def draw_basis_width(key, part):
    broad_key, narrow_key = jax.random.split(key)
    broad_count = 8
    broad = jax.random.uniform(broad_key, (broad_count,), jnp.float32, 3.0, 4.0)
    narrow = jnp.exp(jax.random.uniform(narrow_key, (NBASIS - broad_count,), jnp.float32, math.log(0.7), math.log(3.0)))
    return jnp.concatenate([broad, narrow]).astype(jnp.float32)


def touch_ends(values, key, smallest, largest):
    spot = [jax.random.randint(jax.random.fold_in(key, axis), (), 0, length) for axis, length in enumerate(values.shape)]
    longest = values.shape.index(max(values.shape))
    neighbour = spot[:longest] + [(spot[longest] + 1) % values.shape[longest]] + spot[longest + 1:]
    return values.at[tuple(spot)].set(smallest).at[tuple(neighbour)].set(largest)


def block_scale(key, dims, pieces, least, top_value):
    loudness, own = 1.0, jax.random.fold_in(key, 6)
    for position, blocks in pieces:
        draws = jnp.exp(jax.random.uniform(jax.random.fold_in(own, position), (blocks,), jnp.float32, least / len(pieces), top_value / len(pieces)))
        loudness = loudness * jnp.repeat(draws, dims[position] // blocks).reshape([-1 if axis == position else 1 for axis in range(len(dims))])
    return loudness


def assign_block(key, own, number, rows, amount, top, most, lean):
    order = jax.random.permutation(key, amount)
    heavy_load, common = shares(amount, rows * top, most, lean, True), shares(amount, rows * top, most, lean, False)
    places = jnp.arange(amount)

    def named(tallies, offset_by):
        used = int((tallies > 0).sum())
        fixed = max(1, used // 4)
        passed = fixed + (places - fixed + offset_by * (used - fixed)) % max(1, amount - fixed)
        return jnp.zeros((amount,), jnp.int32).at[order[jnp.where(places < fixed, places, passed)]].set(jnp.asarray(tallies, jnp.int32))

    tallies = jnp.where(number % 4 == 0, named(heavy_load, number // 4), named(common, number - number // 4 - 1))
    mixed = jax.random.permutation(jax.random.fold_in(own, 3), amount)
    donor, taker = mixed[0:amount // 2 * 2:2], mixed[1:amount // 2 * 2:2]
    room = jnp.minimum(tallies[donor] - 1, most - tallies[taker]) // 2
    room = jnp.where((donor == order[0]) | (taker == order[0]) | (tallies[taker] == 0), 0, jnp.maximum(room, 0))
    passed = jax.random.randint(jax.random.fold_in(own, 4), (amount // 2,), 0, 1 << 20) % (room + 1)
    tallies = tallies.at[donor].add(-passed).at[taker].add(passed)
    items = jnp.searchsorted(jnp.cumsum(tallies), jnp.arange(rows * top), side="right").astype(jnp.int32)
    table = items.reshape(top, rows).T
    table = table[jax.random.permutation(jax.random.fold_in(own, 1), rows)]
    offset_by = jax.random.randint(jax.random.fold_in(own, 2), (rows, 1), 0, top)
    return jnp.take_along_axis(table, (jnp.arange(top)[None, :] + offset_by) % top, axis=1)


def shares(amount, total, limit, slope, full):
    loads = [(1 << 20) // math.isqrt(standing ** slope) + 1 for standing in range(1, amount + 1)]
    largest = limit if full else min(limit, max(-(-total // amount), total * loads[0] // sum(loads)))
    least = 1 if total - largest >= amount - 1 else 0
    holding, rest = [largest] + [least] * (amount - 1), total - largest - least * (amount - 1)
    while rest > 0:
        candidates = [i for i in range(1, amount) if holding[i] < largest] or [i for i in range(1, amount) if holding[i] < limit]
        whole, budget = sum([loads[i] for i in candidates]), rest
        for i in candidates:
            more = min(limit - holding[i], max(1, budget * loads[i] // whole), rest)
            holding[i] = holding[i] + more
            rest = rest - more
    return np.array(holding)


def setup_inputs(seed: int = 0, part: int = 0) -> dict:
    key_of = jax.random.split(jax.random.key(seed), 10)
    own_keys = jax.random.split(jax.random.fold_in(key_of[9], part), 10)
    visit_image = draw_visit_image(jax.random.fold_in(jax.random.fold_in(key_of[9], part), 71), part)
    band_offset = touch_ends(jax.random.randint(own_keys[1], (N_VISIT, 2), -8, 9), jax.random.fold_in(own_keys[1], 1), -8, 8).astype(jnp.int32)
    shift_frac = jnp.clip(1.0 * jax.random.uniform(own_keys[2], (N_VISIT, 2), jnp.float32) ** block_scale(own_keys[2], (N_VISIT, 2), ((0, 16),), -0.2, 0.2), 0.0, 1.0)
    weights = jnp.clip(jnp.exp(math.log(3.0) - 2.306499 * jax.random.uniform(own_keys[3], (N_VISIT,), jnp.float32) ** block_scale(own_keys[3], (N_VISIT,), ((0, 16),), -0.2, 0.2)), 0.29882812, 3.0).astype(jnp.bfloat16)
    box_owner_keys = jax.random.split(jax.random.fold_in(own_keys[4], 1), N_VISIT * NB // NB)
    box_owner_turns = jax.random.permutation(jax.random.fold_in(own_keys[4], 3), N_VISIT * NB // NB)
    box_owner = jax.vmap(lambda own, number: assign_block(jax.random.fold_in(own_keys[4], 2), own, number, NB, N_VISIT, 1, CAP, 2))(box_owner_keys, box_owner_turns).reshape((N_VISIT, NB, 1))
    box_slot = touch_ends(jax.random.randint(own_keys[5], (N_VISIT, NB), 0, PS), jax.random.fold_in(own_keys[5], 1), 0, PS - 1).astype(jnp.int32)
    basis_index = touch_ends(jax.random.randint(own_keys[6], (N_VISIT, KB), 0, NBASIS), jax.random.fold_in(own_keys[6], 1), 0, NBASIS - 1).astype(jnp.int32)
    basis_coef = jnp.clip(0.1 + 0.20000001043081284 * jax.random.uniform(own_keys[7], (N_VISIT, KB), jnp.float32) ** block_scale(own_keys[7], (N_VISIT, KB), ((0, 16),), -0.2, 0.2), 0.1, 0.3)
    basis_width = draw_basis_width(jax.random.fold_in(key_of[9], 71), part)
    return dict(visit_image=visit_image, band_offset=band_offset, shift_frac=shift_frac, weights=weights, box_owner=box_owner, box_slot=box_slot, basis_index=basis_index, basis_coef=basis_coef, basis_width=basis_width)


band_reach = 8.0


def lanczos_band(extent, shift_by, by_rows):
    out_index = jnp.arange(extent, dtype=jnp.float32)[:, None]
    in_index = jnp.arange(extent, dtype=jnp.float32)[None, :]
    if by_rows:
        offset = in_index - out_index - shift_by
    else:
        offset = out_index - in_index - shift_by
    kernel_value = jnp.sinc(offset) * jnp.sinc(offset / 3.0)
    return jnp.where(jnp.abs(offset) < 3.0, kernel_value, 0.0).astype(jnp.bfloat16)


def gauss_band(extent, blur_width):
    out_index = jnp.arange(extent, dtype=jnp.float32)[:, None]
    in_index = jnp.arange(extent, dtype=jnp.float32)[None, :]
    pixel_gap = out_index - in_index
    tap_offsets = jnp.arange(17, dtype=jnp.float32) - 8.0
    spread = 2.0 * blur_width * blur_width
    tap_total = jnp.sum(jnp.exp(-tap_offsets * tap_offsets / spread))
    kernel_value = jnp.where(jnp.abs(pixel_gap) <= band_reach, jnp.exp(-pixel_gap * pixel_gap / spread), 0.0)
    return (kernel_value / tap_total).astype(jnp.bfloat16)


def to_boxes(picture, box_rows, box_cols):
    pix_rows, pix_cols = picture.shape
    split = picture.reshape(pix_rows // box_rows, box_rows, pix_cols // box_cols, box_cols)
    return split.transpose(0, 2, 1, 3).reshape(-1, box_rows * box_cols)


def from_boxes(flat_boxes, pix_rows, pix_cols, box_rows, box_cols):
    split = flat_boxes.reshape(pix_rows // box_rows, pix_cols // box_cols, box_rows, box_cols)
    return split.transpose(0, 2, 1, 3).reshape(pix_rows, pix_cols)


def warp_visit(picture, offsets, fractions):
    shifts = offsets.astype(jnp.float32) + fractions
    row_warp = lanczos_band(H, shifts[0], True)
    col_warp = lanczos_band(W, shifts[1], False)
    col_pass = jnp.dot(picture, col_warp, preferred_element_type=jnp.float32).astype(jnp.bfloat16)
    return jnp.dot(row_warp, col_pass, preferred_element_type=jnp.float32).astype(jnp.bfloat16)


def reference(visit_image, band_offset, shift_frac, weights, box_owner, box_slot, basis_index, basis_coef, basis_width):
    warped_all = lax.map(lambda entry: warp_visit(entry[0], entry[1], entry[2]), (visit_image, band_offset, shift_frac))
    box_all = lax.map(lambda picture: to_boxes(picture, BH, BW), warped_all)
    target = (box_owner[:, :, 0] * PS + box_slot).reshape(-1).astype(jnp.int32)
    box_weight = jnp.broadcast_to(weights.astype(jnp.float32)[:, None], (N_VISIT, NB)).reshape(-1)
    slot_count = N_VISIT * PS
    weight_sum = 1.0 + jax.ops.segment_sum(box_weight, target, num_segments=slot_count)
    scaled = box_all.reshape(-1, BH * BW).astype(jnp.float32) * box_weight[:, None]
    summed = jax.ops.segment_sum(scaled, target, num_segments=slot_count)
    template = (summed / weight_sum[:, None]).astype(jnp.bfloat16)

    def match_visit(entry):
        warped, dest_ids, slot_ids, basis_ids, coefs = entry
        returned_boxes = template[dest_ids[:, 0] * PS + slot_ids]
        template_image = from_boxes(returned_boxes, H, W, BH, BW)
        matched = jnp.zeros((H, W), jnp.float32)
        for member in range(KB):
            blur_width = basis_width[basis_ids[member]]
            across = gauss_band(W, blur_width)
            down_band = gauss_band(H, blur_width)
            blurred = jnp.dot(template_image, across, preferred_element_type=jnp.float32).astype(jnp.bfloat16)
            matched = matched + coefs[member] * jnp.dot(down_band, blurred, preferred_element_type=jnp.float32)
        difference = (warped.astype(jnp.float32) - matched).astype(jnp.bfloat16)
        return to_boxes(difference, BH, BW)

    diff_boxes = lax.map(match_visit, (warped_all, box_owner, box_slot, basis_index, basis_coef))
    diff_scaled = diff_boxes.reshape(-1, BH * BW).astype(jnp.float32) * box_weight[:, None]
    diff_summed = jax.ops.segment_sum(diff_scaled, target, num_segments=slot_count)
    difference_coadd = diff_summed / weight_sum[:, None]
    return template.reshape(slot_count, BH, BW), difference_coadd.reshape(slot_count, BH, BW)
```

```python
import functools

import jax
import jax.numpy as jnp
from jax import lax
from jax.experimental import pallas as pl
from jax.experimental.pallas import tpu as pltpu
from jax.sharding import PartitionSpec as P

BH = 16
BW = 128
PS = 16
SIDE = 128
WIDE = 256

band_reach = 8.0

VMEM = pl.BlockSpec(memory_space=pltpu.VMEM)
SMEM = pl.BlockSpec(memory_space=pltpu.SMEM)
ANY = pl.BlockSpec(memory_space=pl.ANY)


def params():
    return pltpu.CompilerParams(vmem_limit_bytes=48 * 1024 * 1024)


def place(owner, me, peers):
    away = jnp.bitwise_xor(owner, me)
    return (away & 1) * (peers // 2) + ((away >> 1) & 1) * (peers // 4) + (away >> 2)


def windows(width):
    found = []
    for first in range(0, width, WIDE):
        low, high = max(first - SIDE, 0), min(first + WIDE + SIDE, width)
        found.append((low, high, low - first + SIDE, high - first + SIDE))
    return found


def lanczos_taps(gap, whole, part):
    shift = whole.astype(jnp.float32) + part
    band = jnp.zeros(gap.shape, jnp.float32)
    for tap in range(-2, 5):
        spot = (whole + tap).astype(jnp.float32)
        x = jnp.full((8, 128), spot - shift, jnp.float32)

        def sinc(v):
            angle = jnp.pi * v
            return jnp.where(v == 0.0, 1.0, jnp.sin(angle) / jnp.where(v == 0.0, 1.0, angle))

        value = jnp.where(jnp.abs(x) < 3.0, sinc(x) * sinc(x / 3.0), 0.0)
        band = jnp.where(gap == spot, value[0:1, 0:1], band)
    return band.astype(jnp.bfloat16)


def warp_kernel(
    peers, picture, band_offset, shift_frac, weight, owner, slot, me_ref, warped, keep, send, total, wide_band
):
    rows, width = warped.shape
    me = me_ref[0]
    gap = (
        lax.broadcasted_iota(jnp.int32, (WIDE + 2 * SIDE, WIDE), 0)
        - lax.broadcasted_iota(jnp.int32, (WIDE + 2 * SIDE, WIDE), 1)
        - SIDE
    ).astype(jnp.float32)
    wide_band[...] = lanczos_taps(gap, band_offset[0, 1], shift_frac[0, 1])
    gap = (
        lax.broadcasted_iota(jnp.int32, (rows, rows), 1) - lax.broadcasted_iota(jnp.int32, (rows, rows), 0)
    ).astype(jnp.float32)
    row_warp = lanczos_taps(gap, band_offset[0, 0], shift_frac[0, 0])
    total[...] = jnp.zeros_like(total)
    heavy = weight[...].astype(jnp.float32)
    for block, (low, high, top, bottom) in enumerate(windows(width)):
        col_pass = jnp.dot(
            picture[:, low:high], wide_band[top:bottom, :], preferred_element_type=jnp.float32
        ).astype(jnp.bfloat16)
        done = jnp.dot(row_warp, col_pass, preferred_element_type=jnp.float32).astype(jnp.bfloat16)
        warped[:, block * WIDE : (block + 1) * WIDE] = done
        add_boxes(peers, me, total, done.astype(jnp.float32) * heavy, owner, slot, block, width)
    store_slots(peers, total, keep, send)


def add_boxes(peers, me, total, scaled, owner, slot, block, width):
    across = WIDE // BW
    for down in range(scaled.shape[0] // BH):
        for col in range(across):
            box = down * (width // BW) + block * across + col
            spot = place(owner[0, box], me, peers) * PS + slot[0, box]
            piece = pl.ds(pl.multiple_of(spot * BH, BH), BH)
            total[piece, :] += scaled[down * BH : (down + 1) * BH, col * BW : (col + 1) * BW]


def store_slots(peers, total, keep, send):
    half = peers // 2 * PS * BH
    step = 1024

    @pl.loop(0, half // step)
    def _(i):
        here = pl.ds(pl.multiple_of(i * step, step), step)
        there = pl.ds(pl.multiple_of(i * step + half, step), step)
        keep[here, :] = total[here, :].astype(jnp.bfloat16)
        send[here, :] = total[there, :].astype(jnp.bfloat16)


def add_kernel(parts, ours, theirs, *outs):
    length = ours.shape[0] // parts
    for i, out in enumerate(outs):
        here = pl.ds(i * length, length)
        out[...] = (ours[here, :].astype(jnp.float32) + theirs[here, :].astype(jnp.float32)).astype(jnp.bfloat16)


def add_parts(ours, theirs, parts):
    length = ours.shape[0] // parts
    return pl.pallas_call(
        functools.partial(add_kernel, parts),
        out_shape=[jax.ShapeDtypeStruct((length, BW), jnp.bfloat16)] * parts,
        in_specs=[VMEM, VMEM],
        out_specs=[VMEM] * parts,
        compiler_params=params(),
        name="add_parts",
    )(ours, theirs)


def swap(x, axis_size, bit):
    return lax.ppermute(x, "visit", [(i, i ^ bit) for i in range(axis_size)])


def scatter_sum(keep, send, peers):
    near = swap(send, peers, 1)
    ours, theirs = add_parts(keep, near, 2)
    near = swap(theirs, peers, 2)
    terms = add_parts(ours, near, peers // 4)
    return [terms[0]] + [swap(terms[far], peers, 4 * far) for far in reversed(range(1, peers // 4))]


def gather_slots(own, peers):
    far = [own] + [swap(own, peers, 4 * away) for away in range(1, peers // 4)]
    line = jnp.concatenate(far, axis=0)
    pair = jnp.concatenate([line, swap(line, peers, 2)], axis=0)
    return pair, swap(pair, peers, 1)


def weight_kernel(tags, me_ref, weight_sum):
    visits = tags.shape[0] // 2
    named = tags[0:visits, :]
    heavy = tags[visits:, :]
    lines = []
    for i in range(PS):
        target = (me_ref[0] * PS + i).astype(jnp.float32)
        hit = jnp.where(named == target, heavy, 0.0)
        lines.append(jnp.sum(jnp.sum(hit, axis=0, keepdims=True), axis=1, keepdims=True))
    weight_sum[...] = jnp.broadcast_to(1.0 + jnp.concatenate(lines, axis=0), weight_sum.shape)


def coadd_kernel(weight_sum, *refs):
    *terms, out = refs
    for i in range(PS):
        here = slice(i * BH, (i + 1) * BH)
        summed = terms[0][here, :].astype(jnp.float32)
        for term in terms[1:]:
            summed = summed + term[here, :].astype(jnp.float32)
        out[here, :] = (summed / weight_sum[i : i + 1, :]).astype(out.dtype)


def coadd(weight_sum, terms, dtype):
    return pl.pallas_call(
        coadd_kernel,
        out_shape=jax.ShapeDtypeStruct((PS * BH, BW), dtype),
        in_specs=[VMEM] * (1 + len(terms)),
        out_specs=VMEM,
        compiler_params=params(),
        name="coadd",
    )(weight_sum, *terms)


def gauss_kernel(basis_index, basis_width, bands):
    bases = bands.shape[0]
    tap = lax.broadcasted_iota(jnp.int32, (8, 128), 1).astype(jnp.float32) - band_reach
    gaps = []
    for shift in (SIDE, 0, -SIDE):
        gap = (
            lax.broadcasted_iota(jnp.int32, (SIDE, SIDE), 0) - lax.broadcasted_iota(jnp.int32, (SIDE, SIDE), 1) - shift
        ).astype(jnp.float32)
        gaps.append(gap)
    for member in range(bases):
        blur_width = basis_width[basis_index[0, member]]
        spread = 2.0 * blur_width * blur_width
        total = jnp.sum(jnp.where(tap <= band_reach, jnp.exp(-tap * tap / spread), 0.0), axis=1, keepdims=True)[0:1]
        blocks = []
        for gap in gaps:
            value = jnp.where(jnp.abs(gap) <= band_reach, jnp.exp(-gap * gap / spread), 0.0)
            blocks.append((value / total).astype(jnp.bfloat16))
        above, middle, below = blocks
        nothing = jnp.zeros_like(middle)
        for place_, pieces in enumerate(((above, nothing), (middle, above), (below, middle), (nothing, below))):
            for col, piece in enumerate(pieces):
                bands[member, place_ * SIDE : (place_ + 1) * SIDE, col * SIDE : (col + 1) * SIDE] = piece


def match_kernel(
    peers,
    warped,
    bands,
    near,
    other,
    weight,
    coef,
    owner,
    slot,
    me_ref,
    keep,
    send,
    table,
    image,
    total,
    sems,
):
    rows, width = warped.shape
    me = me_ref[0]
    half = peers // 2 * PS * BH
    copies = [
        pltpu.make_async_copy(near, table.at[pl.ds(0, half)], sems.at[0]),
        pltpu.make_async_copy(other, table.at[pl.ds(half, half)], sems.at[1]),
    ]
    for copy in copies:
        copy.start()
    total[...] = jnp.zeros_like(total)
    heavy = weight[...].astype(jnp.float32)
    for copy in copies:
        copy.wait()
    for box in range(rows // BH * (width // BW)):
        down, col = divmod(box, width // BW)
        spot = place(owner[0, box], me, peers) * PS + slot[0, box]
        piece = table[pl.ds(pl.multiple_of(spot * BH, BH), BH), :]
        image[down * BH : (down + 1) * BH, col * BW : (col + 1) * BW] = piece
    for block, (low, high, top, bottom) in enumerate(windows(width)):
        matched = jnp.zeros((rows, WIDE), jnp.float32)
        for member in range(bands.shape[0]):
            blurred = jnp.dot(
                image[:, low:high], bands[member, top:bottom, :], preferred_element_type=jnp.float32
            ).astype(jnp.bfloat16)
            matched = matched + coef[0, member] * jnp.dot(
                bands[member, SIDE : SIDE + rows, :], blurred, preferred_element_type=jnp.float32
            )
        ours = warped[:, block * WIDE : (block + 1) * WIDE].astype(jnp.float32)
        difference = (ours - matched).astype(jnp.bfloat16)
        add_boxes(peers, me, total, difference.astype(jnp.float32) * heavy, owner, slot, block, width)
    store_slots(peers, total, keep, send)


def shards(
    visit_image,
    band_offset,
    shift_frac,
    weights,
    box_owner,
    box_slot,
    basis_index,
    basis_coef,
    basis_width,
):
    peers = lax.axis_size("visit")
    rows, width = visit_image.shape[1:]
    bases = basis_index.shape[1]
    lines = peers * PS * BH
    owner = box_owner.reshape(1, -1)
    me = lax.axis_index("visit").astype(jnp.int32).reshape(1)
    weight = weights.reshape(1, 1)

    named = (owner * PS + box_slot).astype(jnp.float32)
    tag = jnp.concatenate([named, jnp.broadcast_to(weight.astype(jnp.float32), named.shape)], axis=0)
    tags = lax.all_gather(tag, "visit", axis=1, tiled=False).reshape(2 * peers, -1)

    half = jax.ShapeDtypeStruct((lines // 2, BW), jnp.bfloat16)
    warped, keep, send = pl.pallas_call(
        functools.partial(warp_kernel, peers),
        out_shape=[jax.ShapeDtypeStruct((rows, width), jnp.bfloat16), half, half],
        in_specs=[VMEM, SMEM, SMEM, VMEM, SMEM, SMEM, SMEM],
        out_specs=[VMEM] * 3,
        scratch_shapes=[
            pltpu.VMEM((lines, BW), jnp.float32),
            pltpu.VMEM((WIDE + 2 * SIDE, WIDE), jnp.bfloat16),
        ],
        compiler_params=params(),
        name="warp",
    )(visit_image[0], band_offset, shift_frac, weight, owner, box_slot, me)

    bands = pl.pallas_call(
        gauss_kernel,
        out_shape=jax.ShapeDtypeStruct((bases, WIDE + 2 * SIDE, WIDE), jnp.bfloat16),
        in_specs=[SMEM, SMEM],
        out_specs=VMEM,
        compiler_params=params(),
        name="gauss_bands",
    )(basis_index, basis_width)

    terms = scatter_sum(keep, send, peers)
    weight_sum = pl.pallas_call(
        weight_kernel,
        out_shape=jax.ShapeDtypeStruct((PS, BW), jnp.float32),
        in_specs=[VMEM, SMEM],
        out_specs=VMEM,
        compiler_params=params(),
        name="weight_sum",
    )(tags, me)
    template = coadd(weight_sum, terms, jnp.bfloat16)
    near, other = gather_slots(template, peers)

    keep, send = pl.pallas_call(
        functools.partial(match_kernel, peers),
        out_shape=[half, half],
        in_specs=[VMEM, VMEM, ANY, ANY, VMEM, SMEM, SMEM, SMEM, SMEM],
        out_specs=[VMEM] * 2,
        scratch_shapes=[
            pltpu.VMEM((lines, BW), jnp.bfloat16),
            pltpu.VMEM((rows, width), jnp.bfloat16),
            pltpu.VMEM((lines, BW), jnp.float32),
            pltpu.SemaphoreType.DMA((2,)),
        ],
        compiler_params=params(),
        name="match",
    )(warped, bands, near, other, weight, basis_coef, owner, box_slot, me)
    terms = scatter_sum(keep, send, peers)
    difference_coadd = coadd(weight_sum, terms, jnp.float32)
    return (template.reshape(PS, BH, BW), difference_coadd.reshape(PS, BH, BW))


def solution(mesh):
    placed = (
        P(("groups", "visit"), None, None),
        P(("groups", "visit"), None),
        P(("groups", "visit"), None),
        P(("groups", "visit")),
        P(("groups", "visit"), None, None),
        P(("groups", "visit"), None),
        P(("groups", "visit"), None),
        P(("groups", "visit"), None),
        P(),
    )
    return jax.shard_map(
        shards,
        mesh=mesh,
        in_specs=placed,
        out_specs=(P(("groups", "visit"), None, None), P(("groups", "visit"), None, None)),
        check_vma=False,
    )
```

```python
import functools

import jax
import jax.numpy as jnp
from jax import lax
from jax.experimental import pallas as pl
from jax.experimental.pallas import tpu as pltpu
from jax.sharding import PartitionSpec as P

BH = 16
BW = 128
PS = 16
SIDE = 128
WIDE = 256

band_reach = 8.0

VMEM = pl.BlockSpec(memory_space=pltpu.VMEM)
SMEM = pl.BlockSpec(memory_space=pltpu.SMEM)
HBM = pl.BlockSpec(memory_space=pltpu.HBM)


def params():
    return pltpu.CompilerParams(vmem_limit_bytes=48 * 1024 * 1024)


def tag_rows(peers):
    return PS * pl.cdiv(2 * peers, BW)


def place(owner, me, peers):
    away = jnp.bitwise_xor(owner, me)
    return (away & 1) * (peers // 2) + ((away >> 1) & 1) * (peers // 4) + (away >> 2)


def windows(width):
    found = []
    for first in range(0, width, WIDE):
        low, high = max(first - SIDE, 0), min(first + WIDE + SIDE, width)
        found.append((low, high, low - first + SIDE, high - first + SIDE))
    return found


def lanczos_taps(gap, whole, part):
    shift = whole.astype(jnp.float32) + part
    band = jnp.zeros(gap.shape, jnp.float32)
    for tap in range(-2, 5):
        spot = (whole + tap).astype(jnp.float32)
        x = jnp.full((8, 128), spot - shift, jnp.float32)

        def sinc(v):
            angle = jnp.pi * v
            return jnp.where(v == 0.0, 1.0, jnp.sin(angle) / jnp.where(v == 0.0, 1.0, angle))

        value = jnp.where(jnp.abs(x) < 3.0, sinc(x) * sinc(x / 3.0), 0.0)
        band = jnp.where(gap == spot, value[0:1, 0:1], band)
    return band.astype(jnp.bfloat16)


def warp_kernel(
    peers,
    picture,
    weight,
    me_ref,
    band_offset_in,
    shift_frac_in,
    owner_in,
    slot_in,
    warped,
    keep,
    send,
    total,
    wide_band,
    band_offset,
    shift_frac,
    owner,
    slot,
    sems,
):
    rows, width = warped.shape
    me = me_ref[0]
    copies = [
        pltpu.make_async_copy(source, target, sems.at[i])
        for i, (source, target) in enumerate(
            (
                (band_offset_in, band_offset),
                (shift_frac_in, shift_frac),
                (owner_in, owner),
                (slot_in, slot),
            )
        )
    ]
    for copy in copies:
        copy.start()
    total[...] = jnp.zeros_like(total)
    heavy = weight[...].astype(jnp.float32)
    for copy in copies:
        copy.wait()
    gap = (
        lax.broadcasted_iota(jnp.int32, (WIDE + 2 * SIDE, WIDE), 0)
        - lax.broadcasted_iota(jnp.int32, (WIDE + 2 * SIDE, WIDE), 1)
        - SIDE
    ).astype(jnp.float32)
    wide_band[...] = lanczos_taps(gap, band_offset[0, 1], shift_frac[0, 1])
    gap = (
        lax.broadcasted_iota(jnp.int32, (rows, rows), 1) - lax.broadcasted_iota(jnp.int32, (rows, rows), 0)
    ).astype(jnp.float32)
    row_warp = lanczos_taps(gap, band_offset[0, 0], shift_frac[0, 0])
    chunk = PS * BH + tag_rows(peers)
    lane = lax.broadcasted_iota(jnp.int32, (1, BW), 1)
    mark = jnp.where(lane == me, heavy, 0.0)
    for box in range(owner.shape[1]):
        spot = place(owner[0, box], me, peers) * chunk + PS * BH + slot[0, box]
        total[pl.ds(spot, 1), :] += mark
    passes = [
        jnp.dot(
            picture[:, low:high], wide_band[top:bottom, :], preferred_element_type=jnp.float32
        ).astype(jnp.bfloat16)
        for low, high, top, bottom in windows(width)
    ]
    for block, col_pass in enumerate(passes):
        done = jnp.dot(row_warp, col_pass, preferred_element_type=jnp.float32).astype(jnp.bfloat16)
        warped[:, block * WIDE : (block + 1) * WIDE] = done
        add_boxes(peers, chunk, me, total, done.astype(jnp.float32) * heavy, owner, slot, block, width)
    store_slots(peers, chunk, total, keep, send)


def add_boxes(peers, chunk, me, total, scaled, owner, slot, block, width):
    across = WIDE // BW
    for down in range(scaled.shape[0] // BH):
        for col in range(across):
            box = down * (width // BW) + block * across + col
            spot = place(owner[0, box], me, peers) * chunk + slot[0, box] * BH
            piece = pl.ds(pl.multiple_of(spot, BH), BH)
            total[piece, :] += scaled[down * BH : (down + 1) * BH, col * BW : (col + 1) * BW]


def store_slots(peers, chunk, total, keep, send):
    half = peers // 2 * chunk
    boxes = PS * BH

    @pl.loop(0, peers // 2)
    def _(i):
        for out, base in ((keep, 0), (send, half)):
            start = pl.multiple_of(i * chunk, PS)
            out[pl.ds(start, boxes), :] = total[pl.ds(base + start, boxes), :].astype(jnp.bfloat16)
            if chunk > boxes:
                tags = total[pl.ds(base + start + boxes, PS), :]
                high = tags.astype(jnp.bfloat16)
                low = tags - high.astype(jnp.float32)
                if chunk == boxes + PS:
                    both = high.astype(jnp.float32) + pltpu.roll(low, peers, 1)
                    out[pl.ds(start + boxes, PS), :] = both.astype(jnp.bfloat16)
                else:
                    out[pl.ds(start + boxes, PS), :] = high
                    out[pl.ds(start + boxes + PS, PS), :] = low.astype(jnp.bfloat16)


def add_kernel(parts, ours, theirs, *outs):
    length = ours.shape[0] // parts
    for i, out in enumerate(outs):
        here = pl.ds(i * length, length)
        out[...] = (ours[here, :].astype(jnp.float32) + theirs[here, :].astype(jnp.float32)).astype(jnp.bfloat16)


def add_parts(ours, theirs, parts):
    length = ours.shape[0] // parts
    return pl.pallas_call(
        functools.partial(add_kernel, parts),
        out_shape=[jax.ShapeDtypeStruct((length, BW), jnp.bfloat16)] * parts,
        in_specs=[VMEM, VMEM],
        out_specs=[VMEM] * parts,
        compiler_params=params(),
        name="add_parts",
    )(ours, theirs)


def swap(x, axis_size, bit):
    return lax.ppermute(x, "visit", [(i, i ^ bit) for i in range(axis_size)])


def scatter_sum(keep, send, peers):
    near = swap(send, peers, 1)
    ours, theirs = add_parts(keep, near, 2)
    near = swap(theirs, peers, 2)
    terms = add_parts(ours, near, peers // 4)
    return [terms[0]] + [swap(terms[far], peers, 4 * far) for far in reversed(range(1, peers // 4))]


def join_kernel(*refs):
    *parts, out = refs
    length = parts[0].shape[0]
    for i, part in enumerate(parts):
        out[i * length : (i + 1) * length, :] = part[...]


def join(*parts):
    rows, lanes = parts[0].shape
    return pl.pallas_call(
        join_kernel,
        out_shape=jax.ShapeDtypeStruct((rows * len(parts), lanes), parts[0].dtype),
        in_specs=[VMEM] * len(parts),
        out_specs=VMEM,
        compiler_params=params(),
        name="join",
    )(*parts)


def gather_slots(own, peers):
    line = join(own, *[swap(own, peers, 4 * away) for away in range(1, peers // 4)])
    pair = join(line, swap(line, peers, 2))
    return pair, swap(pair, peers, 1)


def summed_terms(terms, here):
    total = terms[0][here, :].astype(jnp.float32)
    for term in terms[1:]:
        total = total + term[here, :].astype(jnp.float32)
    return total


def template_kernel(*refs):
    *terms, template, weight_sum = refs
    tags = summed_terms(terms, slice(PS * BH, PS * BH + PS))
    for i in range(1, (terms[0].shape[0] - PS * BH) // PS):
        tags = tags + summed_terms(terms, slice(PS * BH + i * PS, PS * BH + (i + 1) * PS))
    weight_sum[...] = jnp.broadcast_to(1.0 + jnp.sum(tags, axis=1, keepdims=True), weight_sum.shape)
    for i in range(PS):
        here = slice(i * BH, (i + 1) * BH)
        template[here, :] = (summed_terms(terms, here) / weight_sum[i : i + 1, :]).astype(template.dtype)


def difference_kernel(weight_sum, *refs):
    *terms, out = refs
    for i in range(PS):
        here = slice(i * BH, (i + 1) * BH)
        out[here, :] = summed_terms(terms, here) / weight_sum[i : i + 1, :]


def gauss_kernel(basis_index, basis_width, bands):
    bases = bands.shape[0]
    tap = lax.broadcasted_iota(jnp.int32, (8, 128), 1).astype(jnp.float32) - band_reach
    gaps = []
    for shift in (SIDE, 0, -SIDE):
        gap = (
            lax.broadcasted_iota(jnp.int32, (SIDE, SIDE), 0) - lax.broadcasted_iota(jnp.int32, (SIDE, SIDE), 1) - shift
        ).astype(jnp.float32)
        gaps.append(gap)
    for member in range(bases):
        blur_width = basis_width[basis_index[0, member]]
        spread = 2.0 * blur_width * blur_width
        total = jnp.sum(jnp.where(tap <= band_reach, jnp.exp(-tap * tap / spread), 0.0), axis=1, keepdims=True)[0:1]
        blocks = []
        for gap in gaps:
            value = jnp.where(jnp.abs(gap) <= band_reach, jnp.exp(-gap * gap / spread), 0.0)
            blocks.append((value / total).astype(jnp.bfloat16))
        above, middle, below = blocks
        nothing = jnp.zeros_like(middle)
        for place_, pieces in enumerate(((above, nothing), (middle, above), (below, middle), (nothing, below))):
            for col, piece in enumerate(pieces):
                bands[member, place_ * SIDE : (place_ + 1) * SIDE, col * SIDE : (col + 1) * SIDE] = piece


def match_kernel(
    peers, warped, bands, near, other, weight, coef, owner, slot, me_ref, keep, send, image, total
):
    rows, width = warped.shape
    me = me_ref[0]
    boxes = PS * BH
    total[...] = jnp.zeros_like(total)
    heavy = weight[...].astype(jnp.float32)
    for box in range(rows // BH * (width // BW)):
        down, col = divmod(box, width // BW)
        spot = place(owner[0, box], me, peers)
        far = spot // (peers // 2)
        here = (spot - far * (peers // 2)) * boxes + slot[0, box] * BH
        piece = pl.ds(pl.multiple_of(here, BH), BH)
        image[down * BH : (down + 1) * BH, col * BW : (col + 1) * BW] = jnp.where(
            far == 0, near[piece, :], other[piece, :]
        )
    for block, (low, high, top, bottom) in enumerate(windows(width)):
        blurred = [
            jnp.dot(image[:, low:high], bands[member, top:bottom, :], preferred_element_type=jnp.float32).astype(
                jnp.bfloat16
            )
            for member in range(bands.shape[0])
        ]
        matched = jnp.zeros((rows, WIDE), jnp.float32)
        for member in range(bands.shape[0]):
            matched = matched + coef[0, member] * jnp.dot(
                bands[member, SIDE : SIDE + rows, :], blurred[member], preferred_element_type=jnp.float32
            )
        ours = warped[:, block * WIDE : (block + 1) * WIDE].astype(jnp.float32)
        difference = (ours - matched).astype(jnp.bfloat16)
        add_boxes(peers, boxes, me, total, difference.astype(jnp.float32) * heavy, owner, slot, block, width)
    store_slots(peers, boxes, total, keep, send)


def shards(
    visit_image,
    band_offset,
    shift_frac,
    weights,
    box_owner,
    box_slot,
    basis_index,
    basis_coef,
    basis_width,
):
    peers = lax.axis_size("visit")
    rows, width = visit_image.shape[1:]
    bases = basis_index.shape[1]
    owner = box_owner.reshape(1, -1)
    me = lax.axis_index("visit").astype(jnp.int32).reshape(1)
    weight = weights.reshape(1, 1)
    boxes = PS * BH
    chunk = boxes + tag_rows(peers)

    half = jax.ShapeDtypeStruct((peers // 2 * chunk, BW), jnp.bfloat16)
    warped, keep, send = pl.pallas_call(
        functools.partial(warp_kernel, peers),
        out_shape=[jax.ShapeDtypeStruct((rows, width), jnp.bfloat16), half, half],
        in_specs=[VMEM, VMEM, SMEM, HBM, HBM, HBM, HBM],
        out_specs=[VMEM] * 3,
        scratch_shapes=[
            pltpu.VMEM((peers * chunk, BW), jnp.float32),
            pltpu.VMEM((WIDE + 2 * SIDE, WIDE), jnp.bfloat16),
            pltpu.SMEM(band_offset.shape, jnp.int32),
            pltpu.SMEM(shift_frac.shape, jnp.float32),
            pltpu.SMEM(owner.shape, jnp.int32),
            pltpu.SMEM(box_slot.shape, jnp.int32),
            pltpu.SemaphoreType.DMA((4,)),
        ],
        compiler_params=params(),
        name="warp",
    )(visit_image[0], weight, me, band_offset, shift_frac, owner, box_slot)

    bands = pl.pallas_call(
        gauss_kernel,
        out_shape=jax.ShapeDtypeStruct((bases, WIDE + 2 * SIDE, WIDE), jnp.bfloat16),
        in_specs=[SMEM, SMEM],
        out_specs=VMEM,
        compiler_params=params(),
        name="gauss_bands",
    )(basis_index, basis_width)

    terms = scatter_sum(keep, send, peers)
    template, weight_sum = pl.pallas_call(
        template_kernel,
        out_shape=[
            jax.ShapeDtypeStruct((boxes, BW), jnp.bfloat16),
            jax.ShapeDtypeStruct((PS, BW), jnp.float32),
        ],
        in_specs=[VMEM] * len(terms),
        out_specs=[VMEM] * 2,
        compiler_params=params(),
        name="template",
    )(*terms)
    near, other = gather_slots(template, peers)

    half = jax.ShapeDtypeStruct((peers // 2 * boxes, BW), jnp.bfloat16)
    keep, send = pl.pallas_call(
        functools.partial(match_kernel, peers),
        out_shape=[half, half],
        in_specs=[VMEM] * 5 + [SMEM] * 4,
        out_specs=[VMEM] * 2,
        scratch_shapes=[
            pltpu.VMEM((rows, width), jnp.bfloat16),
            pltpu.VMEM((peers * boxes, BW), jnp.float32),
        ],
        compiler_params=params(),
        name="match",
    )(warped, bands, near, other, weight, basis_coef, owner, box_slot, me)
    terms = scatter_sum(keep, send, peers)
    difference_coadd = pl.pallas_call(
        difference_kernel,
        out_shape=jax.ShapeDtypeStruct((boxes, BW), jnp.float32),
        in_specs=[VMEM] * (1 + len(terms)),
        out_specs=VMEM,
        compiler_params=params(),
        name="difference_coadd",
    )(weight_sum, *terms)
    return (template.reshape(PS, BH, BW), difference_coadd.reshape(PS, BH, BW))


def solution(mesh):
    placed = (
        P(("groups", "visit"), None, None),
        P(("groups", "visit"), None),
        P(("groups", "visit"), None),
        P(("groups", "visit")),
        P(("groups", "visit"), None, None),
        P(("groups", "visit"), None),
        P(("groups", "visit"), None),
        P(("groups", "visit"), None),
        P(),
    )
    return jax.shard_map(
        shards,
        mesh=mesh,
        in_specs=placed,
        out_specs=(P(("groups", "visit"), None, None), P(("groups", "visit"), None, None)),
        check_vma=False,
    )
```

```python
import functools

import jax
import jax.numpy as jnp
from jax import lax
from jax.experimental import pallas as pl
from jax.experimental.pallas import tpu as pltpu
from jax.sharding import PartitionSpec as P

BH = 16
BW = 128
PS = 16
BOXES = PS * BH
SIDE = 128
WIDE = 256
LEAN = 64
TALL = 2 * BH
GROUP = 8

band_reach = 8.0

VMEM = pl.BlockSpec(memory_space=pltpu.VMEM)
SMEM = pl.BlockSpec(memory_space=pltpu.SMEM)


def params():
    return pltpu.CompilerParams(vmem_limit_bytes=48 * 1024 * 1024)


def place(owner, me, peers):
    away = jnp.bitwise_xor(owner, me)
    return (away & 1) * (peers // 2) + ((away >> 1) & 1) * (peers // 4) + (away >> 2)


def name_tiles(peers):
    return 1 if peers * PS <= 256 else 2


def chunk_rows(peers):
    return BOXES + (name_tiles(peers) + 1) * peers


def windows(width):
    found = []
    for first in range(0, width, WIDE):
        low, high = max(first - SIDE, 0), min(first + WIDE + SIDE, width)
        found.append((low, high, low - first + SIDE, high - first + SIDE))
    return found


def turned(x, by):
    return pltpu.roll(x, by % BW, 1)


def lanczos_taps(gap, whole, part):
    shift = whole + part
    band = jnp.zeros(gap.shape, jnp.float32)
    for tap in range(-2, 5):
        spot = whole + tap
        x = jnp.full((8, 128), spot - shift, jnp.float32)

        def sinc(v):
            angle = jnp.pi * v
            return jnp.where(v == 0.0, 1.0, jnp.sin(angle) / jnp.where(v == 0.0, 1.0, angle))

        value = jnp.where(jnp.abs(x) < 3.0, sinc(x) * sinc(x / 3.0), 0.0)
        band = jnp.where(gap == spot, value[0:1, 0:1], band)
    return band.astype(jnp.bfloat16)


OWNER, SLOT, MISC = 0, 1, 2
OFFSET, FRACTION, WEIGHT, BASES = 0, 2, 4, 5


def pack(owner, slot, band_offset, shift_frac, weight, basis_index, basis_coef):
    def line(x):
        return x.astype(jnp.float32).reshape(1, -1)

    misc = jnp.concatenate([line(x) for x in (band_offset, shift_frac, weight, basis_index, basis_coef)], axis=1)
    misc = jnp.pad(misc, ((0, 0), (0, BW - misc.shape[1])))
    return jnp.concatenate([line(owner), line(slot), misc, jnp.zeros((5, BW), jnp.float32)], axis=0)


def warp_kernel(peers, bases, picture, packed, scalars, me_ref, keep, send, total, wide_band, spots, starts, sem):
    rows, width = picture.shape
    me = me_ref[0]
    chunk = chunk_rows(peers)
    half = peers // 2 * chunk
    named = packed[OWNER : OWNER + 1, :].astype(jnp.int32)
    slots = packed[SLOT : SLOT + 1, :].astype(jnp.int32)
    spots[...] = (place(named, me, peers) * PS + slots) * BH
    copy = pltpu.make_async_copy(spots, starts, sem)
    copy.start()
    total[...] = jnp.zeros_like(total)

    heavy = packed[MISC : MISC + 1, WEIGHT : WEIGHT + 1]
    mean = jnp.sum(jnp.sum(picture[...].astype(jnp.float32), axis=0, keepdims=True), axis=1, keepdims=True)
    mean = (mean * (1.0 / (rows * width))).astype(jnp.bfloat16).astype(jnp.float32)

    if name_tiles(peers) == 1:
        names = [packed[OWNER : OWNER + 1, :] * PS + packed[SLOT : SLOT + 1, :]]
    else:
        names = [packed[OWNER : OWNER + 1, :], packed[SLOT : SLOT + 1, :]]
    misc = packed[MISC : MISC + 1, :]
    lane = lax.broadcasted_iota(jnp.int32, (1, BW), 1)

    def lanes(x, first, count, to):
        moved = turned(jnp.broadcast_to(x, (8, BW)), to - first)[0:1]
        return jnp.where((lane >= to) & (lane < to + count), moved, 0.0)

    high = misc.astype(jnp.bfloat16).astype(jnp.float32)
    middle = (misc - high).astype(jnp.bfloat16).astype(jnp.float32)
    low = misc - high - middle
    numbers = lanes(misc, BASES, bases, 0)
    for i, piece in enumerate((high, middle, low)):
        numbers = numbers + lanes(piece, BASES + bases, bases, (1 + i) * bases)
    numbers = numbers + jnp.where(lane == 4 * bases, heavy, 0.0) + jnp.where(lane == 4 * bases + 1, mean, 0.0)
    row = lax.broadcasted_iota(jnp.int32, (peers, BW), 0)
    tags = jnp.concatenate(
        [jnp.where(row == me, x, 0.0).astype(jnp.bfloat16) for x in (*names, numbers)], axis=0
    )

    gap = (
        lax.broadcasted_iota(jnp.int32, (WIDE + 2 * SIDE, WIDE), 0)
        - lax.broadcasted_iota(jnp.int32, (WIDE + 2 * SIDE, WIDE), 1)
        - SIDE
    ).astype(jnp.float32)
    wide_band[...] = lanczos_taps(gap, scalars[MISC, OFFSET + 1], scalars[MISC, FRACTION + 1])
    gap = (
        lax.broadcasted_iota(jnp.int32, (rows, rows), 1) - lax.broadcasted_iota(jnp.int32, (rows, rows), 0)
    ).astype(jnp.float32)
    row_warp = lanczos_taps(gap, scalars[MISC, OFFSET], scalars[MISC, FRACTION])
    passes = [
        jnp.dot(
            picture[:, low:high], wide_band[top:bottom, :], preferred_element_type=jnp.float32
        ).astype(jnp.bfloat16)
        for low, high, top, bottom in windows(width)
    ]
    copy.wait()
    across = WIDE // BW
    for block, col_pass in enumerate(passes):
        done = jnp.dot(row_warp, col_pass, preferred_element_type=jnp.float32).astype(jnp.bfloat16)
        scaled = (done.astype(jnp.float32) - mean) * heavy
        for down in range(rows // BH):
            for col in range(across):
                box = down * (width // BW) + block * across + col
                piece = pl.ds(pl.multiple_of(starts[0, box], BH), BH)
                total[piece, :] += scaled[down * BH : (down + 1) * BH, col * BW : (col + 1) * BW]

    @pl.loop(0, peers // 2)
    def _(i):
        start = pl.multiple_of(i * chunk, PS)
        for out, base in ((keep, 0), (send, peers // 2 * BOXES)):
            source = pl.multiple_of(base + i * BOXES, BOXES)
            out[pl.ds(start, BOXES), :] = total[pl.ds(source, BOXES), :].astype(jnp.bfloat16)
            out[pl.ds(start + BOXES, chunk - BOXES), :] = tags


def add_kernel(parts, ours, theirs, *outs):
    length = ours.shape[0] // parts
    for i, out in enumerate(outs):
        here = pl.ds(i * length, length)
        out[...] = (ours[here, :].astype(jnp.float32) + theirs[here, :].astype(jnp.float32)).astype(jnp.bfloat16)


def add_parts(ours, theirs, parts):
    length = ours.shape[0] // parts
    return pl.pallas_call(
        functools.partial(add_kernel, parts),
        out_shape=[jax.ShapeDtypeStruct((length, BW), jnp.bfloat16)] * parts,
        in_specs=[VMEM, VMEM],
        out_specs=[VMEM] * parts,
        compiler_params=params(),
        name="add_parts",
    )(ours, theirs)


def swap(x, axis_size, bit):
    return lax.ppermute(x, "visit", [(i, i ^ bit) for i in range(axis_size)])


def scatter_sum(keep, send, peers):
    near = swap(send, peers, 1)
    ours, theirs = add_parts(keep, near, 2)
    near = swap(theirs, peers, 2)
    terms = add_parts(ours, near, peers // 4)
    return [terms[0]] + [swap(terms[far], peers, 4 * far) for far in reversed(range(1, peers // 4))]


def join_kernel(*refs):
    *parts, out = refs
    length = parts[0].shape[0]
    for i, part in enumerate(parts):
        out[i * length : (i + 1) * length, :] = part[...]


def join(*parts):
    rows, lanes = parts[0].shape
    return pl.pallas_call(
        join_kernel,
        out_shape=jax.ShapeDtypeStruct((rows * len(parts), lanes), parts[0].dtype),
        in_specs=[VMEM] * len(parts),
        out_specs=VMEM,
        compiler_params=params(),
        name="join",
    )(*parts)


def gather_slots(own, peers):
    line = join(own, *[swap(own, peers, 4 * away) for away in range(1, peers // 4)])
    pair = join(line, swap(line, peers, 2))
    return pair, swap(pair, peers, 1)


def summed_terms(terms, here):
    total = terms[0][here, :].astype(jnp.float32)
    for term in terms[1:]:
        total = total + term[here, :].astype(jnp.float32)
    return total


def read_tags(peers, terms):
    tiles = [
        summed_terms(terms, slice(BOXES + i * peers, BOXES + (i + 1) * peers)) for i in range(name_tiles(peers) + 1)
    ]
    if name_tiles(peers) == 1:
        name = tiles[0].astype(jnp.int32)
        owner, slot = name >> 4, name & (PS - 1)
    else:
        owner, slot = tiles[0].astype(jnp.int32), tiles[1].astype(jnp.int32)
    return owner, slot, tiles[-1]


def template_kernel(peers, bases, me_ref, *refs):
    *terms, template, leaning, coadd, weight_sum = refs
    me = me_ref[0]
    owner, slot, numbers = read_tags(peers, terms)
    heavy = numbers[:, 4 * bases : 4 * bases + 1]
    level = heavy * numbers[:, 4 * bases + 1 : 4 * bases + 2]
    mine = owner == me
    for i in range(PS):
        hit = mine & (slot == i)

        def over(x):
            found = jnp.sum(jnp.where(hit, x, 0.0), axis=0, keepdims=True)
            return jnp.sum(found, axis=1, keepdims=True)

        total = 1.0 + over(heavy)
        here = slice(i * BH, (i + 1) * BH)
        mean = (summed_terms(terms, here) + over(level)) / total
        rounded = mean.astype(jnp.bfloat16)
        template[here, :] = rounded
        leaning[here, :] = turned(rounded.astype(jnp.float32), LEAN).astype(jnp.bfloat16)
        coadd[here, :] = mean
        weight_sum[i : i + 1, :] = jnp.broadcast_to(total, (1, BW))


AROUND = [(down, across) for down in (-1, 0, 1) for across in (-1, 0, 1)]


def plan_kernel(peers, bases, most, rows_of_boxes, me_ref, *refs):
    *terms, spots, scales = refs
    me = me_ref[0]
    owner, slot, numbers = read_tags(peers, terms)
    nothing = peers * PS
    tile = place(owner, me, peers) * PS + slot
    boxes = owner.shape[1]
    cols = boxes // rows_of_boxes
    box = lax.broadcasted_iota(jnp.int32, (peers, BW), 1)
    lane = lax.broadcasted_iota(jnp.int32, (peers, BW), 1)
    mine = owner == me
    before = (
        lax.broadcasted_iota(jnp.int32, (boxes, boxes), 0) < lax.broadcasted_iota(jnp.int32, (boxes, boxes), 1)
    )
    rank = jnp.dot(
        jnp.where(mine, 1.0, 0.0).astype(jnp.bfloat16),
        jnp.where(before, 1.0, 0.0).astype(jnp.bfloat16),
        preferred_element_type=jnp.float32,
    ).astype(jnp.int32)
    tables = []
    for down, across in AROUND:
        row, col = box // cols + down, box % cols + across
        inside = (row >= 0) & (row < rows_of_boxes) & (col >= 0) & (col < cols)
        moved = turned(tile, -(down * cols + across)) if (down, across) != (0, 0) else tile
        tables.append(jnp.where(inside, moved - nothing, 0).astype(jnp.float32))
    tables.append((slot - PS).astype(jnp.float32))
    first = jnp.zeros((peers, BW), jnp.float32)
    second = jnp.zeros((peers, BW), jnp.float32)
    for j in range(most):
        chosen = mine & (rank == j)
        for i, table in enumerate(tables):
            value = jnp.sum(jnp.where(chosen, table, 0.0), axis=1, keepdims=True)
            value = value + (nothing if i < 9 else PS)
            if i < 8:
                first = jnp.where(lane == i * most + j, value, first)
            else:
                second = jnp.where(lane == (i - 8) * most + j, value, second)
    index = turned(numbers, 2 * most)
    second = jnp.where((lane >= 2 * most) & (lane < 2 * most + bases), index, second)
    spots[0:peers, :] = (first * BH).astype(jnp.int32)
    spots[peers : 2 * peers, :] = (jnp.where(lane < 2 * most, second * BH, second)).astype(jnp.int32)
    coef = turned(numbers, -bases) + turned(numbers, -2 * bases) + turned(numbers, -3 * bases)
    heavy = numbers[:, 4 * bases : 4 * bases + 1]
    scales[...] = jnp.where(lane < bases, coef * heavy, 0.0)


def gauss_kernel(basis_width, across_bands, down_bands):
    tap = lax.broadcasted_iota(jnp.int32, (8, 128), 1).astype(jnp.float32) - band_reach
    shape = across_bands.shape[1:]
    across_gap = (
        lax.broadcasted_iota(jnp.int32, shape, 0) - lax.broadcasted_iota(jnp.int32, shape, 1) - LEAN
    ).astype(jnp.float32)
    shape = down_bands.shape[1:]
    out_row = lax.broadcasted_iota(jnp.int32, shape, 0)
    in_row = lax.broadcasted_iota(jnp.int32, shape, 1)
    inner = in_row % TALL
    down_gap = jnp.where(inner < BH + BH // 2, inner, inner - TALL) - out_row % BH
    down_gap = jnp.where(out_row // BH == in_row // TALL, down_gap, 1024).astype(jnp.float32)
    for member in range(across_bands.shape[0]):
        blur_width = basis_width[member]
        spread = 2.0 * blur_width * blur_width
        total = jnp.sum(jnp.where(tap <= band_reach, jnp.exp(-tap * tap / spread), 0.0), axis=1, keepdims=True)[0:1]
        for gap, out in ((across_gap, across_bands), (down_gap, down_bands)):
            value = jnp.where(jnp.abs(gap) <= band_reach, jnp.exp(-gap * gap / spread), 0.0)
            out[member] = (value / total).astype(jnp.bfloat16)


def match_kernel(
    peers,
    bases,
    most,
    steps,
    near,
    other,
    across_bands,
    down_bands,
    coadd,
    weight_sum,
    spots,
    scales,
    out,
    table,
    window,
    blurred,
    matched,
):
    groups = pl.cdiv(most, GROUP)
    high = GROUP * TALL
    half = near.shape[0]
    table[0:half, :] = near[...]
    table[half : 2 * half, :] = other[...]
    table[2 * half :, :] = jnp.zeros((BH, BW), jnp.bfloat16)
    matched[...] = jnp.zeros_like(matched)
    if most % GROUP:
        window[...] = jnp.zeros_like(window)
    lane = lax.broadcasted_iota(jnp.int32, (BH, BW), 1)
    row = lax.broadcasted_iota(jnp.int32, (BH, BW), 0)
    left = lane < LEAN
    upper = row < BH // 2

    @pl.loop(0, peers // steps)
    def _(turn):
        for step in range(steps):
            visit = turn * steps + step
            for j in range(most):

                def tile(i):
                    at = spots[visit, i * most + j] if i < 8 else spots[peers + visit, j]
                    return table[pl.ds(pl.multiple_of(at, BH), BH), :]

                tiles = [tile(i) for i in range(9)]
                mixed = [jnp.where(upper, tiles[6 + i], tiles[i]) for i in range(3)]
                start = (step * groups * GROUP + j) * TALL
                for base, (west, middle, east) in ((0, tiles[3:6]), (BH, mixed)):
                    window[start + base : start + base + BH, 0:BW] = jnp.where(left, west, middle)
                    window[start + base : start + base + BH, BW:] = jnp.where(left, middle, east)
        for step in range(steps):
            visit = turn * steps + step
            here = slice(step * groups * high, (step + 1) * groups * high)
            for member in range(0, bases, 2):
                pair = range(member, min(member + 2, bases))
                band = [across_bands[spots[peers + visit, 2 * most + k]] for k in pair]
                band = jnp.concatenate(band, axis=1) if len(band) > 1 else band[0]
                blurred[here, member * BW : member * BW + band.shape[1]] = jnp.dot(
                    window[here, :], band, preferred_element_type=jnp.float32
                ).astype(jnp.bfloat16)
        for step in range(steps):
            visit = turn * steps + step
            for group in range(groups):
                here = slice((step * groups + group) * high, (step * groups + group + 1) * high)
                total = jnp.zeros((GROUP * BH, BW), jnp.float32)
                for k in range(bases):
                    total = total + scales[visit, k] * jnp.dot(
                        down_bands[spots[peers + visit, 2 * most + k]],
                        blurred[here, k * BW : (k + 1) * BW],
                        preferred_element_type=jnp.float32,
                    )
                for i in range(min(GROUP, most - group * GROUP)):
                    at = spots[peers + visit, most + group * GROUP + i]
                    matched[pl.ds(pl.multiple_of(at, BH), BH), :] += total[i * BH : (i + 1) * BH]

    for i in range(PS):
        here = slice(i * BH, (i + 1) * BH)
        out[here, :] = coadd[here, :] - matched[here, :] / weight_sum[i : i + 1, :]


def shards(
    visit_image,
    band_offset,
    shift_frac,
    weights,
    box_owner,
    box_slot,
    basis_index,
    basis_coef,
    basis_width,
):
    peers = lax.axis_size("visit")
    rows, width = visit_image.shape[1:]
    bases = basis_index.shape[1]
    table_size = basis_width.shape[0]
    most = max(2, 2 * box_slot.shape[1] // peers)
    me = lax.axis_index("visit").astype(jnp.int32).reshape(1)
    chunk = chunk_rows(peers)
    packed = pack(box_owner, box_slot, band_offset, shift_frac, weights, basis_index, basis_coef)

    half = jax.ShapeDtypeStruct((peers // 2 * chunk, BW), jnp.bfloat16)
    keep, send = pl.pallas_call(
        functools.partial(warp_kernel, peers, bases),
        out_shape=[half, half],
        in_specs=[VMEM, VMEM, SMEM, SMEM],
        out_specs=[VMEM] * 2,
        scratch_shapes=[
            pltpu.VMEM((peers * BOXES, BW), jnp.float32),
            pltpu.VMEM((WIDE + 2 * SIDE, WIDE), jnp.bfloat16),
            pltpu.VMEM((1, BW), jnp.int32),
            pltpu.SMEM((1, BW), jnp.int32),
            pltpu.SemaphoreType.DMA,
        ],
        compiler_params=params(),
        name="warp",
    )(visit_image[0], packed, packed, me)

    across_bands, down_bands = pl.pallas_call(
        gauss_kernel,
        out_shape=[
            jax.ShapeDtypeStruct((table_size, BW + 2 * LEAN, BW), jnp.bfloat16),
            jax.ShapeDtypeStruct((table_size, GROUP * BH, GROUP * TALL), jnp.bfloat16),
        ],
        in_specs=[SMEM],
        out_specs=[VMEM] * 2,
        compiler_params=params(),
        name="gauss_bands",
    )(basis_width)

    terms = scatter_sum(keep, send, peers)
    square = jax.ShapeDtypeStruct((BOXES, BW), jnp.bfloat16)
    template, leaning, coadd, weight_sum = pl.pallas_call(
        functools.partial(template_kernel, peers, bases),
        out_shape=[
            square,
            square,
            jax.ShapeDtypeStruct((BOXES, BW), jnp.float32),
            jax.ShapeDtypeStruct((PS, BW), jnp.float32),
        ],
        in_specs=[SMEM] + [VMEM] * len(terms),
        out_specs=[VMEM] * 4,
        compiler_params=params(),
        name="template",
    )(me, *terms)
    near, other = gather_slots(leaning, peers)
    spots, scales = pl.pallas_call(
        functools.partial(plan_kernel, peers, bases, most, rows // BH),
        out_shape=[
            jax.ShapeDtypeStruct((2 * peers, BW), jnp.int32),
            jax.ShapeDtypeStruct((peers, BW), jnp.float32),
        ],
        in_specs=[SMEM] + [VMEM] * len(terms),
        out_specs=[VMEM] * 2,
        compiler_params=params(),
        name="plan",
    )(me, *terms)

    steps = 4
    tall = steps * pl.cdiv(most, GROUP) * GROUP * TALL
    difference_coadd = pl.pallas_call(
        functools.partial(match_kernel, peers, bases, most, steps),
        out_shape=jax.ShapeDtypeStruct((BOXES, BW), jnp.float32),
        in_specs=[VMEM] * 6 + [SMEM] * 2,
        out_specs=VMEM,
        scratch_shapes=[
            pltpu.VMEM(((peers * PS + 1) * BH, BW), jnp.bfloat16),
            pltpu.VMEM((tall, BW + 2 * LEAN), jnp.bfloat16),
            pltpu.VMEM((tall, bases * BW), jnp.bfloat16),
            pltpu.VMEM(((PS + 1) * BH, BW), jnp.float32),
        ],
        compiler_params=params(),
        name="match",
    )(near, other, across_bands, down_bands, coadd, weight_sum, spots, scales)
    return (template.reshape(PS, BH, BW), difference_coadd.reshape(PS, BH, BW))


def solution(mesh):
    placed = (
        P(("groups", "visit"), None, None),
        P(("groups", "visit"), None),
        P(("groups", "visit"), None),
        P(("groups", "visit")),
        P(("groups", "visit"), None, None),
        P(("groups", "visit"), None),
        P(("groups", "visit"), None),
        P(("groups", "visit"), None),
        P(),
    )
    return jax.shard_map(
        shards,
        mesh=mesh,
        in_specs=placed,
        out_specs=(P(("groups", "visit"), None, None), P(("groups", "visit"), None, None)),
        check_vma=False,
    )
```

```python
import functools

import jax
import jax.numpy as jnp
from jax import lax
from jax.experimental import pallas as pl
from jax.experimental.pallas import tpu as pltpu
from jax.sharding import PartitionSpec as P

BH = 16
BW = 128
PS = 16
BOXES = PS * BH
SIDE = 128
WIDE = 256
LEAN = 64
TALL = 2 * BH
GROUP = 8

band_reach = 8.0

VMEM = pl.BlockSpec(memory_space=pltpu.VMEM)
SMEM = pl.BlockSpec(memory_space=pltpu.SMEM)


def params():
    return pltpu.CompilerParams(vmem_limit_bytes=48 * 1024 * 1024)


def place(owner, me, peers):
    away = jnp.bitwise_xor(owner, me)
    return (away & 1) * (peers // 2) + ((away >> 1) & 1) * (peers // 4) + (away >> 2)


def name_tiles(peers):
    return 1 if peers * PS <= 256 else 2


def chunk_rows(peers):
    return BOXES + (name_tiles(peers) + 1) * peers


def windows(width):
    found = []
    for first in range(0, width, WIDE):
        low, high = max(first - SIDE, 0), min(first + WIDE + SIDE, width)
        found.append((low, high, low - first + SIDE, high - first + SIDE))
    return found


def turned(x, by):
    return pltpu.roll(x, by % BW, 1)


def lanczos_taps(gap, whole, part):
    shift = whole + part
    band = jnp.zeros(gap.shape, jnp.float32)
    for tap in range(-2, 5):
        spot = whole + tap
        x = jnp.full((8, 128), spot - shift, jnp.float32)

        def sinc(v):
            angle = jnp.pi * v
            return jnp.where(v == 0.0, 1.0, jnp.sin(angle) / jnp.where(v == 0.0, 1.0, angle))

        value = jnp.where(jnp.abs(x) < 3.0, sinc(x) * sinc(x / 3.0), 0.0)
        band = jnp.where(gap == spot, value[0:1, 0:1], band)
    return band.astype(jnp.bfloat16)


OWNER, SLOT, MISC = 0, 1, 2
OFFSET, FRACTION, WEIGHT, BASES = 0, 2, 4, 5


def pack(owner, slot, band_offset, shift_frac, weight, basis_index, basis_coef):
    def put(x, row, lane):
        x = x.astype(jnp.float32).reshape(1, -1)
        return jnp.pad(x, ((row, 7 - row), (lane, BW - lane - x.shape[1])))

    bases = basis_index.shape[1]
    return (
        put(owner, OWNER, 0)
        + put(slot, SLOT, 0)
        + put(band_offset, MISC, OFFSET)
        + put(shift_frac, MISC, FRACTION)
        + put(weight, MISC, WEIGHT)
        + put(basis_index, MISC, BASES)
        + put(basis_coef, MISC, BASES + bases)
    )


def warp_kernel(peers, bases, picture, packed, scalars, me_ref, keep, send, total, wide_band, spots, starts, sem):
    rows, width = picture.shape
    me = me_ref[0]
    chunk = chunk_rows(peers)
    half = peers // 2 * chunk
    named = packed[OWNER : OWNER + 1, :].astype(jnp.int32)
    slots = packed[SLOT : SLOT + 1, :].astype(jnp.int32)
    spots[...] = (place(named, me, peers) * PS + slots) * BH
    copy = pltpu.make_async_copy(spots, starts, sem)
    copy.start()
    total[...] = jnp.zeros_like(total)

    heavy = packed[MISC : MISC + 1, WEIGHT : WEIGHT + 1]
    mean = jnp.sum(jnp.sum(picture[...].astype(jnp.float32), axis=0, keepdims=True), axis=1, keepdims=True)
    mean = (mean * (1.0 / (rows * width))).astype(jnp.bfloat16).astype(jnp.float32)

    if name_tiles(peers) == 1:
        names = [packed[OWNER : OWNER + 1, :] * PS + packed[SLOT : SLOT + 1, :]]
    else:
        names = [packed[OWNER : OWNER + 1, :], packed[SLOT : SLOT + 1, :]]
    misc = packed[MISC : MISC + 1, :]
    lane = lax.broadcasted_iota(jnp.int32, (1, BW), 1)

    def lanes(x, first, count, to):
        moved = turned(jnp.broadcast_to(x, (8, BW)), to - first)[0:1]
        return jnp.where((lane >= to) & (lane < to + count), moved, 0.0)

    high = misc.astype(jnp.bfloat16).astype(jnp.float32)
    middle = (misc - high).astype(jnp.bfloat16).astype(jnp.float32)
    low = misc - high - middle
    numbers = lanes(misc, BASES, bases, 0)
    for i, piece in enumerate((high, middle, low)):
        numbers = numbers + lanes(piece, BASES + bases, bases, (1 + i) * bases)
    numbers = numbers + jnp.where(lane == 4 * bases, heavy, 0.0) + jnp.where(lane == 4 * bases + 1, mean, 0.0)
    row = lax.broadcasted_iota(jnp.int32, (peers, BW), 0)
    tags = jnp.concatenate(
        [jnp.where(row == me, x, 0.0).astype(jnp.bfloat16) for x in (*names, numbers)], axis=0
    )

    gap = (
        lax.broadcasted_iota(jnp.int32, (WIDE + 2 * SIDE, WIDE), 0)
        - lax.broadcasted_iota(jnp.int32, (WIDE + 2 * SIDE, WIDE), 1)
        - SIDE
    ).astype(jnp.float32)
    wide_band[...] = lanczos_taps(gap, scalars[MISC, OFFSET + 1], scalars[MISC, FRACTION + 1])
    gap = (
        lax.broadcasted_iota(jnp.int32, (rows, rows), 1) - lax.broadcasted_iota(jnp.int32, (rows, rows), 0)
    ).astype(jnp.float32)
    row_warp = lanczos_taps(gap, scalars[MISC, OFFSET], scalars[MISC, FRACTION])
    passes = [
        jnp.dot(
            picture[:, low:high], wide_band[top:bottom, :], preferred_element_type=jnp.float32
        ).astype(jnp.bfloat16)
        for low, high, top, bottom in windows(width)
    ]
    copy.wait()
    across = WIDE // BW
    for block, col_pass in enumerate(passes):
        done = jnp.dot(row_warp, col_pass, preferred_element_type=jnp.float32).astype(jnp.bfloat16)
        scaled = (done.astype(jnp.float32) - mean) * heavy
        for down in range(rows // BH):
            for col in range(across):
                box = down * (width // BW) + block * across + col
                piece = pl.ds(pl.multiple_of(starts[0, box], BH), BH)
                total[piece, :] += scaled[down * BH : (down + 1) * BH, col * BW : (col + 1) * BW]

    @pl.loop(0, peers // 2)
    def _(i):
        start = pl.multiple_of(i * chunk, PS)
        for out, base in ((keep, 0), (send, peers // 2 * BOXES)):
            source = pl.multiple_of(base + i * BOXES, BOXES)
            out[pl.ds(start, BOXES), :] = total[pl.ds(source, BOXES), :].astype(jnp.bfloat16)
            out[pl.ds(start + BOXES, chunk - BOXES), :] = tags


def add_kernel(parts, ours, theirs, *outs):
    length = ours.shape[0] // parts
    for i, out in enumerate(outs):
        here = pl.ds(i * length, length)
        out[...] = (ours[here, :].astype(jnp.float32) + theirs[here, :].astype(jnp.float32)).astype(jnp.bfloat16)


def add_parts(ours, theirs, parts):
    length = ours.shape[0] // parts
    return pl.pallas_call(
        functools.partial(add_kernel, parts),
        out_shape=[jax.ShapeDtypeStruct((length, BW), jnp.bfloat16)] * parts,
        in_specs=[VMEM, VMEM],
        out_specs=[VMEM] * parts,
        compiler_params=params(),
        name="add_parts",
    )(ours, theirs)


def swap(x, axis_size, bit):
    return lax.ppermute(x, "visit", [(i, i ^ bit) for i in range(axis_size)])


def scatter_sum(keep, send, peers):
    near = swap(send, peers, 1)
    ours, theirs = add_parts(keep, near, 2)
    near = swap(theirs, peers, 2)
    terms = add_parts(ours, near, peers // 4)
    return [terms[0]] + [swap(terms[far], peers, 4 * far) for far in reversed(range(1, peers // 4))]


def join_kernel(*refs):
    *parts, out = refs
    length = parts[0].shape[0]
    for i, part in enumerate(parts):
        out[i * length : (i + 1) * length, :] = part[...]


def join(*parts):
    rows, lanes = parts[0].shape
    return pl.pallas_call(
        join_kernel,
        out_shape=jax.ShapeDtypeStruct((rows * len(parts), lanes), parts[0].dtype),
        in_specs=[VMEM] * len(parts),
        out_specs=VMEM,
        compiler_params=params(),
        name="join",
    )(*parts)


def gather_slots(own, peers):
    line = join(own, *[swap(own, peers, 4 * away) for away in range(1, peers // 4)])
    pair = join(line, swap(line, peers, 2))
    return pair, swap(pair, peers, 1)


def summed_terms(terms, here):
    total = terms[0][here, :].astype(jnp.float32)
    for term in terms[1:]:
        total = total + term[here, :].astype(jnp.float32)
    return total


def read_tags(peers, terms):
    tiles = [
        summed_terms(terms, slice(BOXES + i * peers, BOXES + (i + 1) * peers)) for i in range(name_tiles(peers) + 1)
    ]
    if name_tiles(peers) == 1:
        name = tiles[0].astype(jnp.int32)
        owner, slot = name >> 4, name & (PS - 1)
    else:
        owner, slot = tiles[0].astype(jnp.int32), tiles[1].astype(jnp.int32)
    return owner, slot, tiles[-1]


def template_kernel(peers, bases, me_ref, *refs):
    *terms, template, leaning, coadd, weight_sum = refs
    me = me_ref[0]
    owner, slot, numbers = read_tags(peers, terms)
    heavy = numbers[:, 4 * bases : 4 * bases + 1]
    level = heavy * numbers[:, 4 * bases + 1 : 4 * bases + 2]
    mine = owner == me
    for i in range(PS):
        hit = mine & (slot == i)

        def over(x):
            found = jnp.sum(jnp.where(hit, x, 0.0), axis=0, keepdims=True)
            return jnp.sum(found, axis=1, keepdims=True)

        total = 1.0 + over(heavy)
        here = slice(i * BH, (i + 1) * BH)
        mean = (summed_terms(terms, here) + over(level)) / total
        rounded = mean.astype(jnp.bfloat16)
        template[here, :] = rounded
        leaning[here, :] = turned(rounded.astype(jnp.float32), LEAN).astype(jnp.bfloat16)
        coadd[here, :] = mean
        weight_sum[i : i + 1, :] = jnp.broadcast_to(total, (1, BW))


AROUND = [(down, across) for down in (-1, 0, 1) for across in (-1, 0, 1)]


def plan_kernel(peers, bases, most, rows_of_boxes, me_ref, *refs):
    *terms, spots, scales = refs
    me = me_ref[0]
    owner, slot, numbers = read_tags(peers, terms)
    nothing = peers * PS
    tile = place(owner, me, peers) * PS + slot
    boxes = owner.shape[1]
    cols = boxes // rows_of_boxes
    box = lax.broadcasted_iota(jnp.int32, (peers, BW), 1)
    lane = lax.broadcasted_iota(jnp.int32, (peers, BW), 1)
    mine = owner == me
    before = (
        lax.broadcasted_iota(jnp.int32, (boxes, boxes), 0) < lax.broadcasted_iota(jnp.int32, (boxes, boxes), 1)
    )
    rank = jnp.dot(
        jnp.where(mine, 1.0, 0.0).astype(jnp.bfloat16),
        jnp.where(before, 1.0, 0.0).astype(jnp.bfloat16),
        preferred_element_type=jnp.float32,
    ).astype(jnp.int32)
    tables = []
    for down, across in AROUND:
        row, col = box // cols + down, box % cols + across
        inside = (row >= 0) & (row < rows_of_boxes) & (col >= 0) & (col < cols)
        moved = turned(tile, -(down * cols + across)) if (down, across) != (0, 0) else tile
        tables.append(jnp.where(inside, moved - nothing, 0).astype(jnp.float32))
    tables.append((slot - PS).astype(jnp.float32))
    first = jnp.zeros((peers, BW), jnp.float32)
    second = jnp.zeros((peers, BW), jnp.float32)
    for j in range(most):
        chosen = mine & (rank == j)
        for i, table in enumerate(tables):
            value = jnp.sum(jnp.where(chosen, table, 0.0), axis=1, keepdims=True)
            value = value + (nothing if i < 9 else PS)
            if i < 8:
                first = jnp.where(lane == i * most + j, value, first)
            else:
                second = jnp.where(lane == (i - 8) * most + j, value, second)
    index = turned(numbers, 2 * most)
    second = jnp.where((lane >= 2 * most) & (lane < 2 * most + bases), index, second)
    spots[0:peers, :] = (first * BH).astype(jnp.int32)
    spots[peers : 2 * peers, :] = (jnp.where(lane < 2 * most, second * BH, second)).astype(jnp.int32)
    coef = turned(numbers, -bases) + turned(numbers, -2 * bases) + turned(numbers, -3 * bases)
    heavy = numbers[:, 4 * bases : 4 * bases + 1]
    scales[...] = jnp.where(lane < bases, coef * heavy, 0.0)


def gauss_kernel(basis_width, across_bands, down_bands):
    tap = lax.broadcasted_iota(jnp.int32, (8, 128), 1).astype(jnp.float32) - band_reach
    shape = across_bands.shape[1:]
    across_gap = (
        lax.broadcasted_iota(jnp.int32, shape, 0) - lax.broadcasted_iota(jnp.int32, shape, 1) - LEAN
    ).astype(jnp.float32)
    shape = down_bands.shape[1:]
    out_row = lax.broadcasted_iota(jnp.int32, shape, 0)
    in_row = lax.broadcasted_iota(jnp.int32, shape, 1)
    inner = in_row % TALL
    down_gap = jnp.where(inner < BH + BH // 2, inner, inner - TALL) - out_row % BH
    down_gap = jnp.where(out_row // BH == in_row // TALL, down_gap, 1024).astype(jnp.float32)
    for member in range(across_bands.shape[0]):
        blur_width = basis_width[member]
        spread = 2.0 * blur_width * blur_width
        total = jnp.sum(jnp.where(tap <= band_reach, jnp.exp(-tap * tap / spread), 0.0), axis=1, keepdims=True)[0:1]
        for gap, out in ((across_gap, across_bands), (down_gap, down_bands)):
            value = jnp.where(jnp.abs(gap) <= band_reach, jnp.exp(-gap * gap / spread), 0.0)
            out[member] = (value / total).astype(jnp.bfloat16)


def match_kernel(
    peers,
    bases,
    most,
    steps,
    near,
    other,
    across_bands,
    down_bands,
    coadd,
    weight_sum,
    spots,
    scales,
    out,
    table,
    window,
    blurred,
    matched,
):
    groups = pl.cdiv(most, GROUP)
    high = GROUP * TALL
    half = near.shape[0]
    table[0:half, :] = near[...]
    table[half : 2 * half, :] = other[...]
    table[2 * half :, :] = jnp.zeros((BH, BW), jnp.bfloat16)
    matched[...] = jnp.zeros_like(matched)
    if most % GROUP:
        window[...] = jnp.zeros_like(window)
    lane = lax.broadcasted_iota(jnp.int32, (BH, BW), 1)
    row = lax.broadcasted_iota(jnp.int32, (BH, BW), 0)
    left = lane < LEAN
    upper = row < BH // 2

    @pl.loop(0, peers // steps)
    def _(turn):
        for step in range(steps):
            visit = turn * steps + step
            for j in range(most):

                def tile(i):
                    at = spots[visit, i * most + j] if i < 8 else spots[peers + visit, j]
                    return table[pl.ds(pl.multiple_of(at, BH), BH), :]

                tiles = [tile(i) for i in range(9)]
                mixed = [jnp.where(upper, tiles[6 + i], tiles[i]) for i in range(3)]
                start = (step * groups * GROUP + j) * TALL
                for base, (west, middle, east) in ((0, tiles[3:6]), (BH, mixed)):
                    window[start + base : start + base + BH, 0:BW] = jnp.where(left, west, middle)
                    window[start + base : start + base + BH, BW:] = jnp.where(left, middle, east)
        for step in range(steps):
            visit = turn * steps + step
            here = slice(step * groups * high, (step + 1) * groups * high)
            for member in range(0, bases, 2):
                pair = range(member, min(member + 2, bases))
                band = [across_bands[spots[peers + visit, 2 * most + k]] for k in pair]
                band = jnp.concatenate(band, axis=1) if len(band) > 1 else band[0]
                blurred[here, member * BW : member * BW + band.shape[1]] = jnp.dot(
                    window[here, :], band, preferred_element_type=jnp.float32
                ).astype(jnp.bfloat16)
        for step in range(steps):
            visit = turn * steps + step
            parts = [slice((step * groups + i) * high, (step * groups + i + 1) * high) for i in range(groups)]
            total = jnp.zeros((GROUP * BH, groups * BW), jnp.float32)
            for k in range(bases):
                side = [blurred[here, k * BW : (k + 1) * BW] for here in parts]
                side = jnp.concatenate(side, axis=1) if groups > 1 else side[0]
                total = total + scales[visit, k] * jnp.dot(
                    down_bands[spots[peers + visit, 2 * most + k]], side, preferred_element_type=jnp.float32
                )
            for j in range(most):
                group, i = divmod(j, GROUP)
                at = spots[peers + visit, most + j]
                matched[pl.ds(pl.multiple_of(at, BH), BH), :] += total[
                    i * BH : (i + 1) * BH, group * BW : (group + 1) * BW
                ]

    for i in range(PS):
        here = slice(i * BH, (i + 1) * BH)
        out[here, :] = coadd[here, :] - matched[here, :] / weight_sum[i : i + 1, :]


def shards(
    visit_image,
    band_offset,
    shift_frac,
    weights,
    box_owner,
    box_slot,
    basis_index,
    basis_coef,
    basis_width,
):
    peers = lax.axis_size("visit")
    rows, width = visit_image.shape[1:]
    bases = basis_index.shape[1]
    table_size = basis_width.shape[0]
    most = max(2, 2 * box_slot.shape[1] // peers)
    me = lax.axis_index("visit").astype(jnp.int32).reshape(1)
    chunk = chunk_rows(peers)
    packed = pack(box_owner, box_slot, band_offset, shift_frac, weights, basis_index, basis_coef)

    half = jax.ShapeDtypeStruct((peers // 2 * chunk, BW), jnp.bfloat16)
    keep, send = pl.pallas_call(
        functools.partial(warp_kernel, peers, bases),
        out_shape=[half, half],
        in_specs=[VMEM, VMEM, SMEM, SMEM],
        out_specs=[VMEM] * 2,
        scratch_shapes=[
            pltpu.VMEM((peers * BOXES, BW), jnp.float32),
            pltpu.VMEM((WIDE + 2 * SIDE, WIDE), jnp.bfloat16),
            pltpu.VMEM((1, BW), jnp.int32),
            pltpu.SMEM((1, BW), jnp.int32),
            pltpu.SemaphoreType.DMA,
        ],
        compiler_params=params(),
        name="warp",
    )(visit_image[0], packed, packed, me)

    across_bands, down_bands = pl.pallas_call(
        gauss_kernel,
        out_shape=[
            jax.ShapeDtypeStruct((table_size, BW + 2 * LEAN, BW), jnp.bfloat16),
            jax.ShapeDtypeStruct((table_size, GROUP * BH, GROUP * TALL), jnp.bfloat16),
        ],
        in_specs=[SMEM],
        out_specs=[VMEM] * 2,
        compiler_params=params(),
        name="gauss_bands",
    )(basis_width)

    terms = scatter_sum(keep, send, peers)
    square = jax.ShapeDtypeStruct((BOXES, BW), jnp.bfloat16)
    template, leaning, coadd, weight_sum = pl.pallas_call(
        functools.partial(template_kernel, peers, bases),
        out_shape=[
            square,
            square,
            jax.ShapeDtypeStruct((BOXES, BW), jnp.float32),
            jax.ShapeDtypeStruct((PS, BW), jnp.float32),
        ],
        in_specs=[SMEM] + [VMEM] * len(terms),
        out_specs=[VMEM] * 4,
        compiler_params=params(),
        name="template",
    )(me, *terms)
    near, other = gather_slots(leaning, peers)
    spots, scales = pl.pallas_call(
        functools.partial(plan_kernel, peers, bases, most, rows // BH),
        out_shape=[
            jax.ShapeDtypeStruct((2 * peers, BW), jnp.int32),
            jax.ShapeDtypeStruct((peers, BW), jnp.float32),
        ],
        in_specs=[SMEM] + [VMEM] * len(terms),
        out_specs=[VMEM] * 2,
        compiler_params=params(),
        name="plan",
    )(me, *terms)

    steps = min(peers, 16)
    tall = steps * pl.cdiv(most, GROUP) * GROUP * TALL
    difference_coadd = pl.pallas_call(
        functools.partial(match_kernel, peers, bases, most, steps),
        out_shape=jax.ShapeDtypeStruct((BOXES, BW), jnp.float32),
        in_specs=[VMEM] * 6 + [SMEM] * 2,
        out_specs=VMEM,
        scratch_shapes=[
            pltpu.VMEM(((peers * PS + 1) * BH, BW), jnp.bfloat16),
            pltpu.VMEM((tall, BW + 2 * LEAN), jnp.bfloat16),
            pltpu.VMEM((tall, bases * BW), jnp.bfloat16),
            pltpu.VMEM(((PS + 1) * BH, BW), jnp.float32),
        ],
        compiler_params=params(),
        name="match",
    )(near, other, across_bands, down_bands, coadd, weight_sum, spots, scales)
    return (template.reshape(PS, BH, BW), difference_coadd.reshape(PS, BH, BW))


def solution(mesh):
    placed = (
        P(("groups", "visit"), None, None),
        P(("groups", "visit"), None),
        P(("groups", "visit"), None),
        P(("groups", "visit")),
        P(("groups", "visit"), None, None),
        P(("groups", "visit"), None),
        P(("groups", "visit"), None),
        P(("groups", "visit"), None),
        P(),
    )
    return jax.shard_map(
        shards,
        mesh=mesh,
        in_specs=placed,
        out_specs=(P(("groups", "visit"), None, None), P(("groups", "visit"), None, None)),
        check_vma=False,
    )
```

```python
import functools

import jax
import jax.numpy as jnp
from jax import lax
from jax.experimental import pallas as pl
from jax.experimental.pallas import tpu as pltpu
from jax.sharding import PartitionSpec as P

BH = 16
BW = 128
PS = 16
BOXES = PS * BH
SIDE = 128
WIDE = 256
LEAN = 64
TALL = 2 * BH
GROUP = 8

band_reach = 8.0

VMEM = pl.BlockSpec(memory_space=pltpu.VMEM)
SMEM = pl.BlockSpec(memory_space=pltpu.SMEM)
ANY = pl.BlockSpec(memory_space=pl.ANY)


def params():
    return pltpu.CompilerParams(vmem_limit_bytes=48 * 1024 * 1024)


def place(owner, me, peers):
    away = jnp.bitwise_xor(owner, me)
    return (away & 1) * (peers // 2) + ((away >> 1) & 1) * (peers // 4) + (away >> 2)


def name_tiles(peers):
    return 1 if peers * PS <= 256 else 2


def chunk_rows(peers):
    return BOXES + (name_tiles(peers) + 1) * peers


def windows(width):
    found = []
    for first in range(0, width, WIDE):
        low, high = max(first - SIDE, 0), min(first + WIDE + SIDE, width)
        found.append((low, high, low - first + SIDE, high - first + SIDE))
    return found


def turned(x, by):
    return pltpu.roll(x, by % BW, 1)


def lanczos_taps(gap, whole, part):
    shift = whole + part
    band = jnp.zeros(gap.shape, jnp.float32)
    for tap in range(-2, 5):
        spot = whole + tap
        x = jnp.full((8, 128), spot - shift, jnp.float32)

        def sinc(v):
            angle = jnp.pi * v
            return jnp.where(v == 0.0, 1.0, jnp.sin(angle) / jnp.where(v == 0.0, 1.0, angle))

        value = jnp.where(jnp.abs(x) < 3.0, sinc(x) * sinc(x / 3.0), 0.0)
        band = jnp.where(gap == spot, value[0:1, 0:1], band)
    return band.astype(jnp.bfloat16)


def warp_kernel(
    peers,
    bases,
    me_ref,
    picture_in,
    owner_in,
    slot_in,
    offset_in,
    fraction_in,
    weight_in,
    index_in,
    coef_in,
    keep,
    send,
    picture,
    owner,
    slot,
    offset,
    fraction,
    weight,
    index,
    coef,
    total,
    wide_band,
    spots,
    starts,
    sems,
):
    rows, width = picture.shape
    me = me_ref[0]
    chunk = chunk_rows(peers)
    sources = (owner_in, slot_in, offset_in, fraction_in, weight_in, index_in, coef_in, picture_in)
    targets = (owner, slot, offset, fraction, weight, index, coef, picture)
    copies = [pltpu.make_async_copy(x, y, sems.at[i]) for i, (x, y) in enumerate(zip(sources, targets))]
    for copy in copies:
        copy.start()
    total[...] = jnp.zeros_like(total)
    for copy in copies[:-1]:
        copy.wait()
    spots[...] = (place(owner[...], me, peers) * PS + slot[...]) * BH
    turn_in = pltpu.make_async_copy(spots, starts, sems.at[len(copies)])
    turn_in.start()

    gap = (
        lax.broadcasted_iota(jnp.int32, (WIDE + 2 * SIDE, WIDE), 0)
        - lax.broadcasted_iota(jnp.int32, (WIDE + 2 * SIDE, WIDE), 1)
        - SIDE
    ).astype(jnp.float32)
    wide_band[...] = lanczos_taps(gap, offset[0, 1].astype(jnp.float32), fraction[0, 1])
    gap = (
        lax.broadcasted_iota(jnp.int32, (rows, rows), 1) - lax.broadcasted_iota(jnp.int32, (rows, rows), 0)
    ).astype(jnp.float32)
    row_warp = lanczos_taps(gap, offset[0, 0].astype(jnp.float32), fraction[0, 0])
    heavy = weight[...].astype(jnp.float32)
    named, slotted = owner[...].astype(jnp.float32), slot[...].astype(jnp.float32)
    names = [named * PS + slotted] if name_tiles(peers) == 1 else [named, slotted]
    lane = lax.broadcasted_iota(jnp.int32, (8, BW), 1)
    numbers = jnp.zeros((8, BW), jnp.float32)
    share = jnp.zeros((8, BW), jnp.float32)
    for k in range(bases):
        numbers = jnp.where(lane == k, index[0, k].astype(jnp.float32), numbers)
        share = jnp.where(lane == k, coef[0, k], share)
    for i in range(1, 4):
        piece = share.astype(jnp.bfloat16).astype(jnp.float32)
        share = share - piece
        numbers = numbers + turned(piece, i * bases)
    numbers = jnp.where(lane == 4 * bases, heavy, numbers)

    copies[-1].wait()
    mean = jnp.sum(jnp.sum(picture[...].astype(jnp.float32), axis=0, keepdims=True), axis=1, keepdims=True)
    mean = (mean * (1.0 / (rows * width))).astype(jnp.bfloat16).astype(jnp.float32)
    numbers = jnp.where(lane == 4 * bases + 1, mean, numbers)[0:1]
    row = lax.broadcasted_iota(jnp.int32, (peers, BW), 0)
    tags = jnp.concatenate(
        [jnp.where(row == me, x, 0.0).astype(jnp.bfloat16) for x in (*names, numbers)], axis=0
    )
    passes = [
        jnp.dot(
            picture[:, low:high], wide_band[top:bottom, :], preferred_element_type=jnp.float32
        ).astype(jnp.bfloat16)
        for low, high, top, bottom in windows(width)
    ]
    turn_in.wait()
    across = WIDE // BW
    for block, col_pass in enumerate(passes):
        done = jnp.dot(row_warp, col_pass, preferred_element_type=jnp.float32).astype(jnp.bfloat16)
        scaled = (done.astype(jnp.float32) - mean) * heavy
        for down in range(rows // BH):
            for col in range(across):
                box = down * (width // BW) + block * across + col
                piece = pl.ds(pl.multiple_of(starts[0, box], BH), BH)
                total[piece, :] += scaled[down * BH : (down + 1) * BH, col * BW : (col + 1) * BW]

    @pl.loop(0, peers // 2)
    def _(i):
        start = pl.multiple_of(i * chunk, PS)
        for out, base in ((keep, 0), (send, peers // 2 * BOXES)):
            source = pl.multiple_of(base + i * BOXES, BOXES)
            out[pl.ds(start, BOXES), :] = total[pl.ds(source, BOXES), :].astype(jnp.bfloat16)
            out[pl.ds(start + BOXES, chunk - BOXES), :] = tags


def add_kernel(parts, ours, theirs, *outs):
    length = ours.shape[0] // parts
    for i, out in enumerate(outs):
        here = pl.ds(i * length, length)
        out[...] = (ours[here, :].astype(jnp.float32) + theirs[here, :].astype(jnp.float32)).astype(jnp.bfloat16)


def add_parts(ours, theirs, parts):
    length = ours.shape[0] // parts
    return pl.pallas_call(
        functools.partial(add_kernel, parts),
        out_shape=[jax.ShapeDtypeStruct((length, BW), jnp.bfloat16)] * parts,
        in_specs=[VMEM, VMEM],
        out_specs=[VMEM] * parts,
        compiler_params=params(),
        name="add_parts",
    )(ours, theirs)


def swap(x, axis_size, bit):
    return lax.ppermute(x, "visit", [(i, i ^ bit) for i in range(axis_size)])


def scatter_sum(keep, send, peers):
    near = swap(send, peers, 1)
    ours, theirs = add_parts(keep, near, 2)
    near = swap(theirs, peers, 2)
    terms = add_parts(ours, near, peers // 4)
    return [terms[0]] + [swap(terms[far], peers, 4 * far) for far in reversed(range(1, peers // 4))]


def join_kernel(*refs):
    *parts, out = refs
    length = parts[0].shape[0]
    for i, part in enumerate(parts):
        out[i * length : (i + 1) * length, :] = part[...]


def join(*parts):
    rows, lanes = parts[0].shape
    return pl.pallas_call(
        join_kernel,
        out_shape=jax.ShapeDtypeStruct((rows * len(parts), lanes), parts[0].dtype),
        in_specs=[VMEM] * len(parts),
        out_specs=VMEM,
        compiler_params=params(),
        name="join",
    )(*parts)


def gather_slots(own, peers):
    line = join(own, *[swap(own, peers, 4 * away) for away in range(1, peers // 4)])
    pair = join(line, swap(line, peers, 2))
    return pair, swap(pair, peers, 1)


def summed_terms(terms, here):
    total = terms[0][here, :].astype(jnp.float32)
    for term in terms[1:]:
        total = total + term[here, :].astype(jnp.float32)
    return total


def read_tags(peers, terms):
    tiles = [
        summed_terms(terms, slice(BOXES + i * peers, BOXES + (i + 1) * peers)) for i in range(name_tiles(peers) + 1)
    ]
    if name_tiles(peers) == 1:
        name = tiles[0].astype(jnp.int32)
        owner, slot = name >> 4, name & (PS - 1)
    else:
        owner, slot = tiles[0].astype(jnp.int32), tiles[1].astype(jnp.int32)
    return owner, slot, tiles[-1]


def template_kernel(peers, bases, me_ref, *refs):
    *terms, template, leaning, coadd, weight_sum = refs
    me = me_ref[0]
    owner, slot, numbers = read_tags(peers, terms)
    heavy = numbers[:, 4 * bases : 4 * bases + 1]
    level = heavy * numbers[:, 4 * bases + 1 : 4 * bases + 2]
    mine = owner == me
    for i in range(PS):
        hit = mine & (slot == i)

        def over(x):
            found = jnp.sum(jnp.where(hit, x, 0.0), axis=0, keepdims=True)
            return jnp.sum(found, axis=1, keepdims=True)

        total = 1.0 + over(heavy)
        here = slice(i * BH, (i + 1) * BH)
        mean = (summed_terms(terms, here) + over(level)) / total
        rounded = mean.astype(jnp.bfloat16)
        template[here, :] = rounded
        leaning[here, :] = turned(rounded.astype(jnp.float32), LEAN).astype(jnp.bfloat16)
        coadd[here, :] = mean
        weight_sum[i : i + 1, :] = jnp.broadcast_to(total, (1, BW))


AROUND = [(down, across) for down in (-1, 0, 1) for across in (-1, 0, 1)]


def plan_kernel(peers, bases, most, rows_of_boxes, me_ref, *refs):
    *terms, spots, scales = refs
    me = me_ref[0]
    owner, slot, numbers = read_tags(peers, terms)
    nothing = peers * PS
    tile = place(owner, me, peers) * PS + slot
    boxes = owner.shape[1]
    cols = boxes // rows_of_boxes
    box = lax.broadcasted_iota(jnp.int32, (peers, BW), 1)
    lane = lax.broadcasted_iota(jnp.int32, (peers, BW), 1)
    mine = owner == me
    before = (
        lax.broadcasted_iota(jnp.int32, (boxes, boxes), 0) < lax.broadcasted_iota(jnp.int32, (boxes, boxes), 1)
    )
    rank = jnp.dot(
        jnp.where(mine, 1.0, 0.0).astype(jnp.bfloat16),
        jnp.where(before, 1.0, 0.0).astype(jnp.bfloat16),
        preferred_element_type=jnp.float32,
    ).astype(jnp.int32)
    tables = []
    for down, across in AROUND:
        row, col = box // cols + down, box % cols + across
        inside = (row >= 0) & (row < rows_of_boxes) & (col >= 0) & (col < cols)
        moved = turned(tile, -(down * cols + across)) if (down, across) != (0, 0) else tile
        tables.append(jnp.where(inside, moved - nothing, 0).astype(jnp.float32))
    tables.append((slot - PS).astype(jnp.float32))
    first = jnp.zeros((peers, BW), jnp.float32)
    second = jnp.zeros((peers, BW), jnp.float32)
    for j in range(most):
        chosen = mine & (rank == j)
        for i, table in enumerate(tables):
            value = jnp.sum(jnp.where(chosen, table, 0.0), axis=1, keepdims=True)
            value = value + (nothing if i < 9 else PS)
            if i < 8:
                first = jnp.where(lane == i * most + j, value, first)
            else:
                second = jnp.where(lane == (i - 8) * most + j, value, second)
    index = turned(numbers, 2 * most)
    second = jnp.where((lane >= 2 * most) & (lane < 2 * most + bases), index, second)
    spots[0:peers, :] = (first * BH).astype(jnp.int32)
    spots[peers : 2 * peers, :] = (jnp.where(lane < 2 * most, second * BH, second)).astype(jnp.int32)
    coef = turned(numbers, -bases) + turned(numbers, -2 * bases) + turned(numbers, -3 * bases)
    heavy = numbers[:, 4 * bases : 4 * bases + 1]
    scales[...] = jnp.where(lane < bases, coef * heavy, 0.0)


def gauss_kernel(basis_width, across_bands, down_bands):
    tap = lax.broadcasted_iota(jnp.int32, (8, 128), 1).astype(jnp.float32) - band_reach
    shape = across_bands.shape[1:]
    across_gap = (
        lax.broadcasted_iota(jnp.int32, shape, 0) - lax.broadcasted_iota(jnp.int32, shape, 1) - LEAN
    ).astype(jnp.float32)
    shape = down_bands.shape[1:]
    out_row = lax.broadcasted_iota(jnp.int32, shape, 0)
    in_row = lax.broadcasted_iota(jnp.int32, shape, 1)
    inner = in_row % TALL
    down_gap = jnp.where(inner < BH + BH // 2, inner, inner - TALL) - out_row % BH
    down_gap = jnp.where(out_row // BH == in_row // TALL, down_gap, 1024).astype(jnp.float32)
    for member in range(across_bands.shape[0]):
        blur_width = basis_width[member]
        spread = 2.0 * blur_width * blur_width
        total = jnp.sum(jnp.where(tap <= band_reach, jnp.exp(-tap * tap / spread), 0.0), axis=1, keepdims=True)[0:1]
        for gap, out in ((across_gap, across_bands), (down_gap, down_bands)):
            value = jnp.where(jnp.abs(gap) <= band_reach, jnp.exp(-gap * gap / spread), 0.0)
            out[member] = (value / total).astype(jnp.bfloat16)


def match_kernel(
    peers,
    bases,
    most,
    steps,
    near,
    other,
    across_bands,
    down_bands,
    coadd,
    weight_sum,
    spots,
    scales,
    out,
    table,
    window,
    blurred,
    matched,
):
    groups = pl.cdiv(most, GROUP)
    high = GROUP * TALL
    half = near.shape[0]
    table[0:half, :] = near[...]
    table[half : 2 * half, :] = other[...]
    table[2 * half :, :] = jnp.zeros((BH, BW), jnp.bfloat16)
    matched[...] = jnp.zeros_like(matched)
    if most % GROUP:
        window[...] = jnp.zeros_like(window)
    lane = lax.broadcasted_iota(jnp.int32, (BH, BW), 1)
    row = lax.broadcasted_iota(jnp.int32, (BH, BW), 0)
    left = lane < LEAN
    upper = row < BH // 2

    @pl.loop(0, peers // steps)
    def _(turn):
        for step in range(steps):
            visit = turn * steps + step
            for j in range(most):

                def tile(i):
                    at = spots[visit, i * most + j] if i < 8 else spots[peers + visit, j]
                    return table[pl.ds(pl.multiple_of(at, BH), BH), :]

                tiles = [tile(i) for i in range(9)]
                mixed = [jnp.where(upper, tiles[6 + i], tiles[i]) for i in range(3)]
                start = (step * groups * GROUP + j) * TALL
                for base, (west, middle, east) in ((0, tiles[3:6]), (BH, mixed)):
                    window[start + base : start + base + BH, 0:BW] = jnp.where(left, west, middle)
                    window[start + base : start + base + BH, BW:] = jnp.where(left, middle, east)
        for step in range(steps):
            visit = turn * steps + step
            here = slice(step * groups * high, (step + 1) * groups * high)
            for member in range(0, bases, 2):
                pair = range(member, min(member + 2, bases))
                band = [across_bands[spots[peers + visit, 2 * most + k]] for k in pair]
                band = jnp.concatenate(band, axis=1) if len(band) > 1 else band[0]
                blurred[here, member * BW : member * BW + band.shape[1]] = jnp.dot(
                    window[here, :], band, preferred_element_type=jnp.float32
                ).astype(jnp.bfloat16)
        for step in range(steps):
            visit = turn * steps + step
            parts = [slice((step * groups + i) * high, (step * groups + i + 1) * high) for i in range(groups)]
            total = jnp.zeros((GROUP * BH, groups * BW), jnp.float32)
            for k in range(bases):
                side = [blurred[here, k * BW : (k + 1) * BW] for here in parts]
                side = jnp.concatenate(side, axis=1) if groups > 1 else side[0]
                total = total + scales[visit, k] * jnp.dot(
                    down_bands[spots[peers + visit, 2 * most + k]], side, preferred_element_type=jnp.float32
                )
            for j in range(most):
                group, i = divmod(j, GROUP)
                at = spots[peers + visit, most + j]
                matched[pl.ds(pl.multiple_of(at, BH), BH), :] += total[
                    i * BH : (i + 1) * BH, group * BW : (group + 1) * BW
                ]

    for i in range(PS):
        here = slice(i * BH, (i + 1) * BH)
        out[here, :] = coadd[here, :] - matched[here, :] / weight_sum[i : i + 1, :]


def shards(
    visit_image,
    band_offset,
    shift_frac,
    weights,
    box_owner,
    box_slot,
    basis_index,
    basis_coef,
    basis_width,
):
    peers = lax.axis_size("visit")
    rows, width = visit_image.shape[1:]
    bases = basis_index.shape[1]
    table_size = basis_width.shape[0]
    most = max(2, 2 * box_slot.shape[1] // peers)
    me = lax.axis_index("visit").astype(jnp.int32).reshape(1)
    chunk = chunk_rows(peers)
    owner = box_owner.reshape(1, -1)

    half = jax.ShapeDtypeStruct((peers // 2 * chunk, BW), jnp.bfloat16)
    keep, send = pl.pallas_call(
        functools.partial(warp_kernel, peers, bases),
        out_shape=[half, half],
        in_specs=[SMEM] + [ANY] * 8,
        out_specs=[VMEM] * 2,
        scratch_shapes=[
            pltpu.VMEM((rows, width), jnp.bfloat16),
            pltpu.VMEM(owner.shape, jnp.int32),
            pltpu.VMEM(box_slot.shape, jnp.int32),
            pltpu.SMEM(band_offset.shape, jnp.int32),
            pltpu.SMEM(shift_frac.shape, jnp.float32),
            pltpu.VMEM((1, 1), jnp.bfloat16),
            pltpu.SMEM(basis_index.shape, jnp.int32),
            pltpu.SMEM(basis_coef.shape, jnp.float32),
            pltpu.VMEM((peers * BOXES, BW), jnp.float32),
            pltpu.VMEM((WIDE + 2 * SIDE, WIDE), jnp.bfloat16),
            pltpu.VMEM((1, BW), jnp.int32),
            pltpu.SMEM((1, BW), jnp.int32),
            pltpu.SemaphoreType.DMA((9,)),
        ],
        compiler_params=pltpu.CompilerParams(vmem_limit_bytes=48 * 1024 * 1024),
        name="warp",
    )(
        me,
        visit_image[0],
        owner,
        box_slot,
        band_offset,
        shift_frac,
        weights.reshape(1, 1),
        basis_index,
        basis_coef,
    )

    across_bands, down_bands = pl.pallas_call(
        gauss_kernel,
        out_shape=[
            jax.ShapeDtypeStruct((table_size, BW + 2 * LEAN, BW), jnp.bfloat16),
            jax.ShapeDtypeStruct((table_size, GROUP * BH, GROUP * TALL), jnp.bfloat16),
        ],
        in_specs=[SMEM],
        out_specs=[VMEM] * 2,
        compiler_params=params(),
        name="gauss_bands",
    )(basis_width)

    terms = scatter_sum(keep, send, peers)
    square = jax.ShapeDtypeStruct((BOXES, BW), jnp.bfloat16)
    template, leaning, coadd, weight_sum = pl.pallas_call(
        functools.partial(template_kernel, peers, bases),
        out_shape=[
            square,
            square,
            jax.ShapeDtypeStruct((BOXES, BW), jnp.float32),
            jax.ShapeDtypeStruct((PS, BW), jnp.float32),
        ],
        in_specs=[SMEM] + [VMEM] * len(terms),
        out_specs=[VMEM] * 4,
        compiler_params=params(),
        name="template",
    )(me, *terms)
    near, other = gather_slots(leaning, peers)
    spots, scales = pl.pallas_call(
        functools.partial(plan_kernel, peers, bases, most, rows // BH),
        out_shape=[
            jax.ShapeDtypeStruct((2 * peers, BW), jnp.int32),
            jax.ShapeDtypeStruct((peers, BW), jnp.float32),
        ],
        in_specs=[SMEM] + [VMEM] * len(terms),
        out_specs=[VMEM] * 2,
        compiler_params=params(),
        name="plan",
    )(me, *terms)

    steps = min(peers, 16)
    tall = steps * pl.cdiv(most, GROUP) * GROUP * TALL
    difference_coadd = pl.pallas_call(
        functools.partial(match_kernel, peers, bases, most, steps),
        out_shape=jax.ShapeDtypeStruct((BOXES, BW), jnp.float32),
        in_specs=[VMEM] * 6 + [SMEM] * 2,
        out_specs=VMEM,
        scratch_shapes=[
            pltpu.VMEM(((peers * PS + 1) * BH, BW), jnp.bfloat16),
            pltpu.VMEM((tall, BW + 2 * LEAN), jnp.bfloat16),
            pltpu.VMEM((tall, bases * BW), jnp.bfloat16),
            pltpu.VMEM(((PS + 1) * BH, BW), jnp.float32),
        ],
        compiler_params=params(),
        name="match",
    )(near, other, across_bands, down_bands, coadd, weight_sum, spots, scales)
    return (template.reshape(PS, BH, BW), difference_coadd.reshape(PS, BH, BW))


def solution(mesh):
    placed = (
        P(("groups", "visit"), None, None),
        P(("groups", "visit"), None),
        P(("groups", "visit"), None),
        P(("groups", "visit")),
        P(("groups", "visit"), None, None),
        P(("groups", "visit"), None),
        P(("groups", "visit"), None),
        P(("groups", "visit"), None),
        P(),
    )
    return jax.shard_map(
        shards,
        mesh=mesh,
        in_specs=placed,
        out_specs=(P(("groups", "visit"), None, None), P(("groups", "visit"), None, None)),
        check_vma=False,
    )
```

```python
import functools

import jax
import jax.numpy as jnp
from jax import lax
from jax.experimental import pallas as pl
from jax.experimental.pallas import tpu as pltpu
from jax.sharding import PartitionSpec as P

BH = 16
BW = 128
PS = 16
BOXES = PS * BH
SIDE = 128
WIDE = 256
LEAN = 64
TALL = 2 * BH
GROUP = 8

band_reach = 8.0

VMEM = pl.BlockSpec(memory_space=pltpu.VMEM)
SMEM = pl.BlockSpec(memory_space=pltpu.SMEM)
ANY = pl.BlockSpec(memory_space=pl.ANY)


def params():
    return pltpu.CompilerParams(vmem_limit_bytes=48 * 1024 * 1024)


def place(owner, me, peers):
    away = jnp.bitwise_xor(owner, me)
    return (away & 1) * (peers // 2) + ((away >> 1) & 1) * (peers // 4) + (away >> 2)


def name_tiles(peers):
    return 1 if peers * PS <= 256 else 2


def chunk_rows(peers):
    return BOXES + (name_tiles(peers) + 1) * peers


def windows(width):
    found = []
    for first in range(0, width, WIDE):
        low, high = max(first - SIDE, 0), min(first + WIDE + SIDE, width)
        found.append((low, high, low - first + SIDE, high - first + SIDE))
    return found


def turned(x, by):
    return pltpu.roll(x, by % BW, 1)


def lanczos_taps(whole, part):
    lane = lax.broadcasted_iota(jnp.int32, (8, BW), 1).astype(jnp.float32)
    x = (whole + lane - 2.0) - (whole + part)

    def sinc(v):
        angle = jnp.pi * v
        return jnp.where(v == 0.0, 1.0, jnp.sin(angle) / jnp.where(v == 0.0, 1.0, angle))

    return jnp.where(jnp.abs(x) < 3.0, sinc(x) * sinc(x / 3.0), 0.0)


def lanczos_band(gap, whole, taps):
    band = jnp.zeros(gap.shape, jnp.float32)
    for tap in range(7):
        band = jnp.where(gap == whole + (tap - 2), taps[0:1, tap : tap + 1], band)
    return band.astype(jnp.bfloat16)


def warp_kernel(
    peers,
    bases,
    me_ref,
    picture_in,
    owner_in,
    slot_in,
    offset_in,
    fraction_in,
    weight_in,
    index_in,
    coef_in,
    keep,
    send,
    picture,
    owner,
    slot,
    offset,
    fraction,
    weight,
    index,
    coef,
    total,
    wide_band,
    spots,
    starts,
    sems,
):
    rows, width = picture.shape
    me = me_ref[0]
    chunk = chunk_rows(peers)
    sources = (owner_in, slot_in, offset_in, fraction_in, weight_in, index_in, coef_in, picture_in)
    targets = (owner, slot, offset, fraction, weight, index, coef, picture)
    copies = [pltpu.make_async_copy(x, y, sems.at[i]) for i, (x, y) in enumerate(zip(sources, targets))]
    for copy in copies:
        copy.start()
    total[...] = jnp.zeros_like(total)
    for copy in copies[:-1]:
        copy.wait()
    spots[...] = (place(owner[...], me, peers) * PS + slot[...]) * BH
    turn_in = pltpu.make_async_copy(spots, starts, sems.at[len(copies)])
    turn_in.start()

    whole = offset[0, 1].astype(jnp.float32)
    taps = lanczos_taps(whole, fraction[0, 1])
    place_of = lax.broadcasted_iota(jnp.int32, (SIDE, SIDE), 0) - lax.broadcasted_iota(jnp.int32, (SIDE, SIDE), 1)
    above, middle, below = [
        lanczos_band((place_of - shift).astype(jnp.float32), whole, taps) for shift in (SIDE, 0, -SIDE)
    ]
    nothing = jnp.zeros_like(middle)
    for down, pieces in enumerate(((above, nothing), (middle, above), (below, middle), (nothing, below))):
        for col, piece in enumerate(pieces):
            wide_band[down * SIDE : (down + 1) * SIDE, col * SIDE : (col + 1) * SIDE] = piece
    gap = (
        lax.broadcasted_iota(jnp.int32, (rows, rows), 1) - lax.broadcasted_iota(jnp.int32, (rows, rows), 0)
    ).astype(jnp.float32)
    whole = offset[0, 0].astype(jnp.float32)
    row_warp = lanczos_band(gap, whole, lanczos_taps(whole, fraction[0, 0]))

    heavy = weight[...].astype(jnp.float32)
    named, slotted = owner[...].astype(jnp.float32), slot[...].astype(jnp.float32)
    names = [named * PS + slotted] if name_tiles(peers) == 1 else [named, slotted]
    lane = lax.broadcasted_iota(jnp.int32, (8, BW), 1)
    numbers = jnp.zeros((8, BW), jnp.float32)
    share = jnp.zeros((8, BW), jnp.float32)
    for k in range(bases):
        numbers = jnp.where(lane == k, index[0, k].astype(jnp.float32), numbers)
        share = jnp.where(lane == k, coef[0, k], share)
    for i in range(1, 4):
        piece = share.astype(jnp.bfloat16).astype(jnp.float32)
        share = share - piece
        numbers = numbers + turned(piece, i * bases)
    numbers = jnp.where(lane == 4 * bases, heavy, numbers)

    copies[-1].wait()
    mean = jnp.sum(jnp.sum(picture[...].astype(jnp.float32), axis=0, keepdims=True), axis=1, keepdims=True)
    mean = (mean * (1.0 / (rows * width))).astype(jnp.bfloat16).astype(jnp.float32)
    numbers = jnp.where(lane == 4 * bases + 1, mean, numbers)[0:1]
    row = lax.broadcasted_iota(jnp.int32, (peers, BW), 0)
    tags = jnp.concatenate(
        [jnp.where(row == me, x, 0.0).astype(jnp.bfloat16) for x in (*names, numbers)], axis=0
    )
    passes = [
        jnp.dot(
            picture[:, low:high], wide_band[top:bottom, :], preferred_element_type=jnp.float32
        ).astype(jnp.bfloat16)
        for low, high, top, bottom in windows(width)
    ]
    turn_in.wait()
    across = WIDE // BW
    for block, col_pass in enumerate(passes):
        done = jnp.dot(row_warp, col_pass, preferred_element_type=jnp.float32).astype(jnp.bfloat16)
        scaled = (done.astype(jnp.float32) - mean) * heavy
        for down in range(rows // BH):
            for col in range(across):
                box = down * (width // BW) + block * across + col
                piece = pl.ds(pl.multiple_of(starts[0, box], BH), BH)
                total[piece, :] += scaled[down * BH : (down + 1) * BH, col * BW : (col + 1) * BW]

    @pl.loop(0, peers // 2)
    def _(i):
        start = pl.multiple_of(i * chunk, PS)
        for out, base in ((keep, 0), (send, peers // 2 * BOXES)):
            source = pl.multiple_of(base + i * BOXES, BOXES)
            out[pl.ds(start, BOXES), :] = total[pl.ds(source, BOXES), :].astype(jnp.bfloat16)
            out[pl.ds(start + BOXES, chunk - BOXES), :] = tags


def add_kernel(parts, ours, theirs, *outs):
    length = ours.shape[0] // parts
    for i, out in enumerate(outs):
        here = pl.ds(i * length, length)
        out[...] = (ours[here, :].astype(jnp.float32) + theirs[here, :].astype(jnp.float32)).astype(jnp.bfloat16)


def add_parts(ours, theirs, parts):
    length = ours.shape[0] // parts
    return pl.pallas_call(
        functools.partial(add_kernel, parts),
        out_shape=[jax.ShapeDtypeStruct((length, BW), jnp.bfloat16)] * parts,
        in_specs=[VMEM, VMEM],
        out_specs=[VMEM] * parts,
        compiler_params=params(),
        name="add_parts",
    )(ours, theirs)


def swap(x, axis_size, bit):
    return lax.ppermute(x, "visit", [(i, i ^ bit) for i in range(axis_size)])


def scatter_sum(keep, send, peers):
    near = swap(send, peers, 1)
    ours, theirs = add_parts(keep, near, 2)
    near = swap(theirs, peers, 2)
    terms = add_parts(ours, near, peers // 4)
    return [terms[0]] + [swap(terms[far], peers, 4 * far) for far in reversed(range(1, peers // 4))]


def join_kernel(*refs):
    *parts, out = refs
    length = parts[0].shape[0]
    for i, part in enumerate(parts):
        out[i * length : (i + 1) * length, :] = part[...]


def join(*parts):
    rows, lanes = parts[0].shape
    return pl.pallas_call(
        join_kernel,
        out_shape=jax.ShapeDtypeStruct((rows * len(parts), lanes), parts[0].dtype),
        in_specs=[VMEM] * len(parts),
        out_specs=VMEM,
        compiler_params=params(),
        name="join",
    )(*parts)


def gather_slots(own, peers):
    line = join(own, *[swap(own, peers, 4 * away) for away in range(1, peers // 4)])
    pair = join(line, swap(line, peers, 2))
    return pair, swap(pair, peers, 1)


def summed_terms(terms, here):
    total = terms[0][here, :].astype(jnp.float32)
    for term in terms[1:]:
        total = total + term[here, :].astype(jnp.float32)
    return total


def read_tags(peers, terms):
    tiles = [
        summed_terms(terms, slice(BOXES + i * peers, BOXES + (i + 1) * peers)) for i in range(name_tiles(peers) + 1)
    ]
    if name_tiles(peers) == 1:
        name = tiles[0].astype(jnp.int32)
        owner, slot = name >> 4, name & (PS - 1)
    else:
        owner, slot = tiles[0].astype(jnp.int32), tiles[1].astype(jnp.int32)
    return owner, slot, tiles[-1]


def template_kernel(peers, bases, me_ref, *refs):
    *terms, leaning, coadd, weight_sum = refs
    me = me_ref[0]
    owner, slot, numbers = read_tags(peers, terms)
    heavy = numbers[:, 4 * bases : 4 * bases + 1]
    level = heavy * numbers[:, 4 * bases + 1 : 4 * bases + 2]
    mine = owner == me
    weighed, levelled = [], []
    for i in range(PS):
        hit = mine & (slot == i)
        weighed.append(jnp.sum(jnp.where(hit, heavy, 0.0), axis=0, keepdims=True))
        levelled.append(jnp.sum(jnp.where(hit, level, 0.0), axis=0, keepdims=True))
    total = 1.0 + jnp.sum(jnp.concatenate(weighed, axis=0), axis=1, keepdims=True)
    over = jnp.sum(jnp.concatenate(levelled, axis=0), axis=1, keepdims=True)
    weight_sum[...] = jnp.broadcast_to(total, weight_sum.shape)
    for i in range(PS):
        here = slice(i * BH, (i + 1) * BH)
        mean = (summed_terms(terms, here) + over[i : i + 1, :]) / total[i : i + 1, :]
        rounded = mean.astype(jnp.bfloat16).astype(jnp.float32)
        leaning[here, :] = turned(rounded, LEAN).astype(jnp.bfloat16)
        coadd[here, :] = mean


AROUND = [(down, across) for down in (-1, 0, 1) for across in (-1, 0, 1)]


def plan_kernel(peers, bases, most, rows_of_boxes, me_ref, *refs):
    *terms, spots, scales = refs
    me = me_ref[0]
    owner, slot, numbers = read_tags(peers, terms)
    nothing = peers * PS
    tile = place(owner, me, peers) * PS + slot
    boxes = owner.shape[1]
    cols = boxes // rows_of_boxes
    box = lax.broadcasted_iota(jnp.int32, (peers, BW), 1)
    lane = lax.broadcasted_iota(jnp.int32, (peers, BW), 1)
    mine = owner == me
    before = (
        lax.broadcasted_iota(jnp.int32, (boxes, boxes), 0) < lax.broadcasted_iota(jnp.int32, (boxes, boxes), 1)
    )
    rank = jnp.dot(
        jnp.where(mine, 1.0, 0.0).astype(jnp.bfloat16),
        jnp.where(before, 1.0, 0.0).astype(jnp.bfloat16),
        preferred_element_type=jnp.float32,
    ).astype(jnp.int32)
    tables = []
    for down, across in AROUND:
        row, col = box // cols + down, box % cols + across
        inside = (row >= 0) & (row < rows_of_boxes) & (col >= 0) & (col < cols)
        moved = turned(tile, -(down * cols + across)) if (down, across) != (0, 0) else tile
        tables.append(jnp.where(inside, moved - nothing, 0).astype(jnp.float32))
    tables.append((slot - PS).astype(jnp.float32))
    first = jnp.zeros((peers, BW), jnp.float32)
    second = jnp.zeros((peers, BW), jnp.float32)
    for j in range(most):
        chosen = mine & (rank == j)
        for i, table in enumerate(tables):
            value = jnp.sum(jnp.where(chosen, table, 0.0), axis=1, keepdims=True)
            value = value + (nothing if i < 9 else PS)
            if i < 8:
                first = jnp.where(lane == i * most + j, value, first)
            else:
                second = jnp.where(lane == (i - 8) * most + j, value, second)
    index = turned(numbers, 2 * most)
    second = jnp.where((lane >= 2 * most) & (lane < 2 * most + bases), index, second)
    spots[0:peers, :] = (first * BH).astype(jnp.int32)
    spots[peers : 2 * peers, :] = (jnp.where(lane < 2 * most, second * BH, second)).astype(jnp.int32)
    coef = turned(numbers, -bases) + turned(numbers, -2 * bases) + turned(numbers, -3 * bases)
    heavy = numbers[:, 4 * bases : 4 * bases + 1]
    scales[...] = jnp.where(lane < bases, coef * heavy, 0.0)


def gauss_kernel(basis_width, across_bands, down_bands):
    tap = lax.broadcasted_iota(jnp.int32, (8, 128), 1).astype(jnp.float32) - band_reach
    shape = across_bands.shape[1:]
    across_gap = (
        lax.broadcasted_iota(jnp.int32, shape, 0) - lax.broadcasted_iota(jnp.int32, shape, 1) - LEAN
    ).astype(jnp.float32)
    shape = down_bands.shape[1:]
    out_row = lax.broadcasted_iota(jnp.int32, shape, 0)
    in_row = lax.broadcasted_iota(jnp.int32, shape, 1)
    inner = in_row % TALL
    down_gap = jnp.where(inner < BH + BH // 2, inner, inner - TALL) - out_row % BH
    down_gap = jnp.where(out_row // BH == in_row // TALL, down_gap, 1024).astype(jnp.float32)
    for member in range(across_bands.shape[0]):
        blur_width = basis_width[member]
        spread = 2.0 * blur_width * blur_width
        total = jnp.sum(jnp.where(tap <= band_reach, jnp.exp(-tap * tap / spread), 0.0), axis=1, keepdims=True)[0:1]
        for gap, out in ((across_gap, across_bands), (down_gap, down_bands)):
            value = jnp.where(jnp.abs(gap) <= band_reach, jnp.exp(-gap * gap / spread), 0.0)
            out[member] = (value / total).astype(jnp.bfloat16)


def match_kernel(
    peers,
    bases,
    most,
    steps,
    near,
    other,
    across_bands,
    down_bands,
    coadd,
    weight_sum,
    spots,
    scales,
    template,
    out,
    table,
    window,
    blurred,
    matched,
):
    groups = pl.cdiv(most, GROUP)
    high = GROUP * TALL
    half = near.shape[0]
    table[0:half, :] = near[...]
    table[half : 2 * half, :] = other[...]
    table[2 * half :, :] = jnp.zeros((BH, BW), jnp.bfloat16)
    matched[...] = jnp.zeros_like(matched)
    template[...] = coadd[...].astype(jnp.bfloat16)
    if most % GROUP:
        window[...] = jnp.zeros_like(window)
    lane = lax.broadcasted_iota(jnp.int32, (BH, BW), 1)
    row = lax.broadcasted_iota(jnp.int32, (BH, BW), 0)
    left = lane < LEAN
    upper = row < BH // 2

    @pl.loop(0, peers // steps)
    def _(turn):
        for step in range(steps):
            visit = turn * steps + step
            for j in range(most):

                def tile(i):
                    at = spots[visit, i * most + j] if i < 8 else spots[peers + visit, j]
                    return table[pl.ds(pl.multiple_of(at, BH), BH), :]

                tiles = [tile(i) for i in range(9)]
                mixed = [jnp.where(upper, tiles[6 + i], tiles[i]) for i in range(3)]
                start = (step * groups * GROUP + j) * TALL
                for base, (west, middle, east) in ((0, tiles[3:6]), (BH, mixed)):
                    window[start + base : start + base + BH, 0:BW] = jnp.where(left, west, middle)
                    window[start + base : start + base + BH, BW:] = jnp.where(left, middle, east)
        for step in range(steps):
            visit = turn * steps + step
            here = slice(step * groups * high, (step + 1) * groups * high)
            for member in range(0, bases, 2):
                pair = range(member, min(member + 2, bases))
                band = [across_bands[spots[peers + visit, 2 * most + k]] for k in pair]
                band = jnp.concatenate(band, axis=1) if len(band) > 1 else band[0]
                blurred[here, member * BW : member * BW + band.shape[1]] = jnp.dot(
                    window[here, :], band, preferred_element_type=jnp.float32
                ).astype(jnp.bfloat16)
        for step in range(steps):
            visit = turn * steps + step
            parts = [slice((step * groups + i) * high, (step * groups + i + 1) * high) for i in range(groups)]
            total = jnp.zeros((GROUP * BH, groups * BW), jnp.float32)
            for k in range(bases):
                side = [blurred[here, k * BW : (k + 1) * BW] for here in parts]
                side = jnp.concatenate(side, axis=1) if groups > 1 else side[0]
                total = total + scales[visit, k] * jnp.dot(
                    down_bands[spots[peers + visit, 2 * most + k]], side, preferred_element_type=jnp.float32
                )
            for j in range(most):
                group, i = divmod(j, GROUP)
                at = spots[peers + visit, most + j]
                matched[pl.ds(pl.multiple_of(at, BH), BH), :] += total[
                    i * BH : (i + 1) * BH, group * BW : (group + 1) * BW
                ]

    for i in range(PS):
        here = slice(i * BH, (i + 1) * BH)
        out[here, :] = coadd[here, :] - matched[here, :] / weight_sum[i : i + 1, :]


def shards(
    visit_image,
    band_offset,
    shift_frac,
    weights,
    box_owner,
    box_slot,
    basis_index,
    basis_coef,
    basis_width,
):
    peers = lax.axis_size("visit")
    rows, width = visit_image.shape[1:]
    bases = basis_index.shape[1]
    table_size = basis_width.shape[0]
    most = max(2, 2 * box_slot.shape[1] // peers)
    me = lax.axis_index("visit").astype(jnp.int32).reshape(1)
    chunk = chunk_rows(peers)
    owner = box_owner.reshape(1, -1)

    half = jax.ShapeDtypeStruct((peers // 2 * chunk, BW), jnp.bfloat16)
    keep, send = pl.pallas_call(
        functools.partial(warp_kernel, peers, bases),
        out_shape=[half, half],
        in_specs=[SMEM] + [ANY] * 8,
        out_specs=[VMEM] * 2,
        scratch_shapes=[
            pltpu.VMEM((rows, width), jnp.bfloat16),
            pltpu.VMEM(owner.shape, jnp.int32),
            pltpu.VMEM(box_slot.shape, jnp.int32),
            pltpu.SMEM(band_offset.shape, jnp.int32),
            pltpu.SMEM(shift_frac.shape, jnp.float32),
            pltpu.VMEM((1, 1), jnp.bfloat16),
            pltpu.SMEM(basis_index.shape, jnp.int32),
            pltpu.SMEM(basis_coef.shape, jnp.float32),
            pltpu.VMEM((peers * BOXES, BW), jnp.float32),
            pltpu.VMEM((WIDE + 2 * SIDE, WIDE), jnp.bfloat16),
            pltpu.VMEM((1, BW), jnp.int32),
            pltpu.SMEM((1, BW), jnp.int32),
            pltpu.SemaphoreType.DMA((9,)),
        ],
        compiler_params=pltpu.CompilerParams(vmem_limit_bytes=48 * 1024 * 1024),
        name="warp",
    )(
        me,
        visit_image[0],
        owner,
        box_slot,
        band_offset,
        shift_frac,
        weights.reshape(1, 1),
        basis_index,
        basis_coef,
    )

    across_bands, down_bands = pl.pallas_call(
        gauss_kernel,
        out_shape=[
            jax.ShapeDtypeStruct((table_size, BW + 2 * LEAN, BW), jnp.bfloat16),
            jax.ShapeDtypeStruct((table_size, GROUP * BH, GROUP * TALL), jnp.bfloat16),
        ],
        in_specs=[SMEM],
        out_specs=[VMEM] * 2,
        compiler_params=params(),
        name="gauss_bands",
    )(basis_width)

    terms = scatter_sum(keep, send, peers)
    leaning, coadd, weight_sum = pl.pallas_call(
        functools.partial(template_kernel, peers, bases),
        out_shape=[
            jax.ShapeDtypeStruct((BOXES, BW), jnp.bfloat16),
            jax.ShapeDtypeStruct((BOXES, BW), jnp.float32),
            jax.ShapeDtypeStruct((PS, BW), jnp.float32),
        ],
        in_specs=[SMEM] + [VMEM] * len(terms),
        out_specs=[VMEM] * 3,
        compiler_params=params(),
        name="template",
    )(me, *terms)
    near, other = gather_slots(leaning, peers)
    spots, scales = pl.pallas_call(
        functools.partial(plan_kernel, peers, bases, most, rows // BH),
        out_shape=[
            jax.ShapeDtypeStruct((2 * peers, BW), jnp.int32),
            jax.ShapeDtypeStruct((peers, BW), jnp.float32),
        ],
        in_specs=[SMEM] + [VMEM] * len(terms),
        out_specs=[VMEM] * 2,
        compiler_params=params(),
        name="plan",
    )(me, *terms)

    steps = min(peers, 16)
    tall = steps * pl.cdiv(most, GROUP) * GROUP * TALL
    template, difference_coadd = pl.pallas_call(
        functools.partial(match_kernel, peers, bases, most, steps),
        out_shape=[
            jax.ShapeDtypeStruct((BOXES, BW), jnp.bfloat16),
            jax.ShapeDtypeStruct((BOXES, BW), jnp.float32),
        ],
        in_specs=[VMEM] * 6 + [SMEM] * 2,
        out_specs=[VMEM] * 2,
        scratch_shapes=[
            pltpu.VMEM(((peers * PS + 1) * BH, BW), jnp.bfloat16),
            pltpu.VMEM((tall, BW + 2 * LEAN), jnp.bfloat16),
            pltpu.VMEM((tall, bases * BW), jnp.bfloat16),
            pltpu.VMEM(((PS + 1) * BH, BW), jnp.float32),
        ],
        compiler_params=params(),
        name="match",
    )(near, other, across_bands, down_bands, coadd, weight_sum, spots, scales)
    return (template.reshape(PS, BH, BW), difference_coadd.reshape(PS, BH, BW))


def solution(mesh):
    placed = (
        P(("groups", "visit"), None, None),
        P(("groups", "visit"), None),
        P(("groups", "visit"), None),
        P(("groups", "visit")),
        P(("groups", "visit"), None, None),
        P(("groups", "visit"), None),
        P(("groups", "visit"), None),
        P(("groups", "visit"), None),
        P(),
    )
    return jax.shard_map(
        shards,
        mesh=mesh,
        in_specs=placed,
        out_specs=(P(("groups", "visit"), None, None), P(("groups", "visit"), None, None)),
        check_vma=False,
    )
```

```python
import functools

import jax
import jax.numpy as jnp
from jax import lax
from jax.experimental import pallas as pl
from jax.experimental.pallas import tpu as pltpu
from jax.sharding import PartitionSpec as P

BH = 16
BW = 128
PS = 16
BOXES = PS * BH
SIDE = 128
WIDE = 256
LEAN = 64
TALL = 2 * BH
GROUP = 8

band_reach = 8.0

VMEM = pl.BlockSpec(memory_space=pltpu.VMEM)
SMEM = pl.BlockSpec(memory_space=pltpu.SMEM)
ANY = pl.BlockSpec(memory_space=pl.ANY)


def params():
    return pltpu.CompilerParams(vmem_limit_bytes=48 * 1024 * 1024)


def place(owner, me, peers):
    away = jnp.bitwise_xor(owner, me)
    return (away & 1) * (peers // 2) + ((away >> 1) & 1) * (peers // 4) + (away >> 2)


QUAD = 4
CHUNK = BOXES + BH


def windows(width):
    found = []
    for first in range(0, width, WIDE):
        low, high = max(first - SIDE, 0), min(first + WIDE + SIDE, width)
        found.append((low, high, low - first + SIDE, high - first + SIDE))
    return found


def turned(x, by):
    return pltpu.roll(x, by % BW, 1)


def lanczos_taps(whole, part):
    lane = lax.broadcasted_iota(jnp.int32, (8, BW), 1).astype(jnp.float32)
    x = (whole + lane - 2.0) - (whole + part)

    def sinc(v):
        angle = jnp.pi * v
        return jnp.where(v == 0.0, 1.0, jnp.sin(angle) / jnp.where(v == 0.0, 1.0, angle))

    return jnp.where(jnp.abs(x) < 3.0, sinc(x) * sinc(x / 3.0), 0.0)


def lanczos_band(gap, whole, taps):
    band = jnp.zeros(gap.shape, jnp.float32)
    for tap in range(7):
        band = jnp.where(gap == whole + (tap - 2), taps[0:1, tap : tap + 1], band)
    return band.astype(jnp.bfloat16)


def warp_kernel(
    peers,
    bases,
    me_ref,
    picture_in,
    owner_in,
    slot_in,
    offset_in,
    fraction_in,
    weight_in,
    index_in,
    coef_in,
    keep,
    send,
    picture,
    owner,
    slot,
    offset,
    fraction,
    weight,
    index,
    coef,
    total,
    wide_band,
    spots,
    starts,
    sems,
):
    rows, width = picture.shape
    me = me_ref[0]
    chunk = CHUNK
    sources = (owner_in, slot_in, offset_in, fraction_in, weight_in, index_in, coef_in, picture_in)
    targets = (owner, slot, offset, fraction, weight, index, coef, picture)
    copies = [pltpu.make_async_copy(x, y, sems.at[i]) for i, (x, y) in enumerate(zip(sources, targets))]
    for copy in copies:
        copy.start()
    total[...] = jnp.zeros_like(total)
    for copy in copies[:-1]:
        copy.wait()
    spots[...] = (place(owner[...], me, peers) * PS + slot[...]) * BH
    turn_in = pltpu.make_async_copy(spots, starts, sems.at[len(copies)])
    turn_in.start()

    whole = offset[0, 1].astype(jnp.float32)
    taps = lanczos_taps(whole, fraction[0, 1])
    place_of = lax.broadcasted_iota(jnp.int32, (SIDE, SIDE), 0) - lax.broadcasted_iota(jnp.int32, (SIDE, SIDE), 1)
    above, middle, below = [
        lanczos_band((place_of - shift).astype(jnp.float32), whole, taps) for shift in (SIDE, 0, -SIDE)
    ]
    nothing = jnp.zeros_like(middle)
    for down, pieces in enumerate(((above, nothing), (middle, above), (below, middle), (nothing, below))):
        for col, piece in enumerate(pieces):
            wide_band[down * SIDE : (down + 1) * SIDE, col * SIDE : (col + 1) * SIDE] = piece
    gap = (
        lax.broadcasted_iota(jnp.int32, (rows, rows), 1) - lax.broadcasted_iota(jnp.int32, (rows, rows), 0)
    ).astype(jnp.float32)
    whole = offset[0, 0].astype(jnp.float32)
    row_warp = lanczos_band(gap, whole, lanczos_taps(whole, fraction[0, 0]))

    heavy = weight[...].astype(jnp.float32)
    lane = lax.broadcasted_iota(jnp.int32, (8, BW), 1)
    numbers = jnp.zeros((8, BW), jnp.float32)
    share = jnp.zeros((8, BW), jnp.float32)
    for k in range(bases):
        numbers = jnp.where(lane == k, index[0, k].astype(jnp.float32), numbers)
        share = jnp.where(lane == k, coef[0, k], share)
    for i in range(1, 4):
        piece = share.astype(jnp.bfloat16).astype(jnp.float32)
        share = share - piece
        numbers = numbers + turned(piece, i * bases)
    numbers = jnp.where(lane == 4 * bases, heavy, numbers)

    copies[-1].wait()
    mean = jnp.sum(jnp.sum(picture[...].astype(jnp.float32), axis=0, keepdims=True), axis=1, keepdims=True)
    mean = (mean * (1.0 / (rows * width))).astype(jnp.bfloat16).astype(jnp.float32)
    numbers = jnp.where(lane == 4 * bases + 1, mean, numbers)[0:1]
    row = lax.broadcasted_iota(jnp.int32, (BH, BW), 0) - me % QUAD
    tags = jnp.zeros((BH, BW), jnp.float32)
    for i, line in enumerate((owner[...].astype(jnp.float32), slot[...].astype(jnp.float32), numbers)):
        tags = jnp.where(row == i * QUAD, line, tags)
    tags = tags.astype(jnp.bfloat16)
    passes = [
        jnp.dot(
            picture[:, low:high], wide_band[top:bottom, :], preferred_element_type=jnp.float32
        ).astype(jnp.bfloat16)
        for low, high, top, bottom in windows(width)
    ]
    turn_in.wait()
    across = WIDE // BW
    for block, col_pass in enumerate(passes):
        done = jnp.dot(row_warp, col_pass, preferred_element_type=jnp.float32).astype(jnp.bfloat16)
        scaled = (done.astype(jnp.float32) - mean) * heavy
        for down in range(rows // BH):
            for col in range(across):
                box = down * (width // BW) + block * across + col
                piece = pl.ds(pl.multiple_of(starts[0, box], BH), BH)
                total[piece, :] += scaled[down * BH : (down + 1) * BH, col * BW : (col + 1) * BW]

    @pl.loop(0, peers // 2)
    def _(i):
        start = pl.multiple_of(i * chunk, PS)
        for out, base in ((keep, 0), (send, peers // 2 * BOXES)):
            source = pl.multiple_of(base + i * BOXES, BOXES)
            out[pl.ds(start, BOXES), :] = total[pl.ds(source, BOXES), :].astype(jnp.bfloat16)
            out[pl.ds(start + BOXES, chunk - BOXES), :] = tags


def add_kernel(parts, ours, theirs, *outs):
    length = ours.shape[0] // parts
    for i, out in enumerate(outs):
        here = pl.ds(i * length, length)
        out[...] = (ours[here, :].astype(jnp.float32) + theirs[here, :].astype(jnp.float32)).astype(jnp.bfloat16)


def add_parts(ours, theirs, parts):
    length = ours.shape[0] // parts
    return pl.pallas_call(
        functools.partial(add_kernel, parts),
        out_shape=[jax.ShapeDtypeStruct((length, BW), jnp.bfloat16)] * parts,
        in_specs=[VMEM, VMEM],
        out_specs=[VMEM] * parts,
        compiler_params=params(),
        name="add_parts",
    )(ours, theirs)


def swap(x, axis_size, bit):
    return lax.ppermute(x, "visit", [(i, i ^ bit) for i in range(axis_size)])


def scatter_sum(keep, send, peers):
    near = swap(send, peers, 1)
    ours, theirs = add_parts(keep, near, 2)
    near = swap(theirs, peers, 2)
    terms = add_parts(ours, near, peers // 4)
    return [terms[0]] + [swap(terms[far], peers, 4 * far) for far in reversed(range(1, peers // 4))]


def join_kernel(*refs):
    *parts, out = refs
    length = parts[0].shape[0]
    for i, part in enumerate(parts):
        out[i * length : (i + 1) * length, :] = part[...]


def join(*parts):
    rows, lanes = parts[0].shape
    return pl.pallas_call(
        join_kernel,
        out_shape=jax.ShapeDtypeStruct((rows * len(parts), lanes), parts[0].dtype),
        in_specs=[VMEM] * len(parts),
        out_specs=VMEM,
        compiler_params=params(),
        name="join",
    )(*parts)


def gather_slots(own, peers):
    line = join(own, *[swap(own, peers, 4 * away) for away in range(1, peers // 4)])
    pair = join(line, swap(line, peers, 2))
    return pair, swap(pair, peers, 1)


def summed_terms(terms, here):
    total = terms[0][here, :].astype(jnp.float32)
    for term in terms[1:]:
        total = total + term[here, :].astype(jnp.float32)
    return total


def read_tags(terms):
    tiles = [term[BOXES:, :].astype(jnp.float32) for term in terms]
    owner, slot, numbers = [
        jnp.concatenate([tile[i * QUAD : (i + 1) * QUAD, :] for tile in tiles], axis=0) for i in range(3)
    ]
    return owner.astype(jnp.int32), slot.astype(jnp.int32), numbers


def template_kernel(peers, bases, me_ref, *refs):
    *terms, leaning, coadd, weight_sum = refs
    me = me_ref[0]
    owner, slot, numbers = read_tags(terms)
    heavy = numbers[:, 4 * bases : 4 * bases + 1]
    level = heavy * numbers[:, 4 * bases + 1 : 4 * bases + 2]
    mine = owner == me
    weighed, levelled = [], []
    for i in range(PS):
        hit = mine & (slot == i)
        weighed.append(jnp.sum(jnp.where(hit, heavy, 0.0), axis=0, keepdims=True))
        levelled.append(jnp.sum(jnp.where(hit, level, 0.0), axis=0, keepdims=True))
    total = 1.0 + jnp.sum(jnp.concatenate(weighed, axis=0), axis=1, keepdims=True)
    over = jnp.sum(jnp.concatenate(levelled, axis=0), axis=1, keepdims=True)
    weight_sum[...] = jnp.broadcast_to(total, weight_sum.shape)
    for i in range(PS):
        here = slice(i * BH, (i + 1) * BH)
        mean = (summed_terms(terms, here) + over[i : i + 1, :]) / total[i : i + 1, :]
        rounded = mean.astype(jnp.bfloat16).astype(jnp.float32)
        leaning[here, :] = turned(rounded, LEAN).astype(jnp.bfloat16)
        coadd[here, :] = mean


AROUND = [(down, across) for down in (-1, 0, 1) for across in (-1, 0, 1)]


def plan_kernel(peers, bases, most, rows_of_boxes, me_ref, *refs):
    *terms, spots, scales = refs
    me = me_ref[0]
    owner, slot, numbers = read_tags(terms)
    nothing = peers * PS
    tile = place(owner, me, peers) * PS + slot
    boxes = owner.shape[1]
    cols = boxes // rows_of_boxes
    box = lax.broadcasted_iota(jnp.int32, (peers, BW), 1)
    lane = lax.broadcasted_iota(jnp.int32, (peers, BW), 1)
    mine = owner == me
    before = (
        lax.broadcasted_iota(jnp.int32, (boxes, boxes), 0) < lax.broadcasted_iota(jnp.int32, (boxes, boxes), 1)
    )
    rank = jnp.dot(
        jnp.where(mine, 1.0, 0.0).astype(jnp.bfloat16),
        jnp.where(before, 1.0, 0.0).astype(jnp.bfloat16),
        preferred_element_type=jnp.float32,
    ).astype(jnp.int32)
    tables = []
    for down, across in AROUND:
        row, col = box // cols + down, box % cols + across
        inside = (row >= 0) & (row < rows_of_boxes) & (col >= 0) & (col < cols)
        moved = turned(tile, -(down * cols + across)) if (down, across) != (0, 0) else tile
        tables.append(jnp.where(inside, moved - nothing, 0).astype(jnp.float32))
    tables.append((slot - PS).astype(jnp.float32))
    first = jnp.zeros((peers, BW), jnp.float32)
    second = jnp.zeros((peers, BW), jnp.float32)
    for j in range(most):
        chosen = mine & (rank == j)
        for i, table in enumerate(tables):
            value = jnp.sum(jnp.where(chosen, table, 0.0), axis=1, keepdims=True)
            value = value + (nothing if i < 9 else PS)
            if i < 8:
                first = jnp.where(lane == i * most + j, value, first)
            else:
                second = jnp.where(lane == (i - 8) * most + j, value, second)
    index = turned(numbers, 2 * most)
    second = jnp.where((lane >= 2 * most) & (lane < 2 * most + bases), index, second)
    spots[0:peers, :] = (first * BH).astype(jnp.int32)
    spots[peers : 2 * peers, :] = (jnp.where(lane < 2 * most, second * BH, second)).astype(jnp.int32)
    coef = turned(numbers, -bases) + turned(numbers, -2 * bases) + turned(numbers, -3 * bases)
    heavy = numbers[:, 4 * bases : 4 * bases + 1]
    scales[...] = jnp.where(lane < bases, coef * heavy, 0.0)


def gauss_kernel(basis_width, across_bands, down_bands):
    tap = lax.broadcasted_iota(jnp.int32, (8, 128), 1).astype(jnp.float32) - band_reach
    shape = across_bands.shape[1:]
    across_gap = (
        lax.broadcasted_iota(jnp.int32, shape, 0) - lax.broadcasted_iota(jnp.int32, shape, 1) - LEAN
    ).astype(jnp.float32)
    shape = down_bands.shape[1:]
    out_row = lax.broadcasted_iota(jnp.int32, shape, 0)
    in_row = lax.broadcasted_iota(jnp.int32, shape, 1)
    inner = in_row % TALL
    down_gap = jnp.where(inner < BH + BH // 2, inner, inner - TALL) - out_row % BH
    down_gap = jnp.where(out_row // BH == in_row // TALL, down_gap, 1024).astype(jnp.float32)
    for member in range(across_bands.shape[0]):
        blur_width = basis_width[member]
        spread = 2.0 * blur_width * blur_width
        total = jnp.sum(jnp.where(tap <= band_reach, jnp.exp(-tap * tap / spread), 0.0), axis=1, keepdims=True)[0:1]
        for gap, out in ((across_gap, across_bands), (down_gap, down_bands)):
            value = jnp.where(jnp.abs(gap) <= band_reach, jnp.exp(-gap * gap / spread), 0.0)
            out[member] = (value / total).astype(jnp.bfloat16)


def match_kernel(
    peers,
    bases,
    most,
    steps,
    near,
    other,
    across_bands,
    down_bands,
    coadd,
    weight_sum,
    spots,
    scales,
    template,
    out,
    table,
    window,
    blurred,
    matched,
):
    groups = pl.cdiv(most, GROUP)
    high = GROUP * TALL
    half = near.shape[0]
    table[0:half, :] = near[...]
    table[half : 2 * half, :] = other[...]
    table[2 * half :, :] = jnp.zeros((BH, BW), jnp.bfloat16)
    matched[...] = jnp.zeros_like(matched)
    template[...] = coadd[...].astype(jnp.bfloat16)
    if most % GROUP:
        window[...] = jnp.zeros_like(window)
    lane = lax.broadcasted_iota(jnp.int32, (BH, BW), 1)
    row = lax.broadcasted_iota(jnp.int32, (BH, BW), 0)
    left = lane < LEAN
    upper = row < BH // 2

    @pl.loop(0, peers // steps)
    def _(turn):
        for step in range(steps):
            visit = turn * steps + step
            for j in range(most):

                def tile(i):
                    at = spots[visit, i * most + j] if i < 8 else spots[peers + visit, j]
                    return table[pl.ds(pl.multiple_of(at, BH), BH), :]

                tiles = [tile(i) for i in range(9)]
                mixed = [jnp.where(upper, tiles[6 + i], tiles[i]) for i in range(3)]
                start = (step * groups * GROUP + j) * TALL
                for base, (west, middle, east) in ((0, tiles[3:6]), (BH, mixed)):
                    window[start + base : start + base + BH, 0:BW] = jnp.where(left, west, middle)
                    window[start + base : start + base + BH, BW:] = jnp.where(left, middle, east)
        for step in range(steps):
            visit = turn * steps + step
            here = slice(step * groups * high, (step + 1) * groups * high)
            for member in range(0, bases, 2):
                pair = range(member, min(member + 2, bases))
                band = [across_bands[spots[peers + visit, 2 * most + k]] for k in pair]
                band = jnp.concatenate(band, axis=1) if len(band) > 1 else band[0]
                blurred[here, member * BW : member * BW + band.shape[1]] = jnp.dot(
                    window[here, :], band, preferred_element_type=jnp.float32
                ).astype(jnp.bfloat16)
        for step in range(steps):
            visit = turn * steps + step
            parts = [slice((step * groups + i) * high, (step * groups + i + 1) * high) for i in range(groups)]
            total = jnp.zeros((GROUP * BH, groups * BW), jnp.float32)
            for k in range(bases):
                side = [blurred[here, k * BW : (k + 1) * BW] for here in parts]
                side = jnp.concatenate(side, axis=1) if groups > 1 else side[0]
                total = total + scales[visit, k] * jnp.dot(
                    down_bands[spots[peers + visit, 2 * most + k]], side, preferred_element_type=jnp.float32
                )
            for j in range(most):
                group, i = divmod(j, GROUP)
                at = spots[peers + visit, most + j]
                matched[pl.ds(pl.multiple_of(at, BH), BH), :] += total[
                    i * BH : (i + 1) * BH, group * BW : (group + 1) * BW
                ]

    for i in range(PS):
        here = slice(i * BH, (i + 1) * BH)
        out[here, :] = coadd[here, :] - matched[here, :] / weight_sum[i : i + 1, :]


def shards(
    visit_image,
    band_offset,
    shift_frac,
    weights,
    box_owner,
    box_slot,
    basis_index,
    basis_coef,
    basis_width,
):
    peers = lax.axis_size("visit")
    rows, width = visit_image.shape[1:]
    bases = basis_index.shape[1]
    table_size = basis_width.shape[0]
    most = max(2, 2 * box_slot.shape[1] // peers)
    me = lax.axis_index("visit").astype(jnp.int32).reshape(1)
    chunk = CHUNK
    owner = box_owner.reshape(1, -1)

    half = jax.ShapeDtypeStruct((peers // 2 * chunk, BW), jnp.bfloat16)
    keep, send = pl.pallas_call(
        functools.partial(warp_kernel, peers, bases),
        out_shape=[half, half],
        in_specs=[SMEM] + [ANY] * 8,
        out_specs=[VMEM] * 2,
        scratch_shapes=[
            pltpu.VMEM((rows, width), jnp.bfloat16),
            pltpu.VMEM(owner.shape, jnp.int32),
            pltpu.VMEM(box_slot.shape, jnp.int32),
            pltpu.SMEM(band_offset.shape, jnp.int32),
            pltpu.SMEM(shift_frac.shape, jnp.float32),
            pltpu.VMEM((1, 1), jnp.bfloat16),
            pltpu.SMEM(basis_index.shape, jnp.int32),
            pltpu.SMEM(basis_coef.shape, jnp.float32),
            pltpu.VMEM((peers * BOXES, BW), jnp.float32),
            pltpu.VMEM((WIDE + 2 * SIDE, WIDE), jnp.bfloat16),
            pltpu.VMEM((1, BW), jnp.int32),
            pltpu.SMEM((1, BW), jnp.int32),
            pltpu.SemaphoreType.DMA((9,)),
        ],
        compiler_params=pltpu.CompilerParams(vmem_limit_bytes=48 * 1024 * 1024),
        name="warp",
    )(
        me,
        visit_image[0],
        owner,
        box_slot,
        band_offset,
        shift_frac,
        weights.reshape(1, 1),
        basis_index,
        basis_coef,
    )

    across_bands, down_bands = pl.pallas_call(
        gauss_kernel,
        out_shape=[
            jax.ShapeDtypeStruct((table_size, BW + 2 * LEAN, BW), jnp.bfloat16),
            jax.ShapeDtypeStruct((table_size, GROUP * BH, GROUP * TALL), jnp.bfloat16),
        ],
        in_specs=[SMEM],
        out_specs=[VMEM] * 2,
        compiler_params=params(),
        name="gauss_bands",
    )(basis_width)

    terms = scatter_sum(keep, send, peers)
    leaning, coadd, weight_sum = pl.pallas_call(
        functools.partial(template_kernel, peers, bases),
        out_shape=[
            jax.ShapeDtypeStruct((BOXES, BW), jnp.bfloat16),
            jax.ShapeDtypeStruct((BOXES, BW), jnp.float32),
            jax.ShapeDtypeStruct((PS, BW), jnp.float32),
        ],
        in_specs=[SMEM] + [VMEM] * len(terms),
        out_specs=[VMEM] * 3,
        compiler_params=params(),
        name="template",
    )(me, *terms)
    near, other = gather_slots(leaning, peers)
    spots, scales = pl.pallas_call(
        functools.partial(plan_kernel, peers, bases, most, rows // BH),
        out_shape=[
            jax.ShapeDtypeStruct((2 * peers, BW), jnp.int32),
            jax.ShapeDtypeStruct((peers, BW), jnp.float32),
        ],
        in_specs=[SMEM] + [VMEM] * len(terms),
        out_specs=[VMEM] * 2,
        compiler_params=params(),
        name="plan",
    )(me, *terms)

    steps = min(peers, 16)
    tall = steps * pl.cdiv(most, GROUP) * GROUP * TALL
    template, difference_coadd = pl.pallas_call(
        functools.partial(match_kernel, peers, bases, most, steps),
        out_shape=[
            jax.ShapeDtypeStruct((BOXES, BW), jnp.bfloat16),
            jax.ShapeDtypeStruct((BOXES, BW), jnp.float32),
        ],
        in_specs=[VMEM] * 6 + [SMEM] * 2,
        out_specs=[VMEM] * 2,
        scratch_shapes=[
            pltpu.VMEM(((peers * PS + 1) * BH, BW), jnp.bfloat16),
            pltpu.VMEM((tall, BW + 2 * LEAN), jnp.bfloat16),
            pltpu.VMEM((tall, bases * BW), jnp.bfloat16),
            pltpu.VMEM(((PS + 1) * BH, BW), jnp.float32),
        ],
        compiler_params=params(),
        name="match",
    )(near, other, across_bands, down_bands, coadd, weight_sum, spots, scales)
    return (template.reshape(PS, BH, BW), difference_coadd.reshape(PS, BH, BW))


def solution(mesh):
    placed = (
        P(("groups", "visit"), None, None),
        P(("groups", "visit"), None),
        P(("groups", "visit"), None),
        P(("groups", "visit")),
        P(("groups", "visit"), None, None),
        P(("groups", "visit"), None),
        P(("groups", "visit"), None),
        P(("groups", "visit"), None),
        P(),
    )
    return jax.shard_map(
        shards,
        mesh=mesh,
        in_specs=placed,
        out_specs=(P(("groups", "visit"), None, None), P(("groups", "visit"), None, None)),
        check_vma=False,
    )
```

```python
import functools

import jax
import jax.numpy as jnp
from jax import lax
from jax.experimental import pallas as pl
from jax.experimental.pallas import tpu as pltpu
from jax.sharding import PartitionSpec as P

BH = 16
BW = 128
PS = 16
BOXES = PS * BH
SIDE = 128
WIDE = 256
LEAN = 64
TALL = 2 * BH
GROUP = 8

band_reach = 8.0

VMEM = pl.BlockSpec(memory_space=pltpu.VMEM)
SMEM = pl.BlockSpec(memory_space=pltpu.SMEM)
ANY = pl.BlockSpec(memory_space=pl.ANY)


def params():
    return pltpu.CompilerParams(vmem_limit_bytes=48 * 1024 * 1024)


def place(owner, me, peers):
    away = jnp.bitwise_xor(owner, me)
    return (away & 1) * (peers // 2) + ((away >> 1) & 1) * (peers // 4) + (away >> 2)


QUAD = 4
CHUNK = BOXES + BH


def windows(width):
    found = []
    for first in range(0, width, WIDE):
        low, high = max(first - SIDE, 0), min(first + WIDE + SIDE, width)
        found.append((low, high, low - first + SIDE, high - first + SIDE))
    return found


def turned(x, by):
    return pltpu.roll(x, by % BW, 1)


def lanczos_taps(whole, part):
    lane = lax.broadcasted_iota(jnp.int32, (8, BW), 1).astype(jnp.float32)
    x = (whole + lane - 2.0) - (whole + part)

    def sinc(v):
        angle = jnp.pi * v
        return jnp.where(v == 0.0, 1.0, jnp.sin(angle) / jnp.where(v == 0.0, 1.0, angle))

    return jnp.where(jnp.abs(x) < 3.0, sinc(x) * sinc(x / 3.0), 0.0)


def lanczos_band(gap, whole, taps):
    band = jnp.zeros(gap.shape, jnp.float32)
    for tap in range(7):
        band = jnp.where(gap == whole + (tap - 2), taps[0:1, tap : tap + 1], band)
    return band.astype(jnp.bfloat16)


def warp_kernel(
    peers,
    bases,
    me_ref,
    picture_in,
    owner_in,
    slot_in,
    offset_in,
    fraction_in,
    weight_in,
    index_in,
    coef_in,
    keep_near,
    keep_far,
    send_near,
    send_far,
    picture,
    owner,
    slot,
    offset,
    fraction,
    weight,
    index,
    coef,
    total,
    wide_band,
    spots,
    starts,
    sems,
):
    rows, width = picture.shape
    me = me_ref[0]
    chunk = CHUNK
    sources = (owner_in, slot_in, offset_in, fraction_in, weight_in, index_in, coef_in, picture_in)
    targets = (owner, slot, offset, fraction, weight, index, coef, picture)
    copies = [pltpu.make_async_copy(x, y, sems.at[i]) for i, (x, y) in enumerate(zip(sources, targets))]
    for copy in copies:
        copy.start()
    total[...] = jnp.zeros_like(total)
    for copy in copies[:-1]:
        copy.wait()
    spots[...] = (place(owner[...], me, peers) * PS + slot[...]) * BH
    turn_in = pltpu.make_async_copy(spots, starts, sems.at[len(copies)])
    turn_in.start()

    whole = offset[0, 1].astype(jnp.float32)
    taps = lanczos_taps(whole, fraction[0, 1])
    place_of = lax.broadcasted_iota(jnp.int32, (SIDE, SIDE), 0) - lax.broadcasted_iota(jnp.int32, (SIDE, SIDE), 1)
    above, middle, below = [
        lanczos_band((place_of - shift).astype(jnp.float32), whole, taps) for shift in (SIDE, 0, -SIDE)
    ]
    nothing = jnp.zeros_like(middle)
    for down, pieces in enumerate(((above, nothing), (middle, above), (below, middle), (nothing, below))):
        for col, piece in enumerate(pieces):
            wide_band[down * SIDE : (down + 1) * SIDE, col * SIDE : (col + 1) * SIDE] = piece
    gap = (
        lax.broadcasted_iota(jnp.int32, (rows, rows), 1) - lax.broadcasted_iota(jnp.int32, (rows, rows), 0)
    ).astype(jnp.float32)
    whole = offset[0, 0].astype(jnp.float32)
    row_warp = lanczos_band(gap, whole, lanczos_taps(whole, fraction[0, 0]))

    heavy = weight[...].astype(jnp.float32)
    lane = lax.broadcasted_iota(jnp.int32, (8, BW), 1)
    numbers = jnp.zeros((8, BW), jnp.float32)
    share = jnp.zeros((8, BW), jnp.float32)
    for k in range(bases):
        numbers = jnp.where(lane == k, index[0, k].astype(jnp.float32), numbers)
        share = jnp.where(lane == k, coef[0, k], share)
    for i in range(1, 4):
        piece = share.astype(jnp.bfloat16).astype(jnp.float32)
        share = share - piece
        numbers = numbers + turned(piece, i * bases)
    numbers = jnp.where(lane == 4 * bases, heavy, numbers)

    copies[-1].wait()
    mean = jnp.sum(jnp.sum(picture[...].astype(jnp.float32), axis=0, keepdims=True), axis=1, keepdims=True)
    mean = (mean * (1.0 / (rows * width))).astype(jnp.bfloat16).astype(jnp.float32)
    numbers = jnp.where(lane == 4 * bases + 1, mean, numbers)[0:1]
    row = lax.broadcasted_iota(jnp.int32, (BH, BW), 0) - me % QUAD
    tags = jnp.zeros((BH, BW), jnp.float32)
    for i, line in enumerate((owner[...].astype(jnp.float32), slot[...].astype(jnp.float32), numbers)):
        tags = jnp.where(row == i * QUAD, line, tags)
    tags = tags.astype(jnp.bfloat16)
    passes = [
        jnp.dot(
            picture[:, low:high], wide_band[top:bottom, :], preferred_element_type=jnp.float32
        ).astype(jnp.bfloat16)
        for low, high, top, bottom in windows(width)
    ]
    turn_in.wait()
    across = WIDE // BW
    for block, col_pass in enumerate(passes):
        done = jnp.dot(row_warp, col_pass, preferred_element_type=jnp.float32).astype(jnp.bfloat16)
        scaled = (done.astype(jnp.float32) - mean) * heavy
        for down in range(rows // BH):
            for col in range(across):
                box = down * (width // BW) + block * across + col
                piece = pl.ds(pl.multiple_of(starts[0, box], BH), BH)
                total[piece, :] += scaled[down * BH : (down + 1) * BH, col * BW : (col + 1) * BW]

    @pl.loop(0, peers // 4)
    def _(i):
        start = pl.multiple_of(i * chunk, PS)
        for quarter, out in enumerate((keep_near, keep_far, send_near, send_far)):
            source = pl.multiple_of((quarter * (peers // 4) + i) * BOXES, BOXES)
            out[pl.ds(start, BOXES), :] = total[pl.ds(source, BOXES), :].astype(jnp.bfloat16)
            out[pl.ds(start + BOXES, chunk - BOXES), :] = tags


def add_kernel(count, *refs):
    parts, outs = refs[:count], refs[count:]
    length = outs[0].shape[0]
    for i, out in enumerate(outs):
        out[...] = summed_terms(parts, slice(i * length, (i + 1) * length)).astype(jnp.bfloat16)


def add_parts(pieces, *parts):
    length = parts[0].shape[0] // pieces
    return pl.pallas_call(
        functools.partial(add_kernel, len(parts)),
        out_shape=[jax.ShapeDtypeStruct((length, BW), jnp.bfloat16)] * pieces,
        in_specs=[VMEM] * len(parts),
        out_specs=[VMEM] * pieces,
        compiler_params=params(),
        name="add_parts",
    )(*parts)


def swap(x, axis_size, bit):
    return lax.ppermute(x, "visit", [(i, i ^ bit) for i in range(axis_size)])


def scatter_sum(keep_near, keep_far, send_near, send_far, peers):
    (beyond,) = add_parts(1, keep_far, swap(send_far, peers, 1))
    terms = add_parts(peers // 4, keep_near, swap(send_near, peers, 1), swap(beyond, peers, 2))
    return [terms[0]] + [swap(terms[far], peers, 4 * far) for far in reversed(range(1, peers // 4))]


def join_kernel(count, *refs):
    parts, out = refs[:count], refs[-1]
    length = parts[0].shape[0]
    for i, part in enumerate(parts):
        out[i * length : (i + 1) * length, :] = part[...]


def join(*parts, before=()):
    rows, lanes = parts[0].shape
    return pl.pallas_call(
        functools.partial(join_kernel, len(parts)),
        out_shape=jax.ShapeDtypeStruct((rows * len(parts), lanes), parts[0].dtype),
        in_specs=[VMEM] * len(parts) + [ANY] * len(before),
        out_specs=VMEM,
        compiler_params=params(),
        name="join",
    )(*parts, *before)


def gather_slots(own, peers, before):
    line = join(*[own] + [swap(own, peers, 4 * away) for away in range(1, peers // 4)], before=before)
    side = swap(line, peers, 2)
    return line, side, swap(line, peers, 1), swap(side, peers, 1)


def summed_terms(terms, here):
    total = terms[0][here, :].astype(jnp.float32)
    for term in terms[1:]:
        total = total + term[here, :].astype(jnp.float32)
    return total


def read_tags(terms):
    tiles = [term[BOXES:, :].astype(jnp.float32) for term in terms]
    owner, slot, numbers = [
        jnp.concatenate([tile[i * QUAD : (i + 1) * QUAD, :] for tile in tiles], axis=0) for i in range(3)
    ]
    return owner.astype(jnp.int32), slot.astype(jnp.int32), numbers


def template_kernel(peers, bases, me_ref, *refs):
    *terms, leaning, coadd, weight_sum = refs
    me = me_ref[0]
    owner, slot, numbers = read_tags(terms)
    heavy = numbers[:, 4 * bases : 4 * bases + 1]
    level = heavy * numbers[:, 4 * bases + 1 : 4 * bases + 2]
    mine = owner == me
    weighed, levelled = [], []
    for i in range(PS):
        hit = mine & (slot == i)
        weighed.append(jnp.sum(jnp.where(hit, heavy, 0.0), axis=0, keepdims=True))
        levelled.append(jnp.sum(jnp.where(hit, level, 0.0), axis=0, keepdims=True))
    total = 1.0 + jnp.sum(jnp.concatenate(weighed, axis=0), axis=1, keepdims=True)
    over = jnp.sum(jnp.concatenate(levelled, axis=0), axis=1, keepdims=True)
    weight_sum[...] = jnp.broadcast_to(total, weight_sum.shape)
    for i in range(PS):
        here = slice(i * BH, (i + 1) * BH)
        mean = (summed_terms(terms, here) + over[i : i + 1, :]) / total[i : i + 1, :]
        rounded = mean.astype(jnp.bfloat16).astype(jnp.float32)
        leaning[here, :] = turned(rounded, LEAN).astype(jnp.bfloat16)
        coadd[here, :] = mean


AROUND = [(down, across) for down in (-1, 0, 1) for across in (-1, 0, 1)]


def plan_kernel(peers, bases, most, rows_of_boxes, me_ref, *refs):
    *terms, spots, scales = refs
    me = me_ref[0]
    owner, slot, numbers = read_tags(terms)
    nothing = peers * PS
    tile = place(owner, me, peers) * PS + slot
    boxes = owner.shape[1]
    cols = boxes // rows_of_boxes
    box = lax.broadcasted_iota(jnp.int32, (peers, BW), 1)
    lane = lax.broadcasted_iota(jnp.int32, (peers, BW), 1)
    mine = owner == me
    before = (
        lax.broadcasted_iota(jnp.int32, (boxes, boxes), 0) < lax.broadcasted_iota(jnp.int32, (boxes, boxes), 1)
    )
    rank = jnp.dot(
        jnp.where(mine, 1.0, 0.0).astype(jnp.bfloat16),
        jnp.where(before, 1.0, 0.0).astype(jnp.bfloat16),
        preferred_element_type=jnp.float32,
    ).astype(jnp.int32)
    tables = []
    for down, across in AROUND:
        row, col = box // cols + down, box % cols + across
        inside = (row >= 0) & (row < rows_of_boxes) & (col >= 0) & (col < cols)
        moved = turned(tile, -(down * cols + across)) if (down, across) != (0, 0) else tile
        tables.append(jnp.where(inside, moved - nothing, 0).astype(jnp.float32))
    tables.append((slot - PS).astype(jnp.float32))
    first = jnp.zeros((peers, BW), jnp.float32)
    second = jnp.zeros((peers, BW), jnp.float32)
    for j in range(most):
        chosen = mine & (rank == j)
        for i, table in enumerate(tables):
            value = jnp.sum(jnp.where(chosen, table, 0.0), axis=1, keepdims=True)
            value = value + (nothing if i < 9 else PS)
            if i < 8:
                first = jnp.where(lane == i * most + j, value, first)
            else:
                second = jnp.where(lane == (i - 8) * most + j, value, second)
    index = turned(numbers, 2 * most)
    second = jnp.where((lane >= 2 * most) & (lane < 2 * most + bases), index, second)
    spots[0:peers, :] = (first * BH).astype(jnp.int32)
    spots[peers : 2 * peers, :] = (jnp.where(lane < 2 * most, second * BH, second)).astype(jnp.int32)
    coef = turned(numbers, -bases) + turned(numbers, -2 * bases) + turned(numbers, -3 * bases)
    heavy = numbers[:, 4 * bases : 4 * bases + 1]
    scales[...] = jnp.where(lane < bases, coef * heavy, 0.0)


def gauss_kernel(basis_width, across_bands, down_bands):
    tap = lax.broadcasted_iota(jnp.int32, (8, 128), 1).astype(jnp.float32) - band_reach
    shape = across_bands.shape[1:]
    across_gap = (
        lax.broadcasted_iota(jnp.int32, shape, 0) - lax.broadcasted_iota(jnp.int32, shape, 1) - LEAN
    ).astype(jnp.float32)
    shape = down_bands.shape[1:]
    out_row = lax.broadcasted_iota(jnp.int32, shape, 0)
    in_row = lax.broadcasted_iota(jnp.int32, shape, 1)
    inner = in_row % TALL
    down_gap = jnp.where(inner < BH + BH // 2, inner, inner - TALL) - out_row % BH
    down_gap = jnp.where(out_row // BH == in_row // TALL, down_gap, 1024).astype(jnp.float32)
    for member in range(across_bands.shape[0]):
        blur_width = basis_width[member]
        spread = 2.0 * blur_width * blur_width
        total = jnp.sum(jnp.where(tap <= band_reach, jnp.exp(-tap * tap / spread), 0.0), axis=1, keepdims=True)[0:1]
        for gap, out in ((across_gap, across_bands), (down_gap, down_bands)):
            value = jnp.where(jnp.abs(gap) <= band_reach, jnp.exp(-gap * gap / spread), 0.0)
            out[member] = (value / total).astype(jnp.bfloat16)


def match_kernel(
    peers,
    bases,
    most,
    steps,
    across_bands,
    down_bands,
    coadd,
    weight_sum,
    spots,
    scales,
    *refs,
):
    pieces, (template, out, table, window, blurred, matched) = refs[:4], refs[4:]
    groups = pl.cdiv(most, GROUP)
    high = GROUP * TALL
    length = pieces[0].shape[0]
    for i, piece in enumerate(pieces):
        table[i * length : (i + 1) * length, :] = piece[...]
    table[4 * length :, :] = jnp.zeros((BH, BW), jnp.bfloat16)
    matched[...] = jnp.zeros_like(matched)
    template[...] = coadd[...].astype(jnp.bfloat16)
    if most % GROUP:
        window[...] = jnp.zeros_like(window)
    lane = lax.broadcasted_iota(jnp.int32, (BH, BW), 1)
    row = lax.broadcasted_iota(jnp.int32, (BH, BW), 0)
    left = lane < LEAN
    upper = row < BH // 2

    @pl.loop(0, peers // steps)
    def _(turn):
        for step in range(steps):
            visit = turn * steps + step
            for j in range(most):

                def tile(i):
                    at = spots[visit, i * most + j] if i < 8 else spots[peers + visit, j]
                    return table[pl.ds(pl.multiple_of(at, BH), BH), :]

                tiles = [tile(i) for i in range(9)]
                mixed = [jnp.where(upper, tiles[6 + i], tiles[i]) for i in range(3)]
                start = (step * groups * GROUP + j) * TALL
                for base, (west, middle, east) in ((0, tiles[3:6]), (BH, mixed)):
                    window[start + base : start + base + BH, 0:BW] = jnp.where(left, west, middle)
                    window[start + base : start + base + BH, BW:] = jnp.where(left, middle, east)
        for step in range(steps):
            visit = turn * steps + step
            here = slice(step * groups * high, (step + 1) * groups * high)
            for member in range(0, bases, 2):
                pair = range(member, min(member + 2, bases))
                band = [across_bands[spots[peers + visit, 2 * most + k]] for k in pair]
                band = jnp.concatenate(band, axis=1) if len(band) > 1 else band[0]
                blurred[here, member * BW : member * BW + band.shape[1]] = jnp.dot(
                    window[here, :], band, preferred_element_type=jnp.float32
                ).astype(jnp.bfloat16)
        for step in range(steps):
            visit = turn * steps + step
            parts = [slice((step * groups + i) * high, (step * groups + i + 1) * high) for i in range(groups)]
            total = jnp.zeros((GROUP * BH, groups * BW), jnp.float32)
            for k in range(bases):
                side = [blurred[here, k * BW : (k + 1) * BW] for here in parts]
                side = jnp.concatenate(side, axis=1) if groups > 1 else side[0]
                total = total + scales[visit, k] * jnp.dot(
                    down_bands[spots[peers + visit, 2 * most + k]], side, preferred_element_type=jnp.float32
                )
            for j in range(most):
                group, i = divmod(j, GROUP)
                at = spots[peers + visit, most + j]
                matched[pl.ds(pl.multiple_of(at, BH), BH), :] += total[
                    i * BH : (i + 1) * BH, group * BW : (group + 1) * BW
                ]

    for i in range(PS):
        here = slice(i * BH, (i + 1) * BH)
        out[here, :] = coadd[here, :] - matched[here, :] / weight_sum[i : i + 1, :]


def shards(
    visit_image,
    band_offset,
    shift_frac,
    weights,
    box_owner,
    box_slot,
    basis_index,
    basis_coef,
    basis_width,
):
    peers = lax.axis_size("visit")
    rows, width = visit_image.shape[1:]
    bases = basis_index.shape[1]
    table_size = basis_width.shape[0]
    most = max(2, 2 * box_slot.shape[1] // peers)
    me = lax.axis_index("visit").astype(jnp.int32).reshape(1)
    chunk = CHUNK
    owner = box_owner.reshape(1, -1)

    quarter = jax.ShapeDtypeStruct((peers // 4 * chunk, BW), jnp.bfloat16)
    sums = pl.pallas_call(
        functools.partial(warp_kernel, peers, bases),
        out_shape=[quarter] * 4,
        in_specs=[SMEM] + [ANY] * 8,
        out_specs=[VMEM] * 4,
        scratch_shapes=[
            pltpu.VMEM((rows, width), jnp.bfloat16),
            pltpu.VMEM(owner.shape, jnp.int32),
            pltpu.VMEM(box_slot.shape, jnp.int32),
            pltpu.SMEM(band_offset.shape, jnp.int32),
            pltpu.SMEM(shift_frac.shape, jnp.float32),
            pltpu.VMEM((1, 1), jnp.bfloat16),
            pltpu.SMEM(basis_index.shape, jnp.int32),
            pltpu.SMEM(basis_coef.shape, jnp.float32),
            pltpu.VMEM((peers * BOXES, BW), jnp.float32),
            pltpu.VMEM((WIDE + 2 * SIDE, WIDE), jnp.bfloat16),
            pltpu.VMEM((1, BW), jnp.int32),
            pltpu.SMEM((1, BW), jnp.int32),
            pltpu.SemaphoreType.DMA((9,)),
        ],
        compiler_params=pltpu.CompilerParams(vmem_limit_bytes=48 * 1024 * 1024),
        name="warp",
    )(
        me,
        visit_image[0],
        owner,
        box_slot,
        band_offset,
        shift_frac,
        weights.reshape(1, 1),
        basis_index,
        basis_coef,
    )

    across_bands, down_bands = pl.pallas_call(
        gauss_kernel,
        out_shape=[
            jax.ShapeDtypeStruct((table_size, BW + 2 * LEAN, BW), jnp.bfloat16),
            jax.ShapeDtypeStruct((table_size, GROUP * BH, GROUP * TALL), jnp.bfloat16),
        ],
        in_specs=[SMEM],
        out_specs=[VMEM] * 2,
        compiler_params=params(),
        name="gauss_bands",
    )(basis_width)

    terms = scatter_sum(*sums, peers)
    leaning, coadd, weight_sum = pl.pallas_call(
        functools.partial(template_kernel, peers, bases),
        out_shape=[
            jax.ShapeDtypeStruct((BOXES, BW), jnp.bfloat16),
            jax.ShapeDtypeStruct((BOXES, BW), jnp.float32),
            jax.ShapeDtypeStruct((PS, BW), jnp.float32),
        ],
        in_specs=[SMEM] + [VMEM] * len(terms),
        out_specs=[VMEM] * 3,
        compiler_params=params(),
        name="template",
    )(me, *terms)
    spots, scales = pl.pallas_call(
        functools.partial(plan_kernel, peers, bases, most, rows // BH),
        out_shape=[
            jax.ShapeDtypeStruct((2 * peers, BW), jnp.int32),
            jax.ShapeDtypeStruct((peers, BW), jnp.float32),
        ],
        in_specs=[SMEM] + [VMEM] * len(terms),
        out_specs=[VMEM] * 2,
        compiler_params=params(),
        name="plan",
    )(me, *terms)

    pieces = gather_slots(leaning, peers, (across_bands, spots))
    steps = min(peers, 16)
    tall = steps * pl.cdiv(most, GROUP) * GROUP * TALL
    template, difference_coadd = pl.pallas_call(
        functools.partial(match_kernel, peers, bases, most, steps),
        out_shape=[
            jax.ShapeDtypeStruct((BOXES, BW), jnp.bfloat16),
            jax.ShapeDtypeStruct((BOXES, BW), jnp.float32),
        ],
        in_specs=[VMEM] * 4 + [SMEM] * 2 + [VMEM] * 4,
        out_specs=[VMEM] * 2,
        scratch_shapes=[
            pltpu.VMEM(((peers * PS + 1) * BH, BW), jnp.bfloat16),
            pltpu.VMEM((tall, BW + 2 * LEAN), jnp.bfloat16),
            pltpu.VMEM((tall, bases * BW), jnp.bfloat16),
            pltpu.VMEM(((PS + 1) * BH, BW), jnp.float32),
        ],
        compiler_params=params(),
        name="match",
    )(across_bands, down_bands, coadd, weight_sum, spots, scales, *pieces)
    return (template.reshape(PS, BH, BW), difference_coadd.reshape(PS, BH, BW))


def solution(mesh):
    placed = (
        P(("groups", "visit"), None, None),
        P(("groups", "visit"), None),
        P(("groups", "visit"), None),
        P(("groups", "visit")),
        P(("groups", "visit"), None, None),
        P(("groups", "visit"), None),
        P(("groups", "visit"), None),
        P(("groups", "visit"), None),
        P(),
    )
    return jax.shard_map(
        shards,
        mesh=mesh,
        in_specs=placed,
        out_specs=(P(("groups", "visit"), None, None), P(("groups", "visit"), None, None)),
        check_vma=False,
    )
```

```python
import functools

import jax
import jax.numpy as jnp
from jax import lax
from jax.experimental import pallas as pl
from jax.experimental.pallas import tpu as pltpu
from jax.sharding import PartitionSpec as P

BH = 16
BW = 128
PS = 16
BOXES = PS * BH
SIDE = 128
WIDE = 256
LEAN = 64
TALL = 2 * BH
GROUP = 8

band_reach = 8.0

VMEM = pl.BlockSpec(memory_space=pltpu.VMEM)
SMEM = pl.BlockSpec(memory_space=pltpu.SMEM)
ANY = pl.BlockSpec(memory_space=pl.ANY)


def params():
    return pltpu.CompilerParams(vmem_limit_bytes=48 * 1024 * 1024)


def place(owner, me, peers):
    away = jnp.bitwise_xor(owner, me)
    return (away & 1) * (peers // 2) + ((away >> 1) & 1) * (peers // 4) + (away >> 2)


QUAD = 4
CHUNK = BOXES + BH


def windows(width):
    found = []
    for first in range(0, width, WIDE):
        low, high = max(first - SIDE, 0), min(first + WIDE + SIDE, width)
        found.append((low, high, low - first + SIDE, high - first + SIDE))
    return found


def turned(x, by):
    return pltpu.roll(x, by % BW, 1)


def lanczos_taps(whole, part):
    lane = lax.broadcasted_iota(jnp.int32, (8, BW), 1).astype(jnp.float32)
    x = (whole + lane - 2.0) - (whole + part)

    def sinc(v):
        angle = jnp.pi * v
        return jnp.where(v == 0.0, 1.0, jnp.sin(angle) / jnp.where(v == 0.0, 1.0, angle))

    return jnp.where(jnp.abs(x) < 3.0, sinc(x) * sinc(x / 3.0), 0.0)


def lanczos_band(gap, whole, taps):
    band = jnp.zeros(gap.shape, jnp.float32)
    for tap in range(7):
        band = jnp.where(gap == whole + (tap - 2), taps[0:1, tap : tap + 1], band)
    return band.astype(jnp.bfloat16)


def warp_kernel(
    peers,
    bases,
    me_ref,
    picture_in,
    owner_in,
    slot_in,
    offset_in,
    fraction_in,
    weight_in,
    index_in,
    coef_in,
    keep_near,
    keep_far,
    send_near,
    send_far,
    picture,
    owner,
    slot,
    offset,
    fraction,
    weight,
    index,
    coef,
    total,
    wide_band,
    spots,
    starts,
    sems,
):
    rows, width = picture.shape
    me = me_ref[0]
    chunk = CHUNK
    sources = (owner_in, slot_in, offset_in, fraction_in, weight_in, index_in, coef_in, picture_in)
    targets = (owner, slot, offset, fraction, weight, index, coef, picture)
    copies = [pltpu.make_async_copy(x, y, sems.at[i]) for i, (x, y) in enumerate(zip(sources, targets))]
    for copy in copies:
        copy.start()
    total[...] = jnp.zeros_like(total)
    for copy in copies[:-1]:
        copy.wait()
    spots[...] = (place(owner[...], me, peers) * PS + slot[...]) * BH
    turn_in = pltpu.make_async_copy(spots, starts, sems.at[len(copies)])
    turn_in.start()

    whole = offset[0, 1].astype(jnp.float32)
    taps = lanczos_taps(whole, fraction[0, 1])
    place_of = lax.broadcasted_iota(jnp.int32, (SIDE, SIDE), 0) - lax.broadcasted_iota(jnp.int32, (SIDE, SIDE), 1)
    above, middle, below = [
        lanczos_band((place_of - shift).astype(jnp.float32), whole, taps) for shift in (SIDE, 0, -SIDE)
    ]
    nothing = jnp.zeros_like(middle)
    for down, pieces in enumerate(((above, nothing), (middle, above), (below, middle), (nothing, below))):
        for col, piece in enumerate(pieces):
            wide_band[down * SIDE : (down + 1) * SIDE, col * SIDE : (col + 1) * SIDE] = piece
    gap = (
        lax.broadcasted_iota(jnp.int32, (rows, rows), 1) - lax.broadcasted_iota(jnp.int32, (rows, rows), 0)
    ).astype(jnp.float32)
    whole = offset[0, 0].astype(jnp.float32)
    row_warp = lanczos_band(gap, whole, lanczos_taps(whole, fraction[0, 0]))

    heavy = weight[...].astype(jnp.float32)
    lane = lax.broadcasted_iota(jnp.int32, (8, BW), 1)
    numbers = jnp.zeros((8, BW), jnp.float32)
    share = jnp.zeros((8, BW), jnp.float32)
    for k in range(bases):
        numbers = jnp.where(lane == k, index[0, k].astype(jnp.float32), numbers)
        share = jnp.where(lane == k, coef[0, k], share)
    for i in range(1, 4):
        piece = share.astype(jnp.bfloat16).astype(jnp.float32)
        share = share - piece
        numbers = numbers + turned(piece, i * bases)
    numbers = jnp.where(lane == 4 * bases, heavy, numbers)

    copies[-1].wait()
    mean = jnp.sum(jnp.sum(picture[...].astype(jnp.float32), axis=0, keepdims=True), axis=1, keepdims=True)
    mean = (mean * (1.0 / (rows * width))).astype(jnp.bfloat16).astype(jnp.float32)
    numbers = jnp.where(lane == 4 * bases + 1, mean, numbers)[0:1]
    row = lax.broadcasted_iota(jnp.int32, (BH, BW), 0) - me % QUAD
    tags = jnp.zeros((BH, BW), jnp.float32)
    for i, line in enumerate((owner[...].astype(jnp.float32), slot[...].astype(jnp.float32), numbers)):
        tags = jnp.where(row == i * QUAD, line, tags)
    tags = tags.astype(jnp.bfloat16)
    passes = [
        jnp.dot(
            picture[:, low:high], wide_band[top:bottom, :], preferred_element_type=jnp.float32
        ).astype(jnp.bfloat16)
        for low, high, top, bottom in windows(width)
    ]
    turn_in.wait()
    across = WIDE // BW
    for block, col_pass in enumerate(passes):
        done = jnp.dot(row_warp, col_pass, preferred_element_type=jnp.float32).astype(jnp.bfloat16)
        scaled = (done.astype(jnp.float32) - mean) * heavy
        for down in range(rows // BH):
            for col in range(across):
                box = down * (width // BW) + block * across + col
                piece = pl.ds(pl.multiple_of(starts[0, box], BH), BH)
                total[piece, :] += scaled[down * BH : (down + 1) * BH, col * BW : (col + 1) * BW]

    @pl.loop(0, peers // 4)
    def _(i):
        start = pl.multiple_of(i * chunk, PS)
        for quarter, out in enumerate((keep_near, keep_far, send_near, send_far)):
            source = pl.multiple_of((quarter * (peers // 4) + i) * BOXES, BOXES)
            out[pl.ds(start, BOXES), :] = total[pl.ds(source, BOXES), :].astype(jnp.bfloat16)
            out[pl.ds(start + BOXES, chunk - BOXES), :] = tags


def add_kernel(count, *refs):
    parts, outs = refs[:count], refs[count:]
    length = outs[0].shape[0]
    for i, out in enumerate(outs):
        out[...] = summed_terms(parts, slice(i * length, (i + 1) * length)).astype(jnp.bfloat16)


def add_parts(pieces, *parts):
    length = parts[0].shape[0] // pieces
    return pl.pallas_call(
        functools.partial(add_kernel, len(parts)),
        out_shape=[jax.ShapeDtypeStruct((length, BW), jnp.bfloat16)] * pieces,
        in_specs=[VMEM] * len(parts),
        out_specs=[VMEM] * pieces,
        compiler_params=params(),
        name="add_parts",
    )(*parts)


def swap(x, axis_size, bit):
    return lax.ppermute(x, "visit", [(i, i ^ bit) for i in range(axis_size)])


def scatter_sum(keep_near, keep_far, send_near, send_far, peers):
    (beyond,) = add_parts(1, keep_far, swap(send_far, peers, 1))
    terms = add_parts(peers // 4, keep_near, swap(send_near, peers, 1), swap(beyond, peers, 2))
    return [terms[0]] + [swap(terms[far], peers, 4 * far) for far in reversed(range(1, peers // 4))]


def join_kernel(count, *refs):
    parts, out = refs[:count], refs[-1]
    length = parts[0].shape[0]
    for i, part in enumerate(parts):
        out[i * length : (i + 1) * length, :] = part[...]


def join(*parts, before=()):
    rows, lanes = parts[0].shape
    return pl.pallas_call(
        functools.partial(join_kernel, len(parts)),
        out_shape=jax.ShapeDtypeStruct((rows * len(parts), lanes), parts[0].dtype),
        in_specs=[VMEM] * len(parts) + [ANY] * len(before),
        out_specs=VMEM,
        compiler_params=params(),
        name="join",
    )(*parts, *before)


def gather_slots(own, peers, before):
    count = peers // 8
    far = {away: swap(own, peers, 4 * away) for away in reversed(range(1, peers // 4))}
    high = join(*[far[away] for away in range(count, 2 * count)], before=before)
    high_side = swap(high, peers, 2)
    low = join(own, *[far[away] for away in range(1, count)])
    low_side = swap(low, peers, 2)
    line = join(low, high)
    side = join(low_side, high_side)
    return line, side, swap(line, peers, 1), swap(side, peers, 1)


def summed_terms(terms, here):
    total = terms[0][here, :].astype(jnp.float32)
    for term in terms[1:]:
        total = total + term[here, :].astype(jnp.float32)
    return total


def read_tags(terms):
    tiles = [term[BOXES:, :].astype(jnp.float32) for term in terms]
    owner, slot, numbers = [
        jnp.concatenate([tile[i * QUAD : (i + 1) * QUAD, :] for tile in tiles], axis=0) for i in range(3)
    ]
    return owner.astype(jnp.int32), slot.astype(jnp.int32), numbers


def template_kernel(peers, bases, me_ref, *refs):
    *terms, leaning, coadd, weight_sum = refs
    me = me_ref[0]
    owner, slot, numbers = read_tags(terms)
    heavy = numbers[:, 4 * bases : 4 * bases + 1]
    level = heavy * numbers[:, 4 * bases + 1 : 4 * bases + 2]
    mine = owner == me
    weighed, levelled = [], []
    for i in range(PS):
        hit = mine & (slot == i)
        weighed.append(jnp.sum(jnp.where(hit, heavy, 0.0), axis=0, keepdims=True))
        levelled.append(jnp.sum(jnp.where(hit, level, 0.0), axis=0, keepdims=True))
    total = 1.0 + jnp.sum(jnp.concatenate(weighed, axis=0), axis=1, keepdims=True)
    over = jnp.sum(jnp.concatenate(levelled, axis=0), axis=1, keepdims=True)
    weight_sum[...] = jnp.broadcast_to(total, weight_sum.shape)
    for i in range(PS):
        here = slice(i * BH, (i + 1) * BH)
        mean = (summed_terms(terms, here) + over[i : i + 1, :]) / total[i : i + 1, :]
        rounded = mean.astype(jnp.bfloat16).astype(jnp.float32)
        leaning[here, :] = turned(rounded, LEAN).astype(jnp.bfloat16)
        coadd[here, :] = mean


AROUND = [(down, across) for down in (-1, 0, 1) for across in (-1, 0, 1)]


def plan_kernel(peers, bases, most, rows_of_boxes, me_ref, *refs):
    *terms, spots, scales = refs
    me = me_ref[0]
    owner, slot, numbers = read_tags(terms)
    nothing = peers * PS
    tile = place(owner, me, peers) * PS + slot
    boxes = owner.shape[1]
    cols = boxes // rows_of_boxes
    box = lax.broadcasted_iota(jnp.int32, (peers, BW), 1)
    lane = lax.broadcasted_iota(jnp.int32, (peers, BW), 1)
    mine = owner == me
    before = (
        lax.broadcasted_iota(jnp.int32, (boxes, boxes), 0) < lax.broadcasted_iota(jnp.int32, (boxes, boxes), 1)
    )
    rank = jnp.dot(
        jnp.where(mine, 1.0, 0.0).astype(jnp.bfloat16),
        jnp.where(before, 1.0, 0.0).astype(jnp.bfloat16),
        preferred_element_type=jnp.float32,
    ).astype(jnp.int32)
    tables = []
    for down, across in AROUND:
        row, col = box // cols + down, box % cols + across
        inside = (row >= 0) & (row < rows_of_boxes) & (col >= 0) & (col < cols)
        moved = turned(tile, -(down * cols + across)) if (down, across) != (0, 0) else tile
        tables.append(jnp.where(inside, moved - nothing, 0).astype(jnp.float32))
    tables.append((slot - PS).astype(jnp.float32))
    first = jnp.zeros((peers, BW), jnp.float32)
    second = jnp.zeros((peers, BW), jnp.float32)
    for j in range(most):
        chosen = mine & (rank == j)
        for i, table in enumerate(tables):
            value = jnp.sum(jnp.where(chosen, table, 0.0), axis=1, keepdims=True)
            value = value + (nothing if i < 9 else PS)
            if i < 8:
                first = jnp.where(lane == i * most + j, value, first)
            else:
                second = jnp.where(lane == (i - 8) * most + j, value, second)
    index = turned(numbers, 2 * most)
    second = jnp.where((lane >= 2 * most) & (lane < 2 * most + bases), index, second)
    spots[0:peers, :] = (first * BH).astype(jnp.int32)
    spots[peers : 2 * peers, :] = (jnp.where(lane < 2 * most, second * BH, second)).astype(jnp.int32)
    coef = turned(numbers, -bases) + turned(numbers, -2 * bases) + turned(numbers, -3 * bases)
    heavy = numbers[:, 4 * bases : 4 * bases + 1]
    scales[...] = jnp.where(lane < bases, coef * heavy, 0.0)


def gauss_kernel(basis_width, across_bands, down_bands):
    tap = lax.broadcasted_iota(jnp.int32, (8, 128), 1).astype(jnp.float32) - band_reach
    shape = across_bands.shape[1:]
    across_gap = (
        lax.broadcasted_iota(jnp.int32, shape, 0) - lax.broadcasted_iota(jnp.int32, shape, 1) - LEAN
    ).astype(jnp.float32)
    shape = down_bands.shape[1:]
    out_row = lax.broadcasted_iota(jnp.int32, shape, 0)
    in_row = lax.broadcasted_iota(jnp.int32, shape, 1)
    inner = in_row % TALL
    down_gap = jnp.where(inner < BH + BH // 2, inner, inner - TALL) - out_row % BH
    down_gap = jnp.where(out_row // BH == in_row // TALL, down_gap, 1024).astype(jnp.float32)
    for member in range(across_bands.shape[0]):
        blur_width = basis_width[member]
        spread = 2.0 * blur_width * blur_width
        total = jnp.sum(jnp.where(tap <= band_reach, jnp.exp(-tap * tap / spread), 0.0), axis=1, keepdims=True)[0:1]
        for gap, out in ((across_gap, across_bands), (down_gap, down_bands)):
            value = jnp.where(jnp.abs(gap) <= band_reach, jnp.exp(-gap * gap / spread), 0.0)
            out[member] = (value / total).astype(jnp.bfloat16)


def match_kernel(
    peers,
    bases,
    most,
    steps,
    across_bands,
    down_bands,
    coadd,
    weight_sum,
    spots,
    scales,
    *refs,
):
    pieces, (template, out, table, window, blurred, matched) = refs[:4], refs[4:]
    groups = pl.cdiv(most, GROUP)
    high = GROUP * TALL
    length = pieces[0].shape[0]
    for i, piece in enumerate(pieces):
        table[i * length : (i + 1) * length, :] = piece[...]
    table[4 * length :, :] = jnp.zeros((BH, BW), jnp.bfloat16)
    matched[...] = jnp.zeros_like(matched)
    template[...] = coadd[...].astype(jnp.bfloat16)
    if most % GROUP:
        window[...] = jnp.zeros_like(window)
    lane = lax.broadcasted_iota(jnp.int32, (BH, BW), 1)
    row = lax.broadcasted_iota(jnp.int32, (BH, BW), 0)
    left = lane < LEAN
    upper = row < BH // 2

    @pl.loop(0, peers // steps)
    def _(turn):
        for step in range(steps):
            visit = turn * steps + step
            for j in range(most):

                def tile(i):
                    at = spots[visit, i * most + j] if i < 8 else spots[peers + visit, j]
                    return table[pl.ds(pl.multiple_of(at, BH), BH), :]

                tiles = [tile(i) for i in range(9)]
                mixed = [jnp.where(upper, tiles[6 + i], tiles[i]) for i in range(3)]
                start = (step * groups * GROUP + j) * TALL
                for base, (west, middle, east) in ((0, tiles[3:6]), (BH, mixed)):
                    window[start + base : start + base + BH, 0:BW] = jnp.where(left, west, middle)
                    window[start + base : start + base + BH, BW:] = jnp.where(left, middle, east)
        for step in range(steps):
            visit = turn * steps + step
            here = slice(step * groups * high, (step + 1) * groups * high)
            for member in range(0, bases, 2):
                pair = range(member, min(member + 2, bases))
                band = [across_bands[spots[peers + visit, 2 * most + k]] for k in pair]
                band = jnp.concatenate(band, axis=1) if len(band) > 1 else band[0]
                blurred[here, member * BW : member * BW + band.shape[1]] = jnp.dot(
                    window[here, :], band, preferred_element_type=jnp.float32
                ).astype(jnp.bfloat16)
        for step in range(steps):
            visit = turn * steps + step
            parts = [slice((step * groups + i) * high, (step * groups + i + 1) * high) for i in range(groups)]
            total = jnp.zeros((GROUP * BH, groups * BW), jnp.float32)
            for k in range(bases):
                side = [blurred[here, k * BW : (k + 1) * BW] for here in parts]
                side = jnp.concatenate(side, axis=1) if groups > 1 else side[0]
                total = total + scales[visit, k] * jnp.dot(
                    down_bands[spots[peers + visit, 2 * most + k]], side, preferred_element_type=jnp.float32
                )
            for j in range(most):
                group, i = divmod(j, GROUP)
                at = spots[peers + visit, most + j]
                matched[pl.ds(pl.multiple_of(at, BH), BH), :] += total[
                    i * BH : (i + 1) * BH, group * BW : (group + 1) * BW
                ]

    for i in range(PS):
        here = slice(i * BH, (i + 1) * BH)
        out[here, :] = coadd[here, :] - matched[here, :] / weight_sum[i : i + 1, :]


def shards(
    visit_image,
    band_offset,
    shift_frac,
    weights,
    box_owner,
    box_slot,
    basis_index,
    basis_coef,
    basis_width,
):
    peers = lax.axis_size("visit")
    rows, width = visit_image.shape[1:]
    bases = basis_index.shape[1]
    table_size = basis_width.shape[0]
    most = max(2, 2 * box_slot.shape[1] // peers)
    me = lax.axis_index("visit").astype(jnp.int32).reshape(1)
    chunk = CHUNK
    owner = box_owner.reshape(1, -1)

    quarter = jax.ShapeDtypeStruct((peers // 4 * chunk, BW), jnp.bfloat16)
    sums = pl.pallas_call(
        functools.partial(warp_kernel, peers, bases),
        out_shape=[quarter] * 4,
        in_specs=[SMEM] + [ANY] * 8,
        out_specs=[VMEM] * 4,
        scratch_shapes=[
            pltpu.VMEM((rows, width), jnp.bfloat16),
            pltpu.VMEM(owner.shape, jnp.int32),
            pltpu.VMEM(box_slot.shape, jnp.int32),
            pltpu.SMEM(band_offset.shape, jnp.int32),
            pltpu.SMEM(shift_frac.shape, jnp.float32),
            pltpu.VMEM((1, 1), jnp.bfloat16),
            pltpu.SMEM(basis_index.shape, jnp.int32),
            pltpu.SMEM(basis_coef.shape, jnp.float32),
            pltpu.VMEM((peers * BOXES, BW), jnp.float32),
            pltpu.VMEM((WIDE + 2 * SIDE, WIDE), jnp.bfloat16),
            pltpu.VMEM((1, BW), jnp.int32),
            pltpu.SMEM((1, BW), jnp.int32),
            pltpu.SemaphoreType.DMA((9,)),
        ],
        compiler_params=pltpu.CompilerParams(vmem_limit_bytes=48 * 1024 * 1024),
        name="warp",
    )(
        me,
        visit_image[0],
        owner,
        box_slot,
        band_offset,
        shift_frac,
        weights.reshape(1, 1),
        basis_index,
        basis_coef,
    )

    across_bands, down_bands = pl.pallas_call(
        gauss_kernel,
        out_shape=[
            jax.ShapeDtypeStruct((table_size, BW + 2 * LEAN, BW), jnp.bfloat16),
            jax.ShapeDtypeStruct((table_size, GROUP * BH, GROUP * TALL), jnp.bfloat16),
        ],
        in_specs=[SMEM],
        out_specs=[VMEM] * 2,
        compiler_params=params(),
        name="gauss_bands",
    )(basis_width)

    terms = scatter_sum(*sums, peers)
    leaning, coadd, weight_sum = pl.pallas_call(
        functools.partial(template_kernel, peers, bases),
        out_shape=[
            jax.ShapeDtypeStruct((BOXES, BW), jnp.bfloat16),
            jax.ShapeDtypeStruct((BOXES, BW), jnp.float32),
            jax.ShapeDtypeStruct((PS, BW), jnp.float32),
        ],
        in_specs=[SMEM] + [VMEM] * len(terms),
        out_specs=[VMEM] * 3,
        compiler_params=params(),
        name="template",
    )(me, *terms)
    spots, scales = pl.pallas_call(
        functools.partial(plan_kernel, peers, bases, most, rows // BH),
        out_shape=[
            jax.ShapeDtypeStruct((2 * peers, BW), jnp.int32),
            jax.ShapeDtypeStruct((peers, BW), jnp.float32),
        ],
        in_specs=[SMEM] + [VMEM] * len(terms),
        out_specs=[VMEM] * 2,
        compiler_params=params(),
        name="plan",
    )(me, *terms)

    pieces = gather_slots(leaning, peers, (across_bands, spots))
    steps = min(peers, 16)
    tall = steps * pl.cdiv(most, GROUP) * GROUP * TALL
    template, difference_coadd = pl.pallas_call(
        functools.partial(match_kernel, peers, bases, most, steps),
        out_shape=[
            jax.ShapeDtypeStruct((BOXES, BW), jnp.bfloat16),
            jax.ShapeDtypeStruct((BOXES, BW), jnp.float32),
        ],
        in_specs=[VMEM] * 4 + [SMEM] * 2 + [VMEM] * 4,
        out_specs=[VMEM] * 2,
        scratch_shapes=[
            pltpu.VMEM(((peers * PS + 1) * BH, BW), jnp.bfloat16),
            pltpu.VMEM((tall, BW + 2 * LEAN), jnp.bfloat16),
            pltpu.VMEM((tall, bases * BW), jnp.bfloat16),
            pltpu.VMEM(((PS + 1) * BH, BW), jnp.float32),
        ],
        compiler_params=params(),
        name="match",
    )(across_bands, down_bands, coadd, weight_sum, spots, scales, *pieces)
    return (template.reshape(PS, BH, BW), difference_coadd.reshape(PS, BH, BW))


def solution(mesh):
    placed = (
        P(("groups", "visit"), None, None),
        P(("groups", "visit"), None),
        P(("groups", "visit"), None),
        P(("groups", "visit")),
        P(("groups", "visit"), None, None),
        P(("groups", "visit"), None),
        P(("groups", "visit"), None),
        P(("groups", "visit"), None),
        P(),
    )
    return jax.shard_map(
        shards,
        mesh=mesh,
        in_specs=placed,
        out_specs=(P(("groups", "visit"), None, None), P(("groups", "visit"), None, None)),
        check_vma=False,
    )
```

```python
import functools

import jax
import jax.numpy as jnp
from jax import lax
from jax.experimental import pallas as pl
from jax.experimental.pallas import tpu as pltpu
from jax.sharding import PartitionSpec as P

BH = 16
BW = 128
PS = 16
BOXES = PS * BH
SIDE = 128
WIDE = 256
LEAN = 64
TALL = 2 * BH
GROUP = 8

band_reach = 8.0

VMEM = pl.BlockSpec(memory_space=pltpu.VMEM)
SMEM = pl.BlockSpec(memory_space=pltpu.SMEM)
ANY = pl.BlockSpec(memory_space=pl.ANY)


def params():
    return pltpu.CompilerParams(vmem_limit_bytes=48 * 1024 * 1024)


def place(owner, me, peers):
    away = jnp.bitwise_xor(owner, me)
    return (away & 1) * (peers // 2) + ((away >> 1) & 1) * (peers // 4) + (away >> 2)


QUAD = 4
CHUNK = BOXES + BH


def windows(width):
    found = []
    for first in range(0, width, WIDE):
        low, high = max(first - SIDE, 0), min(first + WIDE + SIDE, width)
        found.append((low, high, low - first + SIDE, high - first + SIDE))
    return found


def turned(x, by):
    return pltpu.roll(x, by % BW, 1)


def lanczos_taps(whole, part):
    lane = lax.broadcasted_iota(jnp.int32, (8, BW), 1).astype(jnp.float32)
    x = (whole + lane - 2.0) - (whole + part)

    def sinc(v):
        angle = jnp.pi * v
        return jnp.where(v == 0.0, 1.0, jnp.sin(angle) / jnp.where(v == 0.0, 1.0, angle))

    return jnp.where(jnp.abs(x) < 3.0, sinc(x) * sinc(x / 3.0), 0.0)


def lanczos_band(gap, whole, taps):
    band = jnp.zeros(gap.shape, jnp.float32)
    for tap in range(7):
        band = jnp.where(gap == whole + (tap - 2), taps[0:1, tap : tap + 1], band)
    return band.astype(jnp.bfloat16)


def warp_kernel(
    peers,
    bases,
    me_ref,
    picture_in,
    owner_in,
    slot_in,
    offset_in,
    fraction_in,
    weight_in,
    index_in,
    coef_in,
    keep_near,
    keep_far,
    send_near,
    send_far,
    picture,
    owner,
    slot,
    offset,
    fraction,
    weight,
    index,
    coef,
    total,
    wide_band,
    spots,
    starts,
    sems,
):
    rows, width = picture.shape
    me = me_ref[0]
    chunk = CHUNK
    sources = (owner_in, slot_in, offset_in, fraction_in, weight_in, index_in, coef_in, picture_in)
    targets = (owner, slot, offset, fraction, weight, index, coef, picture)
    copies = [pltpu.make_async_copy(x, y, sems.at[i]) for i, (x, y) in enumerate(zip(sources, targets))]
    for copy in copies:
        copy.start()
    total[...] = jnp.zeros_like(total)
    for copy in copies[:-1]:
        copy.wait()
    spots[...] = (place(owner[...], me, peers) * PS + slot[...]) * BH
    turn_in = pltpu.make_async_copy(spots, starts, sems.at[len(copies)])
    turn_in.start()

    whole = offset[0, 1].astype(jnp.float32)
    taps = lanczos_taps(whole, fraction[0, 1])
    place_of = lax.broadcasted_iota(jnp.int32, (SIDE, SIDE), 0) - lax.broadcasted_iota(jnp.int32, (SIDE, SIDE), 1)
    above, middle, below = [
        lanczos_band((place_of - shift).astype(jnp.float32), whole, taps) for shift in (SIDE, 0, -SIDE)
    ]
    nothing = jnp.zeros_like(middle)
    for down, pieces in enumerate(((above, nothing), (middle, above), (below, middle), (nothing, below))):
        for col, piece in enumerate(pieces):
            wide_band[down * SIDE : (down + 1) * SIDE, col * SIDE : (col + 1) * SIDE] = piece
    gap = (
        lax.broadcasted_iota(jnp.int32, (rows, rows), 1) - lax.broadcasted_iota(jnp.int32, (rows, rows), 0)
    ).astype(jnp.float32)
    whole = offset[0, 0].astype(jnp.float32)
    row_warp = lanczos_band(gap, whole, lanczos_taps(whole, fraction[0, 0]))

    heavy = weight[...].astype(jnp.float32)
    lane = lax.broadcasted_iota(jnp.int32, (8, BW), 1)
    numbers = jnp.zeros((8, BW), jnp.float32)
    share = jnp.zeros((8, BW), jnp.float32)
    for k in range(bases):
        numbers = jnp.where(lane == k, index[0, k].astype(jnp.float32), numbers)
        share = jnp.where(lane == k, coef[0, k], share)
    for i in range(1, 4):
        piece = share.astype(jnp.bfloat16).astype(jnp.float32)
        share = share - piece
        numbers = numbers + turned(piece, i * bases)
    numbers = jnp.where(lane == 4 * bases, heavy, numbers)

    copies[-1].wait()
    mean = jnp.sum(jnp.sum(picture[...].astype(jnp.float32), axis=0, keepdims=True), axis=1, keepdims=True)
    mean = (mean * (1.0 / (rows * width))).astype(jnp.bfloat16).astype(jnp.float32)
    numbers = jnp.where(lane == 4 * bases + 1, mean, numbers)[0:1]
    row = lax.broadcasted_iota(jnp.int32, (BH, BW), 0) - me % QUAD
    tags = jnp.zeros((BH, BW), jnp.float32)
    for i, line in enumerate((owner[...].astype(jnp.float32), slot[...].astype(jnp.float32), numbers)):
        tags = jnp.where(row == i * QUAD, line, tags)
    tags = tags.astype(jnp.bfloat16)
    passes = [
        jnp.dot(
            picture[:, low:high], wide_band[top:bottom, :], preferred_element_type=jnp.float32
        ).astype(jnp.bfloat16)
        for low, high, top, bottom in windows(width)
    ]
    turn_in.wait()
    across = WIDE // BW
    for block, col_pass in enumerate(passes):
        done = jnp.dot(row_warp, col_pass, preferred_element_type=jnp.float32).astype(jnp.bfloat16)
        scaled = (done.astype(jnp.float32) - mean) * heavy
        for down in range(rows // BH):
            for col in range(across):
                box = down * (width // BW) + block * across + col
                piece = pl.ds(pl.multiple_of(starts[0, box], BH), BH)
                total[piece, :] += scaled[down * BH : (down + 1) * BH, col * BW : (col + 1) * BW]

    @pl.loop(0, peers // 4)
    def _(i):
        start = pl.multiple_of(i * chunk, PS)
        for quarter, out in enumerate((keep_near, keep_far, send_near, send_far)):
            source = pl.multiple_of((quarter * (peers // 4) + i) * BOXES, BOXES)
            out[pl.ds(start, BOXES), :] = total[pl.ds(source, BOXES), :].astype(jnp.bfloat16)
            out[pl.ds(start + BOXES, chunk - BOXES), :] = tags


def add_kernel(count, *refs):
    parts, outs = refs[:count], refs[count:]
    length = outs[0].shape[0]
    for i, out in enumerate(outs):
        out[...] = summed_terms(parts, slice(i * length, (i + 1) * length)).astype(jnp.bfloat16)


def add_parts(pieces, *parts):
    length = parts[0].shape[0] // pieces
    return pl.pallas_call(
        functools.partial(add_kernel, len(parts)),
        out_shape=[jax.ShapeDtypeStruct((length, BW), jnp.bfloat16)] * pieces,
        in_specs=[VMEM] * len(parts),
        out_specs=[VMEM] * pieces,
        compiler_params=params(),
        name="add_parts",
    )(*parts)


def swap(x, axis_size, bit):
    return lax.ppermute(x, "visit", [(i, i ^ bit) for i in range(axis_size)])


def scatter_sum(keep_near, keep_far, send_near, send_far, peers):
    (beyond,) = add_parts(1, keep_far, swap(send_far, peers, 1))
    terms = add_parts(peers // 4, keep_near, swap(send_near, peers, 1), swap(beyond, peers, 2))
    return [terms[0]] + [swap(terms[far], peers, 4 * far) for far in reversed(range(1, peers // 4))]


def join_kernel(count, *refs):
    parts, out = refs[:count], refs[-1]
    length = parts[0].shape[0]
    for i, part in enumerate(parts):
        out[i * length : (i + 1) * length, :] = part[...]


def join(*parts, before=()):
    rows, lanes = parts[0].shape
    return pl.pallas_call(
        functools.partial(join_kernel, len(parts)),
        out_shape=jax.ShapeDtypeStruct((rows * len(parts), lanes), parts[0].dtype),
        in_specs=[VMEM] * len(parts) + [ANY] * len(before),
        out_specs=VMEM,
        compiler_params=params(),
        name="join",
    )(*parts, *before)


def gather_slots(own, peers, before):
    count = peers // 8
    far = {away: swap(own, peers, 4 * away) for away in reversed(range(1, peers // 4))}
    high = join(*[far[away] for away in range(count, 2 * count)], before=before)
    high_side = swap(high, peers, 2)
    low = join(own, *[far[away] for away in range(1, count)])
    low_side = swap(low, peers, 2)
    line = join(low, high)
    high_far = swap(high_side, peers, 1)
    return line, low_side, high_side, swap(line, peers, 1), swap(low_side, peers, 1), high_far


def summed_terms(terms, here):
    total = terms[0][here, :].astype(jnp.float32)
    for term in terms[1:]:
        total = total + term[here, :].astype(jnp.float32)
    return total


def read_tags(terms):
    tiles = [term[BOXES:, :].astype(jnp.float32) for term in terms]
    owner, slot, numbers = [
        jnp.concatenate([tile[i * QUAD : (i + 1) * QUAD, :] for tile in tiles], axis=0) for i in range(3)
    ]
    return owner.astype(jnp.int32), slot.astype(jnp.int32), numbers


def template_kernel(peers, bases, me_ref, *refs):
    *terms, leaning, coadd, weight_sum = refs
    me = me_ref[0]
    owner, slot, numbers = read_tags(terms)
    heavy = numbers[:, 4 * bases : 4 * bases + 1]
    level = heavy * numbers[:, 4 * bases + 1 : 4 * bases + 2]
    mine = owner == me
    weighed, levelled = [], []
    for i in range(PS):
        hit = mine & (slot == i)
        weighed.append(jnp.sum(jnp.where(hit, heavy, 0.0), axis=0, keepdims=True))
        levelled.append(jnp.sum(jnp.where(hit, level, 0.0), axis=0, keepdims=True))
    total = 1.0 + jnp.sum(jnp.concatenate(weighed, axis=0), axis=1, keepdims=True)
    over = jnp.sum(jnp.concatenate(levelled, axis=0), axis=1, keepdims=True)
    weight_sum[...] = jnp.broadcast_to(total, weight_sum.shape)
    for i in range(PS):
        here = slice(i * BH, (i + 1) * BH)
        mean = (summed_terms(terms, here) + over[i : i + 1, :]) / total[i : i + 1, :]
        rounded = mean.astype(jnp.bfloat16).astype(jnp.float32)
        leaning[here, :] = turned(rounded, LEAN).astype(jnp.bfloat16)
        coadd[here, :] = mean


AROUND = [(down, across) for down in (-1, 0, 1) for across in (-1, 0, 1)]


def plan_kernel(peers, bases, most, rows_of_boxes, me_ref, *refs):
    *terms, spots, scales = refs
    me = me_ref[0]
    owner, slot, numbers = read_tags(terms)
    nothing = peers * PS
    tile = place(owner, me, peers) * PS + slot
    boxes = owner.shape[1]
    cols = boxes // rows_of_boxes
    box = lax.broadcasted_iota(jnp.int32, (peers, BW), 1)
    lane = lax.broadcasted_iota(jnp.int32, (peers, BW), 1)
    mine = owner == me
    before = (
        lax.broadcasted_iota(jnp.int32, (boxes, boxes), 0) < lax.broadcasted_iota(jnp.int32, (boxes, boxes), 1)
    )
    rank = jnp.dot(
        jnp.where(mine, 1.0, 0.0).astype(jnp.bfloat16),
        jnp.where(before, 1.0, 0.0).astype(jnp.bfloat16),
        preferred_element_type=jnp.float32,
    ).astype(jnp.int32)
    tables = []
    for down, across in AROUND:
        row, col = box // cols + down, box % cols + across
        inside = (row >= 0) & (row < rows_of_boxes) & (col >= 0) & (col < cols)
        moved = turned(tile, -(down * cols + across)) if (down, across) != (0, 0) else tile
        tables.append(jnp.where(inside, moved - nothing, 0).astype(jnp.float32))
    tables.append((slot - PS).astype(jnp.float32))
    first = jnp.zeros((peers, BW), jnp.float32)
    second = jnp.zeros((peers, BW), jnp.float32)
    for j in range(most):
        chosen = mine & (rank == j)
        for i, table in enumerate(tables):
            value = jnp.sum(jnp.where(chosen, table, 0.0), axis=1, keepdims=True)
            value = value + (nothing if i < 9 else PS)
            if i < 8:
                first = jnp.where(lane == i * most + j, value, first)
            else:
                second = jnp.where(lane == (i - 8) * most + j, value, second)
    index = turned(numbers, 2 * most)
    second = jnp.where((lane >= 2 * most) & (lane < 2 * most + bases), index, second)
    spots[0:peers, :] = (first * BH).astype(jnp.int32)
    spots[peers : 2 * peers, :] = (jnp.where(lane < 2 * most, second * BH, second)).astype(jnp.int32)
    coef = turned(numbers, -bases) + turned(numbers, -2 * bases) + turned(numbers, -3 * bases)
    heavy = numbers[:, 4 * bases : 4 * bases + 1]
    scales[...] = jnp.where(lane < bases, coef * heavy, 0.0)


def gauss_kernel(basis_width, across_bands, down_bands):
    tap = lax.broadcasted_iota(jnp.int32, (8, 128), 1).astype(jnp.float32) - band_reach
    shape = across_bands.shape[1:]
    across_gap = (
        lax.broadcasted_iota(jnp.int32, shape, 0) - lax.broadcasted_iota(jnp.int32, shape, 1) - LEAN
    ).astype(jnp.float32)
    shape = down_bands.shape[1:]
    out_row = lax.broadcasted_iota(jnp.int32, shape, 0)
    in_row = lax.broadcasted_iota(jnp.int32, shape, 1)
    inner = in_row % TALL
    down_gap = jnp.where(inner < BH + BH // 2, inner, inner - TALL) - out_row % BH
    down_gap = jnp.where(out_row // BH == in_row // TALL, down_gap, 1024).astype(jnp.float32)
    for member in range(across_bands.shape[0]):
        blur_width = basis_width[member]
        spread = 2.0 * blur_width * blur_width
        total = jnp.sum(jnp.where(tap <= band_reach, jnp.exp(-tap * tap / spread), 0.0), axis=1, keepdims=True)[0:1]
        for gap, out in ((across_gap, across_bands), (down_gap, down_bands)):
            value = jnp.where(jnp.abs(gap) <= band_reach, jnp.exp(-gap * gap / spread), 0.0)
            out[member] = (value / total).astype(jnp.bfloat16)


def match_kernel(
    peers,
    bases,
    most,
    steps,
    across_bands,
    down_bands,
    coadd,
    weight_sum,
    spots,
    scales,
    *refs,
):
    pieces, (template, out, table, window, blurred, matched) = refs[:6], refs[6:]
    groups = pl.cdiv(most, GROUP)
    high = GROUP * TALL
    start = 0
    for piece in pieces:
        table[start : start + piece.shape[0], :] = piece[...]
        start += piece.shape[0]
    table[start:, :] = jnp.zeros((BH, BW), jnp.bfloat16)
    matched[...] = jnp.zeros_like(matched)
    template[...] = coadd[...].astype(jnp.bfloat16)
    if most % GROUP:
        window[...] = jnp.zeros_like(window)
    lane = lax.broadcasted_iota(jnp.int32, (BH, BW), 1)
    row = lax.broadcasted_iota(jnp.int32, (BH, BW), 0)
    left = lane < LEAN
    upper = row < BH // 2

    @pl.loop(0, peers // steps)
    def _(turn):
        for step in range(steps):
            visit = turn * steps + step
            for j in range(most):

                def tile(i):
                    at = spots[visit, i * most + j] if i < 8 else spots[peers + visit, j]
                    return table[pl.ds(pl.multiple_of(at, BH), BH), :]

                tiles = [tile(i) for i in range(9)]
                mixed = [jnp.where(upper, tiles[6 + i], tiles[i]) for i in range(3)]
                start = (step * groups * GROUP + j) * TALL
                for base, (west, middle, east) in ((0, tiles[3:6]), (BH, mixed)):
                    window[start + base : start + base + BH, 0:BW] = jnp.where(left, west, middle)
                    window[start + base : start + base + BH, BW:] = jnp.where(left, middle, east)
        for step in range(steps):
            visit = turn * steps + step
            here = slice(step * groups * high, (step + 1) * groups * high)
            for member in range(0, bases, 2):
                pair = range(member, min(member + 2, bases))
                band = [across_bands[spots[peers + visit, 2 * most + k]] for k in pair]
                band = jnp.concatenate(band, axis=1) if len(band) > 1 else band[0]
                blurred[here, member * BW : member * BW + band.shape[1]] = jnp.dot(
                    window[here, :], band, preferred_element_type=jnp.float32
                ).astype(jnp.bfloat16)
        for step in range(steps):
            visit = turn * steps + step
            parts = [slice((step * groups + i) * high, (step * groups + i + 1) * high) for i in range(groups)]
            total = jnp.zeros((GROUP * BH, groups * BW), jnp.float32)
            for k in range(bases):
                side = [blurred[here, k * BW : (k + 1) * BW] for here in parts]
                side = jnp.concatenate(side, axis=1) if groups > 1 else side[0]
                total = total + scales[visit, k] * jnp.dot(
                    down_bands[spots[peers + visit, 2 * most + k]], side, preferred_element_type=jnp.float32
                )
            for j in range(most):
                group, i = divmod(j, GROUP)
                at = spots[peers + visit, most + j]
                matched[pl.ds(pl.multiple_of(at, BH), BH), :] += total[
                    i * BH : (i + 1) * BH, group * BW : (group + 1) * BW
                ]

    for i in range(PS):
        here = slice(i * BH, (i + 1) * BH)
        out[here, :] = coadd[here, :] - matched[here, :] / weight_sum[i : i + 1, :]


def shards(
    visit_image,
    band_offset,
    shift_frac,
    weights,
    box_owner,
    box_slot,
    basis_index,
    basis_coef,
    basis_width,
):
    peers = lax.axis_size("visit")
    rows, width = visit_image.shape[1:]
    bases = basis_index.shape[1]
    table_size = basis_width.shape[0]
    most = max(2, 2 * box_slot.shape[1] // peers)
    me = lax.axis_index("visit").astype(jnp.int32).reshape(1)
    chunk = CHUNK
    owner = box_owner.reshape(1, -1)

    quarter = jax.ShapeDtypeStruct((peers // 4 * chunk, BW), jnp.bfloat16)
    sums = pl.pallas_call(
        functools.partial(warp_kernel, peers, bases),
        out_shape=[quarter] * 4,
        in_specs=[SMEM] + [ANY] * 8,
        out_specs=[VMEM] * 4,
        scratch_shapes=[
            pltpu.VMEM((rows, width), jnp.bfloat16),
            pltpu.VMEM(owner.shape, jnp.int32),
            pltpu.VMEM(box_slot.shape, jnp.int32),
            pltpu.SMEM(band_offset.shape, jnp.int32),
            pltpu.SMEM(shift_frac.shape, jnp.float32),
            pltpu.VMEM((1, 1), jnp.bfloat16),
            pltpu.SMEM(basis_index.shape, jnp.int32),
            pltpu.SMEM(basis_coef.shape, jnp.float32),
            pltpu.VMEM((peers * BOXES, BW), jnp.float32),
            pltpu.VMEM((WIDE + 2 * SIDE, WIDE), jnp.bfloat16),
            pltpu.VMEM((1, BW), jnp.int32),
            pltpu.SMEM((1, BW), jnp.int32),
            pltpu.SemaphoreType.DMA((9,)),
        ],
        compiler_params=pltpu.CompilerParams(vmem_limit_bytes=48 * 1024 * 1024),
        name="warp",
    )(
        me,
        visit_image[0],
        owner,
        box_slot,
        band_offset,
        shift_frac,
        weights.reshape(1, 1),
        basis_index,
        basis_coef,
    )

    across_bands, down_bands = pl.pallas_call(
        gauss_kernel,
        out_shape=[
            jax.ShapeDtypeStruct((table_size, BW + 2 * LEAN, BW), jnp.bfloat16),
            jax.ShapeDtypeStruct((table_size, GROUP * BH, GROUP * TALL), jnp.bfloat16),
        ],
        in_specs=[SMEM],
        out_specs=[VMEM] * 2,
        compiler_params=params(),
        name="gauss_bands",
    )(basis_width)

    terms = scatter_sum(*sums, peers)
    leaning, coadd, weight_sum = pl.pallas_call(
        functools.partial(template_kernel, peers, bases),
        out_shape=[
            jax.ShapeDtypeStruct((BOXES, BW), jnp.bfloat16),
            jax.ShapeDtypeStruct((BOXES, BW), jnp.float32),
            jax.ShapeDtypeStruct((PS, BW), jnp.float32),
        ],
        in_specs=[SMEM] + [VMEM] * len(terms),
        out_specs=[VMEM] * 3,
        compiler_params=params(),
        name="template",
    )(me, *terms)
    spots, scales = pl.pallas_call(
        functools.partial(plan_kernel, peers, bases, most, rows // BH),
        out_shape=[
            jax.ShapeDtypeStruct((2 * peers, BW), jnp.int32),
            jax.ShapeDtypeStruct((peers, BW), jnp.float32),
        ],
        in_specs=[SMEM] + [VMEM] * len(terms),
        out_specs=[VMEM] * 2,
        compiler_params=params(),
        name="plan",
    )(me, *terms)

    pieces = gather_slots(leaning, peers, (across_bands, spots))
    steps = min(peers, 16)
    tall = steps * pl.cdiv(most, GROUP) * GROUP * TALL
    template, difference_coadd = pl.pallas_call(
        functools.partial(match_kernel, peers, bases, most, steps),
        out_shape=[
            jax.ShapeDtypeStruct((BOXES, BW), jnp.bfloat16),
            jax.ShapeDtypeStruct((BOXES, BW), jnp.float32),
        ],
        in_specs=[VMEM] * 4 + [SMEM] * 2 + [VMEM] * 6,
        out_specs=[VMEM] * 2,
        scratch_shapes=[
            pltpu.VMEM(((peers * PS + 1) * BH, BW), jnp.bfloat16),
            pltpu.VMEM((tall, BW + 2 * LEAN), jnp.bfloat16),
            pltpu.VMEM((tall, bases * BW), jnp.bfloat16),
            pltpu.VMEM(((PS + 1) * BH, BW), jnp.float32),
        ],
        compiler_params=params(),
        name="match",
    )(across_bands, down_bands, coadd, weight_sum, spots, scales, *pieces)
    return (template.reshape(PS, BH, BW), difference_coadd.reshape(PS, BH, BW))


def solution(mesh):
    placed = (
        P(("groups", "visit"), None, None),
        P(("groups", "visit"), None),
        P(("groups", "visit"), None),
        P(("groups", "visit")),
        P(("groups", "visit"), None, None),
        P(("groups", "visit"), None),
        P(("groups", "visit"), None),
        P(("groups", "visit"), None),
        P(),
    )
    return jax.shard_map(
        shards,
        mesh=mesh,
        in_specs=placed,
        out_specs=(P(("groups", "visit"), None, None), P(("groups", "visit"), None, None)),
        check_vma=False,
    )
```
